32 devices in a mesh: groups: 2 (over y), seq: 4 (over z), mp: 4 (over x, core).
Axes of the slice: x: 2, y: 2, z: 4, core: 2. Of those that a mesh axis runs over, the one named last changes fastest.
Arguments:
- tile_features: bfloat16 [1536, 1536], P(('groups', 'seq'), 'mp'), parts along dimension 0, may hold values from -6 to 6
- head_outputs: bfloat16 [1536, 1536], P(('groups', 'seq'), 'mp'), parts along dimension 0, may hold values from -6 to 6
- out_proj: bfloat16 [1536, 1536], P('mp'), may hold values from -0.15625 to 0.15625
- layer_scale: float32 [1536], replicated, may hold values from 0.3 to 1.5
- tile_gain: float32 [1536], replicated, may hold values from 0.5 to 2
- slide_proj: bfloat16 [1536, 768], replicated, may hold values from -0.15625 to 0.15625
- slide_gain: float32 [768], replicated, may hold values from 0.5 to 2
- qkv_weight: bfloat16 [768, 3, 768], P(None, None, 'mp'), may hold values from -1 to 1
- slide_slot: int32 [1536], P('groups'), parts along dimension 0, may hold values from 0 to 767, as said below
- slide_len: int32 [8], P('groups'), parts along dimension 0, may hold values from 1 to 384, 768 in all
- seg_log: int32 [12], replicated, may hold values from 0 to 2, as said below
- rate_log: int32 [12], replicated, may hold values from 0 to 2, as said below
- out_grad: bfloat16 [1536, 768], P(('groups', 'seq'), 'mp'), parts along dimension 0, may hold values from -6 to 6
Outputs:
- slide_heads: bfloat16 [1536, 768], P(('groups', 'seq'), 'mp'), parts along dimension 0
- tile_grad: bfloat16 [1536, 1536], P(('groups', 'seq', 'mp')), parts along dimension 0
- head_grad: bfloat16 [1536, 1536], P(('groups', 'seq'), 'mp'), parts along dimension 0
The draws below stay inside these ranges and needn't reach their ends.
There are 2 independent parts, one for each index of `groups`. The reference program is written for one: setup_inputs(seed, part) draws one part's arguments, and reference() takes and returns one part's arrays. A program takes and returns all parts, laid end to end along the dimension named above; an argument that names none is the same for every part. Nothing has to cross between parts.
Inputs may be any that keep to these rules, and one draw needn't show every extreme that they name: slide_slot is a permutation of the 768 positions. Of the 192 tiles of one index of seq, at most 96 fill positions of any one index of seq (the positions p with the same p // 192); in every draw some index sends exactly 96 to some index. `slide_len`: the slides sum to 768 positions; the longest has exactly 384. `seg_log`: some head has 0 and some head has 2. `rate_log`: some head has 0 and some head has 2.
All inputs are finite; a program needn't handle non-finite values.
Results may differ from the reference program's by a relative error of at most 0.028.
Values may be sent and summed in bfloat16 or wider, within the bound.
A program may use at most 64 MiB of HBM per device.

```python
import math
import jax
import jax.numpy as jnp
import numpy as np
from jax import lax

DT = 1536
DS = 768
HEADS = 12
HEAD_DIM = 64
TILE_DEV = 192
SPAN_LOG = 2
RATE_LOG = 2
NSLIDES = 4
GROUP = 4
TILES = 768
LONGEST = 384
N_SEQ = 4


def draw_slide_slot(key, part):
    key = jax.random.fold_in(key, 11)
    keys_list = jax.random.split(key, 6)
    average = TILE_DEV // N_SEQ
    shifts = jax.random.randint(keys_list[0], (N_SEQ // 2,), -average, average + 1, dtype=jnp.int32)
    shifts = shifts.at[0].set(average)
    counts = jnp.concatenate([average + shifts, average - shifts])
    counts = counts[jax.random.permutation(keys_list[1], N_SEQ)]
    bounds = jnp.cumsum(counts)
    items = jnp.arange(TILE_DEV, dtype=jnp.int32)
    partner = jnp.sum((items[:, None] >= bounds[None, :]).astype(jnp.int32), axis=1)
    mixing = jax.random.permutation(keys_list[2], N_SEQ).astype(jnp.int32)
    offsets = jax.random.permutation(keys_list[3], N_SEQ).astype(jnp.int32)
    target = mixing[(offsets[:, None] + partner[None, :]) % N_SEQ]
    placing = jax.vmap(lambda sub_key: jax.random.permutation(sub_key, TILE_DEV))(jax.random.split(keys_list[4], N_SEQ)).astype(jnp.int32)
    landing = target * TILE_DEV + placing[target, items[None, :]]
    storing = jax.vmap(lambda sub_key: jax.random.permutation(sub_key, TILE_DEV))(jax.random.split(keys_list[5], N_SEQ)).astype(jnp.int32)
    local_order = jnp.argsort(storing, axis=1)
    result = jnp.take_along_axis(landing, local_order, axis=1)
    return result.reshape(-1).astype(jnp.int32)


def draw_seg_log(key, part):
    key = jax.random.fold_in(key, 21)
    first_key, second_key = jax.random.split(key)
    levels = jax.random.randint(first_key, (HEADS,), 0, SPAN_LOG + 1, dtype=jnp.int32)
    chosen = jax.random.permutation(second_key, HEADS)
    levels = levels.at[chosen[0]].set(SPAN_LOG)
    levels = levels.at[chosen[1]].set(0)
    return levels.astype(jnp.int32)


def draw_rate_log(key, part):
    key = jax.random.fold_in(key, 23)
    first_key, second_key = jax.random.split(key)
    levels = jax.random.randint(first_key, (HEADS,), 0, RATE_LOG + 1, dtype=jnp.int32)
    chosen = jax.random.permutation(second_key, HEADS)
    levels = levels.at[chosen[0]].set(RATE_LOG)
    levels = levels.at[chosen[1]].set(0)
    return levels.astype(jnp.int32)


def draw_qkv_weight(key, part):
    key = jax.random.fold_in(key, 31)
    base_key = jax.random.fold_in(key, 0)
    weights = jax.random.normal(base_key, (DS, 3, DS), jnp.float32) * DS ** (-0.5)
    return jnp.clip(weights, -1.0, 1.0).astype(jnp.bfloat16)


def block_scale(rng, dims, shards, least, high):
    level = 1.0
    for axis_at, blocks in shards:
        draws = jax.random.uniform(jax.random.fold_in(jax.random.fold_in(rng, 6), axis_at), (blocks,), jnp.float32, least / len(shards), high / len(shards))
        level = level * jnp.repeat(jnp.exp(draws), dims[axis_at] // blocks).reshape((-1,) + (1,) * (len(dims) - 1 - axis_at))
    return level


def profile(number_of, total, most, slope):
    weights = [(1 << 20) // math.isqrt(standing ** slope) + 1 for standing in range(2, number_of + 1)]
    rest, given = total - most - (number_of - 1), [1] * (number_of - 1)
    while rest > 0:
        candidates = [i for i in range(number_of - 1) if given[i] < most]
        whole, budget = sum([weights[i] for i in candidates]), rest
        for i in candidates:
            addition = min(most - given[i], max(1, budget * weights[i] // whole), rest)
            given[i] = given[i] + addition
            rest = rest - addition
    return np.array([most] + given)


def ragged(stream_key, count, total, limit, lean):
    if count == 2:
        one = jax.random.randint(stream_key, (), max(1, total - limit), min(limit, total - 1) + 1)
        return jnp.stack([one, total - one])
    tallies = jnp.asarray(profile(count, total, limit, lean), jnp.int32)
    twos = (count - 1) // 2
    source_of, sink = tallies[1:1 + 2 * twos:2], tallies[2:2 + 2 * twos:2]
    slack = jnp.minimum(source_of - 1, limit - sink)
    moved = jax.random.randint(jax.random.fold_in(stream_key, 1), (twos,), 0, 1 << 20) % (slack + 1)
    tallies = tallies.at[1:1 + 2 * twos:2].set(source_of - moved).at[2:2 + 2 * twos:2].set(sink + moved)
    return tallies[jax.random.permutation(jax.random.fold_in(stream_key, 2), count)]


def bell_draw(own_key, extent, deviation, limit, pieces=(), held_as=jnp.bfloat16):
    drawn = deviation * jax.random.normal(own_key, extent, jnp.float32)
    if pieces:
        drawn = drawn * block_scale(own_key, extent, pieces, -0.22, 0.18)
    return jnp.clip(drawn, -limit, limit).astype(held_as)


def setup_inputs(seed: int = 0, part: int = 0) -> dict:
    key_of = jax.random.split(jax.random.key(seed), 14)
    own_keys = jax.random.split(jax.random.fold_in(key_of[13], part), 14)
    tile_features = bell_draw(own_keys[0], (TILES, DT), 1.0, 6.0, ((0, 4), (1, 4)))
    head_outputs = bell_draw(own_keys[1], (TILES, DT), 1.0, 6.0, ((0, 4), (1, 4)))
    out_proj = bell_draw(key_of[2], (DT, DT), DT ** -0.5, 0.15625, ((0, 4),))
    layer_scale = jnp.clip(jnp.exp(jax.random.uniform(key_of[3], (DT,), jnp.float32, math.log(0.3), math.log(1.5))), 0.3, 1.5)
    tile_gain = jnp.clip(jnp.exp(jax.random.uniform(key_of[4], (DT,), jnp.float32, math.log(0.5), math.log(2.0))), 0.5, 2.0)
    slide_proj = bell_draw(key_of[5], (DT, DS), DT ** -0.5, 0.15625)
    slide_gain = jnp.clip(jnp.exp(jax.random.uniform(key_of[6], (DS,), jnp.float32, math.log(0.5), math.log(2.0))), 0.5, 2.0)
    qkv_weight = draw_qkv_weight(jax.random.fold_in(key_of[13], 71), part)
    slide_slot = draw_slide_slot(jax.random.fold_in(jax.random.fold_in(key_of[13], part), 71), part)
    slide_len = ragged(own_keys[9], NSLIDES, TILES, LONGEST, 2).astype(jnp.int32)
    seg_log = draw_seg_log(jax.random.fold_in(key_of[13], 71), part)
    rate_log = draw_rate_log(jax.random.fold_in(key_of[13], 71), part)
    out_grad = bell_draw(own_keys[12], (TILES, DS), 1.0, 6.0, ((0, 4), (1, 4)))
    return {"tile_features": tile_features, "head_outputs": head_outputs, "out_proj": out_proj, "layer_scale": layer_scale, "tile_gain": tile_gain, "slide_proj": slide_proj, "slide_gain": slide_gain, "qkv_weight": qkv_weight, "slide_slot": slide_slot, "slide_len": slide_len, "seg_log": seg_log, "rate_log": rate_log, "out_grad": out_grad}


EPSILON = 1e-06

def norm_parts(values):
    center = values - lax.optimization_barrier(jnp.mean(values, axis=-1, keepdims=True))
    inverse = 1.0 / jnp.sqrt(lax.optimization_barrier(jnp.mean(center * center, axis=-1, keepdims=True)) + EPSILON)
    return (center * inverse, inverse)

def norm_back(upstream, normed, inverse):
    first_mean = lax.optimization_barrier(jnp.mean(upstream, axis=-1, keepdims=True))
    second_mean = lax.optimization_barrier(jnp.mean(upstream * normed, axis=-1, keepdims=True))
    return inverse * (upstream - first_mean - normed * second_mean)

def slide_ids(positions, slide_len):
    bounds = jnp.cumsum(slide_len)
    return lax.optimization_barrier(jnp.sum((positions[:, None] >= bounds[None, :]).astype(jnp.int32), axis=1))

def visible(query_pos, key_pos, query_slide, key_slide, widths, strides):
    same_slide = (query_slide[:, None] == key_slide[None, :])[None, :, :]
    window = widths[:, None, None]
    same_window = query_pos[None, :, None] // window == key_pos[None, None, :] // window
    stride = strides[:, None, None]
    same_phase = query_pos[None, :, None] % stride == key_pos[None, None, :] % stride
    return same_slide & same_window & same_phase

def softmax_rows(scores, allowed):
    shifted = jnp.where(allowed, scores, -jnp.inf)
    row_max = lax.optimization_barrier(jnp.max(shifted, axis=-1, keepdims=True))
    raised = jnp.exp(shifted - row_max)
    return raised / lax.optimization_barrier(jnp.sum(raised, axis=-1, keepdims=True))

def reference(tile_features, head_outputs, out_proj, layer_scale, tile_gain, slide_proj, slide_gain, qkv_weight, slide_slot, slide_len, seg_log, rate_log, out_grad):
    mixed = jnp.dot(head_outputs, out_proj, preferred_element_type=jnp.float32)
    summed = tile_features.astype(jnp.float32) + layer_scale * mixed
    tile_normed, tile_inverse = norm_parts(summed)
    lifted = (tile_normed * tile_gain).astype(jnp.bfloat16)
    embedded = jnp.dot(lifted, slide_proj, preferred_element_type=jnp.float32)
    slide_normed, slide_inverse = norm_parts(embedded)
    entering = (slide_normed * slide_gain).astype(jnp.bfloat16)
    weight_flat = qkv_weight.reshape(DS, 3 * DS)
    projected = jnp.dot(entering, weight_flat, preferred_element_type=jnp.float32).astype(jnp.bfloat16)
    positions = jnp.arange(TILES, dtype=jnp.int32)
    anchor = jnp.zeros((TILES,), jnp.int32).at[slide_slot].set(positions)
    ordered = projected[anchor]
    slides = slide_ids(positions, slide_len)
    widths = TILE_DEV * jnp.left_shift(jnp.int32(1), seg_log)
    strides = jnp.left_shift(jnp.int32(1), rate_log)
    block_rows = GROUP * TILE_DEV
    scale = HEAD_DIM ** (-0.5)

    def one_block(block_index):
        block_start = block_index * block_rows
        block_pos = lax.dynamic_slice_in_dim(positions, block_start, block_rows, 0)
        block_slide = lax.dynamic_slice_in_dim(slides, block_start, block_rows, 0)
        block_data = lax.dynamic_slice_in_dim(ordered, block_start, block_rows, 0).astype(jnp.float32)
        block_grad = lax.dynamic_slice_in_dim(out_grad, block_start, block_rows, 0).astype(jnp.float32)
        block_grad = block_grad.reshape(block_rows, HEADS, HEAD_DIM)
        queries = block_data[:, :DS].reshape(block_rows, HEADS, HEAD_DIM)
        keys_block = block_data[:, DS:2 * DS].reshape(block_rows, HEADS, HEAD_DIM)
        values_block = block_data[:, 2 * DS:].reshape(block_rows, HEADS, HEAD_DIM)
        allowed = visible(block_pos, block_pos, block_slide, block_slide, widths, strides)
        scores = jnp.einsum('ihd,jhd->hij', queries, keys_block) * scale
        probability = softmax_rows(scores, allowed)
        rounded = lax.optimization_barrier(probability.astype(jnp.bfloat16)).astype(jnp.float32)
        heads_block = jnp.einsum('hij,jhd->ihd', rounded, values_block).astype(jnp.bfloat16).reshape(block_rows, DS)
        prob_grad = jnp.einsum('ihd,jhd->hij', block_grad, values_block)
        delta = lax.optimization_barrier(jnp.sum(probability * prob_grad, axis=-1, keepdims=True))
        score_grad = lax.optimization_barrier((probability * (prob_grad - delta)).astype(jnp.bfloat16)).astype(jnp.float32)
        query_grad = (jnp.einsum('hij,jhd->ihd', score_grad, keys_block) * scale).astype(jnp.bfloat16)
        key_grad = (jnp.einsum('hij,ihd->jhd', score_grad, queries) * scale).astype(jnp.bfloat16)
        value_grad = jnp.einsum('hij,ihd->jhd', rounded, block_grad).astype(jnp.bfloat16)
        joined = jnp.concatenate([query_grad.reshape(block_rows, DS), key_grad.reshape(block_rows, DS), value_grad.reshape(block_rows, DS)], axis=1)
        return (heads_block, joined)
    block_count = TILES // block_rows
    heads_blocks, grad_blocks = lax.map(one_block, jnp.arange(block_count, dtype=jnp.int32))
    slide_heads = heads_blocks.reshape(TILES, DS)
    projected_grad = grad_blocks.reshape(TILES, 3 * DS)[slide_slot]
    entering_grad = lax.dot_general(projected_grad, weight_flat, (((1,), (1,)), ((), ())), preferred_element_type=jnp.float32)
    embedded_grad = norm_back(entering_grad * slide_gain, slide_normed, slide_inverse).astype(jnp.bfloat16)
    lifted_grad = lax.dot_general(embedded_grad, slide_proj, (((1,), (1,)), ((), ())), preferred_element_type=jnp.float32)
    summed_grad = norm_back(lifted_grad * tile_gain, tile_normed, tile_inverse)
    tile_grad = summed_grad.astype(jnp.bfloat16)
    mixed_grad = (layer_scale * summed_grad).astype(jnp.bfloat16)
    head_grad = lax.dot_general(mixed_grad, out_proj, (((1,), (1,)), ((), ())), preferred_element_type=jnp.float32).astype(jnp.bfloat16)
    return (slide_heads, tile_grad, head_grad)
```

```python
import jax
import jax.numpy as jnp
from jax import lax
from jax.experimental import pallas as pl
from jax.experimental.pallas import tpu as pltpu
from jax.sharding import PartitionSpec as P

HEAD_DIM = 64
SPAN_LOG = 2


EPSILON = 1e-06
SCALE = HEAD_DIM ** (-0.5)


def swapped(block, axis, distance):
    count = lax.axis_size(axis)
    route = []
    for low in range(count):
        high = low | 1 << distance
        if high != low and high < count:
            route += [(low, high), (high, low)]
    return lax.ppermute(block, axis, route)


def norm_parts(values):
    center = values - jnp.mean(values, axis=-1, keepdims=True)
    inverse = 1.0 / jnp.sqrt(jnp.mean(center * center, axis=-1, keepdims=True) + EPSILON)
    return (center * inverse, inverse)


def norm_back(upstream, normed, inverse):
    first_mean = jnp.mean(upstream, axis=-1, keepdims=True)
    second_mean = jnp.mean(upstream * normed, axis=-1, keepdims=True)
    return inverse * (upstream - first_mean - normed * second_mean)


def slide_ids(positions, slide_len):
    bounds = jnp.cumsum(slide_len)
    return jnp.sum((positions[:, None] >= bounds[None, :]).astype(jnp.int32), axis=1)


def visible(query_pos, key_pos, query_slide, key_slide, widths, strides):
    same_slide = (query_slide[:, None] == key_slide[None, :])[None, :, :]
    window = widths[:, None, None]
    same_window = query_pos[None, :, None] // window == key_pos[None, None, :] // window
    stride = strides[:, None, None]
    same_phase = query_pos[None, :, None] % stride == key_pos[None, None, :] % stride
    return same_slide & same_window & same_phase


def softmax_rows(scores, allowed):
    shifted = jnp.where(allowed, scores, -jnp.inf)
    row_max = jnp.max(shifted, axis=-1, keepdims=True)
    raised = jnp.exp(shifted - row_max)
    return raised / jnp.sum(raised, axis=-1, keepdims=True)


def share_sum(values):
    return lax.psum(values, "mp")


def reroute(buffer):
    return lax.all_to_all(buffer, "seq", split_axis=0, concat_axis=0, tiled=True)


def join_halves(own_part, partner_part, upper_half):
    return jnp.where(
        upper_half,
        jnp.concatenate([partner_part, own_part], axis=1),
        jnp.concatenate([own_part, partner_part], axis=1),
    )


def group_collect(stacked, seq_place):
    for bit_place in range(SPAN_LOG):
        partner_part = swapped(stacked, "seq", bit_place)
        stacked = join_halves(stacked, partner_part, seq_place >> bit_place & 1 == 1)
    return stacked


def group_reduce(stacked, seq_place):
    for bit_place in reversed(range(SPAN_LOG)):
        half_rows = stacked.shape[1] // 2
        upper_half = seq_place >> bit_place & 1 == 1
        lower_part = stacked[:, :half_rows]
        higher_part = stacked[:, half_rows:]
        kept_part = jnp.where(upper_half, higher_part, lower_part)
        given_part = jnp.where(upper_half, lower_part, higher_part)
        stacked = kept_part + swapped(given_part.astype(jnp.bfloat16), "seq", bit_place).astype(
            given_part.dtype
        )
    return stacked


def tile_forward(summed, tile_gain, slide_proj, slide_gain):
    tile_normed, tile_inverse = norm_parts(summed)
    lifted = (tile_normed * tile_gain).astype(jnp.bfloat16)
    embedded = jnp.dot(lifted, slide_proj, preferred_element_type=jnp.float32)
    slide_normed, slide_inverse = norm_parts(embedded)
    entering = (slide_normed * slide_gain).astype(jnp.bfloat16)
    return (entering, (tile_normed, tile_inverse, slide_normed, slide_inverse))


def tile_backward(entering_grad, saved_state, tile_gain, slide_proj, slide_gain, layer_scale):
    tile_normed, tile_inverse, slide_normed, slide_inverse = saved_state
    embedded_grad = norm_back(entering_grad * slide_gain, slide_normed, slide_inverse).astype(
        jnp.bfloat16
    )
    lifted_grad = lax.dot_general(
        embedded_grad, slide_proj, (((1,), (1,)), ((), ())), preferred_element_type=jnp.float32
    )
    summed_grad = norm_back(lifted_grad * tile_gain, tile_normed, tile_inverse)
    mixed_grad = (layer_scale * summed_grad).astype(jnp.bfloat16)
    return (summed_grad, mixed_grad)


def shards(
    tile_features,
    head_outputs,
    out_proj,
    layer_scale,
    tile_gain,
    slide_proj,
    slide_gain,
    qkv_weight,
    slide_slot,
    slide_len,
    seg_log,
    rate_log,
    out_grad,
):
    seq_count = lax.axis_size("seq")
    seq_place = lax.axis_index("seq")
    mp_count = lax.axis_size("mp")
    mp_place = lax.axis_index("mp")
    row_count, width_part = tile_features.shape
    share_rows = row_count // mp_count
    head_cols = qkv_weight.shape[2]
    local_heads = head_cols // HEAD_DIM
    group_size = 1 << SPAN_LOG
    group_count = group_size * row_count
    capacity = 2 * (row_count // seq_count)
    slot_total = seq_count * capacity
    column = mp_place * width_part
    weight_flat = qkv_weight.reshape(qkv_weight.shape[0], 3 * head_cols)
    scale = HEAD_DIM ** (-0.5)
    term = layer_scale * jnp.dot(head_outputs, out_proj, preferred_element_type=jnp.float32)
    own_block = lax.dynamic_slice_in_dim(term, column, width_part, 1) + tile_features.astype(
        jnp.float32
    )
    summed = share_sum(lax.dynamic_update_slice_in_dim(term, own_block, column, 1))
    entering, saved_state = tile_forward(summed, tile_gain, slide_proj, slide_gain)
    projected = jnp.dot(entering, weight_flat, preferred_element_type=jnp.float32).astype(
        jnp.bfloat16
    )
    tile_index = jnp.arange(row_count, dtype=jnp.int32)
    my_slots = lax.dynamic_slice_in_dim(slide_slot, seq_place * row_count, row_count, 0)
    target = my_slots // row_count
    send_rank = jnp.sum(
        ((target[:, None] == target[None, :]) & (tile_index[None, :] < tile_index[:, None])).astype(
            jnp.int32
        ),
        axis=1,
    )
    send_slot = target * capacity + send_rank
    every_tile = jnp.arange(slide_slot.shape[0], dtype=jnp.int32)
    anchor_all = jnp.zeros_like(slide_slot).at[slide_slot].set(every_tile)
    anchor = lax.dynamic_slice_in_dim(anchor_all, seq_place * row_count, row_count, 0)
    anchor_device = anchor // row_count
    anchor_row = anchor % row_count
    recv_rank = jnp.sum(
        (
            (anchor_device[:, None] == anchor_device[None, :])
            & (anchor_row[None, :] < anchor_row[:, None])
        ).astype(jnp.int32),
        axis=1,
    )
    recv_slot = anchor_device * capacity + recv_rank

    def pack(values, slot_list):
        slot_table = jnp.full((slot_total,), row_count, jnp.int32).at[slot_list].set(tile_index)
        padded = jnp.concatenate([values, jnp.zeros((1, values.shape[1]), values.dtype)], axis=0)
        return padded[slot_table].reshape(seq_count, capacity, values.shape[1])

    def unpack(buffer, slot_list):
        return buffer.reshape(slot_total, buffer.shape[2])[slot_list]

    arriving = unpack(reroute(pack(projected, send_slot)), recv_slot)
    queries = arriving[:, :head_cols]
    stacked = group_collect(
        jnp.stack([arriving[:, head_cols : 2 * head_cols], arriving[:, 2 * head_cols :]]), seq_place
    )
    keys_all = stacked[0].reshape(group_count, local_heads, HEAD_DIM)
    values_all = stacked[1].reshape(group_count, local_heads, HEAD_DIM)
    query_heads = queries.reshape(row_count, local_heads, HEAD_DIM)
    here_pos = seq_place * row_count + tile_index
    group_first = seq_place // group_size * group_count
    group_pos = group_first + jnp.arange(group_count, dtype=jnp.int32)
    here_slide = slide_ids(here_pos, slide_len)
    group_slide = slide_ids(group_pos, slide_len)
    head_start = mp_place * local_heads
    widths = row_count * jnp.left_shift(
        jnp.int32(1), lax.dynamic_slice_in_dim(seg_log, head_start, local_heads, 0)
    )
    strides = jnp.left_shift(
        jnp.int32(1), lax.dynamic_slice_in_dim(rate_log, head_start, local_heads, 0)
    )
    allowed = visible(here_pos, group_pos, here_slide, group_slide, widths, strides)
    scores = (
        jnp.einsum("ihd,jhd->hij", query_heads, keys_all, preferred_element_type=jnp.float32)
        * scale
    )
    probability = softmax_rows(scores, allowed)
    rounded = probability.astype(jnp.bfloat16)
    slide_heads = (
        jnp.einsum("hij,jhd->ihd", rounded, values_all, preferred_element_type=jnp.float32)
        .astype(jnp.bfloat16)
        .reshape(row_count, head_cols)
    )
    upstream = out_grad.reshape(row_count, local_heads, HEAD_DIM)
    prob_grad = jnp.einsum("ihd,jhd->hij", upstream, values_all, preferred_element_type=jnp.float32)
    delta = jnp.sum(probability * prob_grad, axis=-1, keepdims=True)
    score_grad = (probability * (prob_grad - delta)).astype(jnp.bfloat16)
    query_grad = (
        jnp.einsum("hij,jhd->ihd", score_grad, keys_all, preferred_element_type=jnp.float32) * scale
    ).astype(jnp.bfloat16)
    key_part = (
        jnp.einsum("hij,ihd->jhd", score_grad, query_heads, preferred_element_type=jnp.float32)
        * scale
    )
    value_part = jnp.einsum("hij,ihd->jhd", rounded, upstream, preferred_element_type=jnp.float32)
    reduced = group_reduce(
        jnp.stack(
            [key_part.reshape(group_count, head_cols), value_part.reshape(group_count, head_cols)]
        ),
        seq_place,
    )
    key_grad = reduced[0].astype(jnp.bfloat16)
    value_grad = reduced[1].astype(jnp.bfloat16)
    local_grad = jnp.concatenate(
        [query_grad.reshape(row_count, head_cols), key_grad, value_grad], axis=1
    )
    returning = unpack(reroute(pack(local_grad, recv_slot)), send_slot)
    entering_grad = share_sum(
        lax.dot_general(
            returning, weight_flat, (((1,), (1,)), ((), ())), preferred_element_type=jnp.float32
        )
    )
    summed_grad, mixed_grad = tile_backward(
        entering_grad, saved_state, tile_gain, slide_proj, slide_gain, layer_scale
    )
    tile_grad = lax.dynamic_slice_in_dim(summed_grad, mp_place * share_rows, share_rows, 0).astype(
        jnp.bfloat16
    )
    head_grad = lax.dot_general(
        mixed_grad, out_proj, (((1,), (1,)), ((), ())), preferred_element_type=jnp.float32
    ).astype(jnp.bfloat16)
    return (slide_heads, tile_grad, head_grad)


F32 = jnp.float32
BF16 = jnp.bfloat16
MESH = pl.DeviceIdType.MESH
HIDDEN = -1e30
GROUP_SEQ = 1 << SPAN_LOG
QUAD = 4


def rows_dot(left, right):
    return lax.dot_general(left, right, (((1,), (1,)), ((), ())), preferred_element_type=F32)


def cols_dot(left, right):
    return lax.dot_general(left, right, (((0,), (0,)), ((), ())), preferred_element_type=F32)


def plain_dot(left, right):
    return jnp.dot(left, right, preferred_element_type=F32)


def step_kernel(
    features_ref,
    outputs_ref,
    out_proj_ref,
    layer_scale_ref,
    tile_gain_ref,
    slide_proj_hbm,
    slide_gain_ref,
    weight_hbm,
    slot_ref,
    len_ref,
    seg_ref,
    rate_ref,
    grad_ref,
    heads_out,
    tile_out,
    head_out,
    slide_proj_ref,
    weight_ref,
    upstream_all,
    term_ref,
    first_out,
    first_in,
    second_out,
    second_in,
    entering_all,
    query_ref,
    key_ref,
    value_ref,
    upstream_ref,
    bias_row,
    bias_col,
    score_buf,
    grad_buf,
    stats_pad,
    stats_all,
    heads_all,
    back_ref,
    back_first_out,
    back_first_in,
    back_second_out,
    back_second_in,
    mixed_all,
    load_sem,
    up_send,
    up_recv,
    scatter_send,
    scatter_recv,
    z_send,
    z_recv,
    x_send,
    x_recv,
    core_send,
    core_recv,
    stats_send,
    stats_recv,
    heads_send,
    heads_recv,
    back_send,
    back_recv,
    mixed_send,
    mixed_recv,
):
    rows, width_part = features_ref.shape
    total = GROUP_SEQ * rows
    share = rows // QUAD
    head_cols = grad_ref.shape[1]
    local_heads = head_cols // HEAD_DIM
    seq = lax.axis_index("seq")
    mp = lax.axis_index("mp")
    sibling = mp + 1 - 2 * (mp % 2)
    across = (mp + 2) % QUAD
    corner = (sibling + 2) % QUAD

    def remote(source, target, send, recv, where):
        return pltpu.make_async_remote_copy(
            src_ref=source,
            dst_ref=target,
            send_sem=send,
            recv_sem=recv,
            device_id=where,
            device_id_type=MESH,
        )

    slide_load = pltpu.make_async_copy(slide_proj_hbm, slide_proj_ref, load_sem.at[0])
    weight_load = pltpu.make_async_copy(weight_hbm, weight_ref, load_sem.at[1])
    slide_load.start()
    weight_load.start()

    barrier = pltpu.get_barrier_semaphore()
    for offset in range(1, GROUP_SEQ):
        pl.semaphore_signal(
            barrier, inc=1, device_id={"seq": (seq + offset) % GROUP_SEQ}, device_id_type=MESH
        )
    for offset in range(1, QUAD):
        pl.semaphore_signal(
            barrier, inc=1, device_id={"mp": (mp + offset) % QUAD}, device_id_type=MESH
        )

    term_ref[...] = layer_scale_ref[...] * plain_dot(outputs_ref[...], out_proj_ref[...])
    own_cols = pl.ds(pl.multiple_of(mp * width_part, 128), width_part)
    term_ref[:, own_cols] += features_ref[...].astype(F32)

    def share_of(place):
        return pl.ds(pl.multiple_of(place * share, 16), share)

    pl.semaphore_wait(barrier, GROUP_SEQ - 1 + QUAD - 1)

    def scatter_first(source, out_buf, in_buf, send, recv):
        copies = []
        for slot, place in ((1, corner), (0, sibling)):
            out_buf[slot] = source[share_of(place), :].astype(BF16)
            copy = remote(
                out_buf.at[slot], in_buf.at[slot], send.at[slot], recv.at[slot], {"mp": sibling}
            )
            copy.start()
            copies.append(copy)
        return copies

    def scatter_second(source, copies, in_buf, out_ref, in_ref, send, recv):
        copies[0].wait_recv()
        out_ref[...] = (source[share_of(across), :] + in_buf[1].astype(F32)).astype(BF16)
        copy = remote(out_ref, in_ref, send.at[2], recv.at[2], {"mp": across})
        copy.start()
        copies[1].wait_recv()
        partial = source[share_of(mp), :] + in_buf[0].astype(F32)
        copy.wait_recv()
        for each in copies + [copy]:
            each.wait_send()
        return partial + in_ref[...].astype(F32)

    first = scatter_first(term_ref, first_out, first_in, scatter_send, scatter_recv)

    upstream_all[seq] = grad_ref[...]
    up_copies = []
    for offset in range(1, GROUP_SEQ):
        copy = remote(
            grad_ref,
            upstream_all.at[seq],
            up_send.at[offset - 1],
            up_recv.at[offset - 1],
            {"seq": (seq + offset) % GROUP_SEQ},
        )
        copy.start()
        up_copies.append(copy)

    slots = slot_ref[...]
    base = seq * rows
    bounds = []
    reached = 0
    for index in range(len_ref.shape[0]):
        reached = reached + len_ref[index]
        bounds.append(reached)
    slide_of = jnp.zeros_like(slots)
    for bound in bounds:
        slide_of = slide_of + (slots >= bound).astype(jnp.int32)
    window_of = jnp.zeros_like(slots)
    for index in range(1, GROUP_SEQ):
        window_of = window_of + (slots >= index * rows).astype(jnp.int32)
    lane_all = lax.broadcasted_iota(jnp.int32, (rows, total), 1)
    sub_all = lax.broadcasted_iota(jnp.int32, (rows, total), 0)
    pick_own = (lane_all == sub_all + base).astype(BF16)
    eye = (
        lax.broadcasted_iota(jnp.int32, (total, total), 0)
        == lax.broadcasted_iota(jnp.int32, (total, total), 1)
    ).astype(BF16)
    for head in range(local_heads):
        seg = seg_ref[mp * local_heads + head]
        rate = rate_ref[mp * local_heads + head]
        stride_mask = jnp.left_shift(jnp.int32(1), rate) - 1
        code = (
            slide_of * (GROUP_SEQ * GROUP_SEQ)
            + jnp.right_shift(window_of, jnp.full_like(window_of, seg)) * GROUP_SEQ
            + (slots & stride_mask)
        )
        code_rows = jnp.broadcast_to(code.astype(F32), (rows, total))
        code_bf = code_rows.astype(BF16)
        code_own_lane = rows_dot(code_bf, pick_own)
        code_all_sub = rows_dot(eye, code_bf)
        bias_row[head] = jnp.where(code_all_sub == code_own_lane[:1], 0.0, HIDDEN)
        code_own_sub = rows_dot(pick_own, code_bf)
        bias_col[head] = jnp.where(code_own_sub[:, :1] == code_rows, 0.0, HIDDEN)
    slot_rows = jnp.broadcast_to(slots, (rows, total))
    pick_heads = (slot_rows == sub_all + base).astype(BF16)
    arrange = (
        jnp.broadcast_to(slots, (total, total)) == lax.broadcasted_iota(jnp.int32, (total, total), 0)
    ).astype(BF16)

    summed = scatter_second(
        term_ref, first, first_in, second_out, second_in, scatter_send, scatter_recv
    )
    tile_normed, tile_inverse = norm_parts(summed)
    lifted = (tile_normed * tile_gain_ref[...]).astype(BF16)
    slide_load.wait()
    embedded = plain_dot(lifted, slide_proj_ref[...])
    slide_normed, slide_inverse = norm_parts(embedded)
    entering_all[seq, mp] = (slide_normed * slide_gain_ref[...]).astype(BF16)

    pending = []

    def forward(source_seq, source_mp, send, recv, where):
        copy = remote(
            entering_all.at[source_seq, source_mp],
            entering_all.at[source_seq, source_mp],
            send,
            recv,
            where,
        )
        copy.start()
        pending.append(copy)
        return copy

    z_copies = []
    for offset in range(1, GROUP_SEQ):
        z_copies.append(
            forward(
                seq,
                mp,
                z_send.at[offset - 1],
                z_recv.at[offset - 1],
                {"seq": (seq + offset) % GROUP_SEQ},
            )
        )
    x_copies = [forward(seq, mp, x_send.at[0], x_recv.at[0], {"mp": across})]
    core_copies = [forward(seq, mp, core_send.at[0], core_recv.at[0], {"mp": sibling})]

    for copy in up_copies:
        copy.wait()
    upstream_ref[...] = cols_dot(arrange, upstream_all[...].reshape(total, head_cols)).astype(BF16)

    for offset in range(1, GROUP_SEQ):
        origin = (seq + GROUP_SEQ - offset) % GROUP_SEQ
        z_copies[offset - 1].wait_recv()
        x_copies.append(forward(origin, mp, x_send.at[offset], x_recv.at[offset], {"mp": across}))
        core_copies.append(
            forward(origin, mp, core_send.at[offset], core_recv.at[offset], {"mp": sibling})
        )
    for offset in range(GROUP_SEQ):
        origin = (seq + GROUP_SEQ - offset) % GROUP_SEQ
        x_copies[offset].wait_recv()
        core_copies.append(
            forward(
                origin,
                across,
                core_send.at[GROUP_SEQ + offset],
                core_recv.at[GROUP_SEQ + offset],
                {"mp": sibling},
            )
        )
    weight_load.wait()
    for copy in core_copies:
        copy.wait_recv()
    entering = entering_all[...].reshape(total, entering_all.shape[3])
    query_ref[...] = (rows_dot(entering, weight_ref[0]).astype(BF16).astype(F32) * SCALE).astype(
        BF16
    )
    key_ref[...] = rows_dot(entering, weight_ref[1]).astype(BF16)
    value_ref[...] = rows_dot(entering, weight_ref[2]).astype(BF16)
    for copy in pending:
        copy.wait_send()

    own_rows = pl.ds(pl.multiple_of(base, 64), rows)

    def head_only(values, head):
        lane_head = lax.broadcasted_iota(jnp.int32, values.shape, 1) // HEAD_DIM
        return jnp.where(lane_head == head, values, jnp.zeros_like(values))

    stats_pad[...] = jnp.zeros_like(stats_pad)
    heads_sum = jnp.zeros((rows, head_cols), F32)
    query_sum = jnp.zeros((rows, head_cols), F32)
    keys = key_ref[...]
    values = value_ref[...]
    for head in range(local_heads):
        scores = rows_dot(keys, head_only(query_ref[own_rows, :], head)) + bias_row[head]
        row_max = jnp.max(scores, axis=0, keepdims=True)
        raised = jnp.exp(scores - row_max)
        row_sum = jnp.sum(raised, axis=0, keepdims=True)
        probability = raised * (1.0 / row_sum)
        prob_grad = rows_dot(values, head_only(upstream_ref[own_rows, :], head))
        delta = jnp.sum(probability * prob_grad, axis=0, keepdims=True)
        stats_pad[2 * head : 2 * head + 1, :rows] = row_max + jnp.log(row_sum)
        stats_pad[2 * head + 1 : 2 * head + 2, :rows] = delta
        score_grad = (probability * (prob_grad - delta)).astype(BF16)
        heads_sum = heads_sum + cols_dot(probability.astype(BF16), head_only(values, head))
        query_sum = query_sum + cols_dot(score_grad, head_only(keys, head))
    stats_all[seq] = pltpu.roll(stats_pad[...], base, 1)
    heads_all[seq] = heads_sum.astype(BF16)
    stats_copies = []
    heads_copies = []
    for offset in range(1, GROUP_SEQ):
        copy = remote(
            stats_all.at[seq],
            stats_all.at[seq],
            stats_send.at[offset - 1],
            stats_recv.at[offset - 1],
            {"seq": (seq + offset) % GROUP_SEQ},
        )
        copy.start()
        stats_copies.append(copy)
    for offset in range(1, GROUP_SEQ):
        copy = remote(
            heads_all.at[seq],
            heads_all.at[seq],
            heads_send.at[offset - 1],
            heads_recv.at[offset - 1],
            {"seq": (seq + offset) % GROUP_SEQ},
        )
        copy.start()
        heads_copies.append(copy)
    own_keys = key_ref[own_rows, :]
    own_values = value_ref[own_rows, :]
    queries = query_ref[...]
    upstream = upstream_ref[...]
    for head in range(local_heads):
        score_buf[head] = rows_dot(own_keys, head_only(queries, head)) + bias_col[head]
        grad_buf[head] = rows_dot(own_values, head_only(upstream, head))
    for copy in stats_copies:
        copy.wait()
    stats = stats_all[0] + stats_all[1] + stats_all[2] + stats_all[3]
    key_sum = jnp.zeros((rows, head_cols), F32)
    value_sum = jnp.zeros((rows, head_cols), F32)
    for head in range(local_heads):
        probability = jnp.exp(score_buf[head] - stats[2 * head : 2 * head + 1])
        score_grad = probability * (grad_buf[head] - stats[2 * head + 1 : 2 * head + 2])
        value_sum = value_sum + plain_dot(probability.astype(BF16), head_only(upstream, head))
        key_sum = key_sum + plain_dot(score_grad.astype(BF16), head_only(queries, head))
    back_ref[...] = (
        plain_dot((query_sum * SCALE).astype(BF16), weight_ref[0])
        + plain_dot(key_sum.astype(BF16), weight_ref[1])
        + plain_dot(value_sum.astype(BF16), weight_ref[2])
    )
    back_first = scatter_first(back_ref, back_first_out, back_first_in, back_send, back_recv)
    entering_grad = scatter_second(
        back_ref, back_first, back_first_in, back_second_out, back_second_in, back_send, back_recv
    )
    embedded_grad = norm_back(
        entering_grad * slide_gain_ref[...], slide_normed, slide_inverse
    ).astype(BF16)
    lifted_grad = rows_dot(embedded_grad, slide_proj_ref[...])
    summed_grad = norm_back(lifted_grad * tile_gain_ref[...], tile_normed, tile_inverse)
    mixed_all[mp] = (layer_scale_ref[...] * summed_grad).astype(BF16)

    def mixed_move(place, index, where):
        copy = remote(
            mixed_all.at[place],
            mixed_all.at[place],
            mixed_send.at[index],
            mixed_recv.at[index],
            {"mp": where},
        )
        copy.start()
        return copy

    mixed_x = mixed_move(mp, 0, across)
    mixed_core = mixed_move(mp, 1, sibling)
    tile_out[...] = summed_grad.astype(BF16)
    for copy in heads_copies:
        copy.wait()
    heads_out[...] = plain_dot(pick_heads, heads_all[...].reshape(total, head_cols)).astype(BF16)
    mixed_x.wait()
    mixed_corner = mixed_move(across, 2, sibling)
    mixed_core.wait()
    mixed_corner.wait()
    head_out[...] = rows_dot(
        mixed_all[...].reshape(rows, mixed_all.shape[2]), out_proj_ref[...]
    ).astype(BF16)


def fused_shards(
    tile_features,
    head_outputs,
    out_proj,
    layer_scale,
    tile_gain,
    slide_proj,
    slide_gain,
    qkv_weight,
    slide_slot,
    slide_len,
    seg_log,
    rate_log,
    out_grad,
):
    rows, width_part = tile_features.shape
    width = out_proj.shape[1]
    slide_width = slide_proj.shape[1]
    head_cols = qkv_weight.shape[2]
    local_heads = head_cols // HEAD_DIM
    share = rows // QUAD
    total = GROUP_SEQ * rows
    vmem = pl.BlockSpec(memory_space=pltpu.VMEM)
    smem = pl.BlockSpec(memory_space=pltpu.SMEM)
    hbm = pl.BlockSpec(memory_space=pl.ANY)
    dma = pltpu.SemaphoreType.DMA
    return pl.pallas_call(
        step_kernel,
        out_shape=(
            jax.ShapeDtypeStruct((rows, head_cols), BF16),
            jax.ShapeDtypeStruct((share, width), BF16),
            jax.ShapeDtypeStruct((rows, width_part), BF16),
        ),
        in_specs=[vmem, vmem, vmem, vmem, vmem, hbm, vmem, hbm, vmem, smem, smem, smem, vmem],
        out_specs=(vmem, vmem, vmem),
        scratch_shapes=[
            pltpu.VMEM((width, slide_width), BF16),
            pltpu.VMEM((3, head_cols, slide_width), BF16),
            pltpu.VMEM((GROUP_SEQ, rows, head_cols), BF16),
            pltpu.VMEM((rows, width), F32),
            pltpu.VMEM((2, share, width), BF16),
            pltpu.VMEM((2, share, width), BF16),
            pltpu.VMEM((share, width), BF16),
            pltpu.VMEM((share, width), BF16),
            pltpu.VMEM((GROUP_SEQ, QUAD, share, slide_width), BF16),
            pltpu.VMEM((total, head_cols), BF16),
            pltpu.VMEM((total, head_cols), BF16),
            pltpu.VMEM((total, head_cols), BF16),
            pltpu.VMEM((total, head_cols), BF16),
            pltpu.VMEM((local_heads, total, rows), F32),
            pltpu.VMEM((local_heads, rows, total), F32),
            pltpu.VMEM((local_heads, rows, total), F32),
            pltpu.VMEM((local_heads, rows, total), F32),
            pltpu.VMEM((8, total), F32),
            pltpu.VMEM((GROUP_SEQ, 8, total), F32),
            pltpu.VMEM((GROUP_SEQ, rows, head_cols), BF16),
            pltpu.VMEM((rows, slide_width), F32),
            pltpu.VMEM((2, share, slide_width), BF16),
            pltpu.VMEM((2, share, slide_width), BF16),
            pltpu.VMEM((share, slide_width), BF16),
            pltpu.VMEM((share, slide_width), BF16),
            pltpu.VMEM((QUAD, share, width), BF16),
            dma((2,)),
            dma((3,)),
            dma((3,)),
            dma((3,)),
            dma((3,)),
            dma((3,)),
            dma((3,)),
            dma((4,)),
            dma((4,)),
            dma((8,)),
            dma((8,)),
            dma((3,)),
            dma((3,)),
            dma((3,)),
            dma((3,)),
            dma((3,)),
            dma((3,)),
            dma((3,)),
            dma((3,)),
        ],
        compiler_params=pltpu.CompilerParams(
            collective_id=0, has_side_effects=True, vmem_limit_bytes=48 * 1024 * 1024
        ),
        name="slide_step",
    )(
        tile_features,
        head_outputs,
        out_proj,
        layer_scale.reshape(1, width),
        tile_gain.reshape(1, width),
        slide_proj,
        slide_gain.reshape(1, slide_width),
        jnp.transpose(qkv_weight, (1, 2, 0)),
        slide_slot.reshape(1, total),
        slide_len,
        seg_log,
        rate_log,
        out_grad,
    )


def solution(mesh):
    fused = mesh.shape["seq"] == GROUP_SEQ and mesh.shape["mp"] == QUAD
    body = fused_shards if fused else shards
    in_specs = (
        P(("groups", "seq"), "mp"),
        P(("groups", "seq"), "mp"),
        P("mp", None),
        P(),
        P(),
        P(),
        P(),
        P(None, None, "mp"),
        P("groups"),
        P("groups"),
        P(),
        P(),
        P(("groups", "seq"), "mp"),
    )
    out_specs = (
        P(("groups", "seq"), "mp"),
        P(("groups", "seq", "mp"), None),
        P(("groups", "seq"), "mp"),
    )
    return jax.shard_map(body, mesh=mesh, in_specs=in_specs, out_specs=out_specs, check_vma=False)
```

```python
import jax
import jax.numpy as jnp
from jax import lax
from jax.experimental import pallas as pl
from jax.experimental.pallas import tpu as pltpu
from jax.sharding import PartitionSpec as P

HEAD_DIM = 64
SPAN_LOG = 2


EPSILON = 1e-06
SCALE = HEAD_DIM ** (-0.5)


def swapped(block, axis, distance):
    count = lax.axis_size(axis)
    route = []
    for low in range(count):
        high = low | 1 << distance
        if high != low and high < count:
            route += [(low, high), (high, low)]
    return lax.ppermute(block, axis, route)


def norm_parts(values):
    center = values - jnp.mean(values, axis=-1, keepdims=True)
    inverse = 1.0 / jnp.sqrt(jnp.mean(center * center, axis=-1, keepdims=True) + EPSILON)
    return (center * inverse, inverse)


def norm_back(upstream, normed, inverse):
    first_mean = jnp.mean(upstream, axis=-1, keepdims=True)
    second_mean = jnp.mean(upstream * normed, axis=-1, keepdims=True)
    return inverse * (upstream - first_mean - normed * second_mean)


def slide_ids(positions, slide_len):
    bounds = jnp.cumsum(slide_len)
    return jnp.sum((positions[:, None] >= bounds[None, :]).astype(jnp.int32), axis=1)


def visible(query_pos, key_pos, query_slide, key_slide, widths, strides):
    same_slide = (query_slide[:, None] == key_slide[None, :])[None, :, :]
    window = widths[:, None, None]
    same_window = query_pos[None, :, None] // window == key_pos[None, None, :] // window
    stride = strides[:, None, None]
    same_phase = query_pos[None, :, None] % stride == key_pos[None, None, :] % stride
    return same_slide & same_window & same_phase


def softmax_rows(scores, allowed):
    shifted = jnp.where(allowed, scores, -jnp.inf)
    row_max = jnp.max(shifted, axis=-1, keepdims=True)
    raised = jnp.exp(shifted - row_max)
    return raised / jnp.sum(raised, axis=-1, keepdims=True)


def share_sum(values):
    return lax.psum(values, "mp")


def reroute(buffer):
    return lax.all_to_all(buffer, "seq", split_axis=0, concat_axis=0, tiled=True)


def join_halves(own_part, partner_part, upper_half):
    return jnp.where(
        upper_half,
        jnp.concatenate([partner_part, own_part], axis=1),
        jnp.concatenate([own_part, partner_part], axis=1),
    )


def group_collect(stacked, seq_place):
    for bit_place in range(SPAN_LOG):
        partner_part = swapped(stacked, "seq", bit_place)
        stacked = join_halves(stacked, partner_part, seq_place >> bit_place & 1 == 1)
    return stacked


def group_reduce(stacked, seq_place):
    for bit_place in reversed(range(SPAN_LOG)):
        half_rows = stacked.shape[1] // 2
        upper_half = seq_place >> bit_place & 1 == 1
        lower_part = stacked[:, :half_rows]
        higher_part = stacked[:, half_rows:]
        kept_part = jnp.where(upper_half, higher_part, lower_part)
        given_part = jnp.where(upper_half, lower_part, higher_part)
        stacked = kept_part + swapped(given_part.astype(jnp.bfloat16), "seq", bit_place).astype(
            given_part.dtype
        )
    return stacked


def tile_forward(summed, tile_gain, slide_proj, slide_gain):
    tile_normed, tile_inverse = norm_parts(summed)
    lifted = (tile_normed * tile_gain).astype(jnp.bfloat16)
    embedded = jnp.dot(lifted, slide_proj, preferred_element_type=jnp.float32)
    slide_normed, slide_inverse = norm_parts(embedded)
    entering = (slide_normed * slide_gain).astype(jnp.bfloat16)
    return (entering, (tile_normed, tile_inverse, slide_normed, slide_inverse))


def tile_backward(entering_grad, saved_state, tile_gain, slide_proj, slide_gain, layer_scale):
    tile_normed, tile_inverse, slide_normed, slide_inverse = saved_state
    embedded_grad = norm_back(entering_grad * slide_gain, slide_normed, slide_inverse).astype(
        jnp.bfloat16
    )
    lifted_grad = lax.dot_general(
        embedded_grad, slide_proj, (((1,), (1,)), ((), ())), preferred_element_type=jnp.float32
    )
    summed_grad = norm_back(lifted_grad * tile_gain, tile_normed, tile_inverse)
    mixed_grad = (layer_scale * summed_grad).astype(jnp.bfloat16)
    return (summed_grad, mixed_grad)


def shards(
    tile_features,
    head_outputs,
    out_proj,
    layer_scale,
    tile_gain,
    slide_proj,
    slide_gain,
    qkv_weight,
    slide_slot,
    slide_len,
    seg_log,
    rate_log,
    out_grad,
):
    seq_count = lax.axis_size("seq")
    seq_place = lax.axis_index("seq")
    mp_count = lax.axis_size("mp")
    mp_place = lax.axis_index("mp")
    row_count, width_part = tile_features.shape
    share_rows = row_count // mp_count
    head_cols = qkv_weight.shape[2]
    local_heads = head_cols // HEAD_DIM
    group_size = 1 << SPAN_LOG
    group_count = group_size * row_count
    capacity = 2 * (row_count // seq_count)
    slot_total = seq_count * capacity
    column = mp_place * width_part
    weight_flat = qkv_weight.reshape(qkv_weight.shape[0], 3 * head_cols)
    scale = HEAD_DIM ** (-0.5)
    term = layer_scale * jnp.dot(head_outputs, out_proj, preferred_element_type=jnp.float32)
    own_block = lax.dynamic_slice_in_dim(term, column, width_part, 1) + tile_features.astype(
        jnp.float32
    )
    summed = share_sum(lax.dynamic_update_slice_in_dim(term, own_block, column, 1))
    entering, saved_state = tile_forward(summed, tile_gain, slide_proj, slide_gain)
    projected = jnp.dot(entering, weight_flat, preferred_element_type=jnp.float32).astype(
        jnp.bfloat16
    )
    tile_index = jnp.arange(row_count, dtype=jnp.int32)
    my_slots = lax.dynamic_slice_in_dim(slide_slot, seq_place * row_count, row_count, 0)
    target = my_slots // row_count
    send_rank = jnp.sum(
        ((target[:, None] == target[None, :]) & (tile_index[None, :] < tile_index[:, None])).astype(
            jnp.int32
        ),
        axis=1,
    )
    send_slot = target * capacity + send_rank
    every_tile = jnp.arange(slide_slot.shape[0], dtype=jnp.int32)
    anchor_all = jnp.zeros_like(slide_slot).at[slide_slot].set(every_tile)
    anchor = lax.dynamic_slice_in_dim(anchor_all, seq_place * row_count, row_count, 0)
    anchor_device = anchor // row_count
    anchor_row = anchor % row_count
    recv_rank = jnp.sum(
        (
            (anchor_device[:, None] == anchor_device[None, :])
            & (anchor_row[None, :] < anchor_row[:, None])
        ).astype(jnp.int32),
        axis=1,
    )
    recv_slot = anchor_device * capacity + recv_rank

    def pack(values, slot_list):
        slot_table = jnp.full((slot_total,), row_count, jnp.int32).at[slot_list].set(tile_index)
        padded = jnp.concatenate([values, jnp.zeros((1, values.shape[1]), values.dtype)], axis=0)
        return padded[slot_table].reshape(seq_count, capacity, values.shape[1])

    def unpack(buffer, slot_list):
        return buffer.reshape(slot_total, buffer.shape[2])[slot_list]

    arriving = unpack(reroute(pack(projected, send_slot)), recv_slot)
    queries = arriving[:, :head_cols]
    stacked = group_collect(
        jnp.stack([arriving[:, head_cols : 2 * head_cols], arriving[:, 2 * head_cols :]]), seq_place
    )
    keys_all = stacked[0].reshape(group_count, local_heads, HEAD_DIM)
    values_all = stacked[1].reshape(group_count, local_heads, HEAD_DIM)
    query_heads = queries.reshape(row_count, local_heads, HEAD_DIM)
    here_pos = seq_place * row_count + tile_index
    group_first = seq_place // group_size * group_count
    group_pos = group_first + jnp.arange(group_count, dtype=jnp.int32)
    here_slide = slide_ids(here_pos, slide_len)
    group_slide = slide_ids(group_pos, slide_len)
    head_start = mp_place * local_heads
    widths = row_count * jnp.left_shift(
        jnp.int32(1), lax.dynamic_slice_in_dim(seg_log, head_start, local_heads, 0)
    )
    strides = jnp.left_shift(
        jnp.int32(1), lax.dynamic_slice_in_dim(rate_log, head_start, local_heads, 0)
    )
    allowed = visible(here_pos, group_pos, here_slide, group_slide, widths, strides)
    scores = (
        jnp.einsum("ihd,jhd->hij", query_heads, keys_all, preferred_element_type=jnp.float32)
        * scale
    )
    probability = softmax_rows(scores, allowed)
    rounded = probability.astype(jnp.bfloat16)
    slide_heads = (
        jnp.einsum("hij,jhd->ihd", rounded, values_all, preferred_element_type=jnp.float32)
        .astype(jnp.bfloat16)
        .reshape(row_count, head_cols)
    )
    upstream = out_grad.reshape(row_count, local_heads, HEAD_DIM)
    prob_grad = jnp.einsum("ihd,jhd->hij", upstream, values_all, preferred_element_type=jnp.float32)
    delta = jnp.sum(probability * prob_grad, axis=-1, keepdims=True)
    score_grad = (probability * (prob_grad - delta)).astype(jnp.bfloat16)
    query_grad = (
        jnp.einsum("hij,jhd->ihd", score_grad, keys_all, preferred_element_type=jnp.float32) * scale
    ).astype(jnp.bfloat16)
    key_part = (
        jnp.einsum("hij,ihd->jhd", score_grad, query_heads, preferred_element_type=jnp.float32)
        * scale
    )
    value_part = jnp.einsum("hij,ihd->jhd", rounded, upstream, preferred_element_type=jnp.float32)
    reduced = group_reduce(
        jnp.stack(
            [key_part.reshape(group_count, head_cols), value_part.reshape(group_count, head_cols)]
        ),
        seq_place,
    )
    key_grad = reduced[0].astype(jnp.bfloat16)
    value_grad = reduced[1].astype(jnp.bfloat16)
    local_grad = jnp.concatenate(
        [query_grad.reshape(row_count, head_cols), key_grad, value_grad], axis=1
    )
    returning = unpack(reroute(pack(local_grad, recv_slot)), send_slot)
    entering_grad = share_sum(
        lax.dot_general(
            returning, weight_flat, (((1,), (1,)), ((), ())), preferred_element_type=jnp.float32
        )
    )
    summed_grad, mixed_grad = tile_backward(
        entering_grad, saved_state, tile_gain, slide_proj, slide_gain, layer_scale
    )
    tile_grad = lax.dynamic_slice_in_dim(summed_grad, mp_place * share_rows, share_rows, 0).astype(
        jnp.bfloat16
    )
    head_grad = lax.dot_general(
        mixed_grad, out_proj, (((1,), (1,)), ((), ())), preferred_element_type=jnp.float32
    ).astype(jnp.bfloat16)
    return (slide_heads, tile_grad, head_grad)


F32 = jnp.float32
BF16 = jnp.bfloat16
MESH = pl.DeviceIdType.MESH
HIDDEN = -1e30
GROUP_SEQ = 1 << SPAN_LOG
QUAD = 4
VMEM_LIMIT = 65472 * 1024


def rows_dot(left, right):
    return lax.dot_general(left, right, (((1,), (1,)), ((), ())), preferred_element_type=F32)


def cols_dot(left, right):
    return lax.dot_general(left, right, (((0,), (0,)), ((), ())), preferred_element_type=F32)


def plain_dot(left, right):
    return jnp.dot(left, right, preferred_element_type=F32)


def step_kernel(
    features_hbm,
    outputs_hbm,
    out_proj_hbm,
    layer_scale_hbm,
    tile_gain_hbm,
    slide_proj_hbm,
    slide_gain_hbm,
    weight_hbm,
    slot_hbm,
    len_ref,
    seg_ref,
    rate_ref,
    grad_hbm,
    heads_out,
    tile_out,
    head_out,
    features_ref,
    outputs_ref,
    out_proj_ref,
    layer_scale_ref,
    tile_gain_ref,
    slide_proj_ref,
    slide_gain_ref,
    weight_ref,
    slot_ref,
    upstream_all,
    term_ref,
    first_out,
    first_in,
    second_out,
    second_in,
    entering_all,
    query_ref,
    key_ref,
    value_ref,
    upstream_ref,
    bias_row,
    bias_col,
    score_buf,
    grad_buf,
    stats_pad,
    stats_all,
    heads_all,
    back_ref,
    back_first_out,
    back_first_in,
    back_second_out,
    back_second_in,
    mixed_all,
    load_sem,
    up_send,
    up_recv,
    scatter_send,
    scatter_recv,
    z_send,
    z_recv,
    x_send,
    x_recv,
    core_send,
    core_recv,
    stats_send,
    stats_recv,
    heads_send,
    heads_recv,
    back_send,
    back_recv,
    mixed_send,
    mixed_recv,
):
    rows, width_part = features_ref.shape
    total = GROUP_SEQ * rows
    share = rows // QUAD
    head_cols = grad_hbm.shape[1]
    local_heads = head_cols // HEAD_DIM
    seq = lax.axis_index("seq")
    mp = lax.axis_index("mp")
    sibling = mp + 1 - 2 * (mp % 2)
    across = (mp + 2) % QUAD
    corner = (sibling + 2) % QUAD

    def remote(source, target, send, recv, where):
        return pltpu.make_async_remote_copy(
            src_ref=source,
            dst_ref=target,
            send_sem=send,
            recv_sem=recv,
            device_id=where,
            device_id_type=MESH,
        )

    barrier = pltpu.get_barrier_semaphore()
    for offset in range(1, GROUP_SEQ):
        pl.semaphore_signal(
            barrier, inc=1, device_id={"seq": (seq + offset) % GROUP_SEQ}, device_id_type=MESH
        )
    for offset in range(1, QUAD):
        pl.semaphore_signal(
            barrier, inc=1, device_id={"mp": (mp + offset) % QUAD}, device_id_type=MESH
        )

    loads = [
        pltpu.make_async_copy(source, target, load_sem.at[index])
        for index, (source, target) in enumerate(
            (
                (outputs_hbm, outputs_ref),
                (out_proj_hbm, out_proj_ref),
                (layer_scale_hbm, layer_scale_ref),
                (features_hbm, features_ref),
                (slot_hbm, slot_ref),
                (tile_gain_hbm, tile_gain_ref),
                (slide_gain_hbm, slide_gain_ref),
                (grad_hbm, upstream_all.at[seq]),
                (slide_proj_hbm, slide_proj_ref),
                (weight_hbm, weight_ref),
            )
        )
    ]
    for load in loads:
        load.start()
    for load in loads[:4]:
        load.wait()
    layer_scale = layer_scale_ref[...].reshape(1, layer_scale_ref.shape[0])
    term_ref[...] = layer_scale * plain_dot(outputs_ref[...], out_proj_ref[...])
    own_cols = pl.ds(pl.multiple_of(mp * width_part, 128), width_part)
    term_ref[:, own_cols] += features_ref[...].astype(F32)

    def share_of(place):
        return pl.ds(pl.multiple_of(place * share, 16), share)

    pl.semaphore_wait(barrier, GROUP_SEQ - 1 + QUAD - 1)

    def scatter_first(source, out_buf, in_buf, send, recv):
        copies = []
        for slot, place in ((1, corner), (0, sibling)):
            out_buf[slot] = source[share_of(place), :].astype(BF16)
            copy = remote(
                out_buf.at[slot], in_buf.at[slot], send.at[slot], recv.at[slot], {"mp": sibling}
            )
            copy.start()
            copies.append(copy)
        return copies

    def scatter_second(source, copies, in_buf, out_ref, in_ref, send, recv):
        copies[0].wait_recv()
        out_ref[...] = (source[share_of(across), :] + in_buf[1].astype(F32)).astype(BF16)
        copy = remote(out_ref, in_ref, send.at[2], recv.at[2], {"mp": across})
        copy.start()
        return copies + [copy]

    def scatter_third(source, copies, in_buf, in_ref):
        copies[1].wait_recv()
        partial = source[share_of(mp), :] + in_buf[0].astype(F32)
        copies[2].wait_recv()
        for each in copies:
            each.wait_send()
        return partial + in_ref[...].astype(F32)

    first = scatter_first(term_ref, first_out, first_in, scatter_send, scatter_recv)

    up_copies = []
    for offset in range(1, GROUP_SEQ):
        copy = remote(
            grad_hbm,
            upstream_all.at[seq],
            up_send.at[offset - 1],
            up_recv.at[offset - 1],
            {"seq": (seq + offset) % GROUP_SEQ},
        )
        copy.start()
        up_copies.append(copy)

    second = scatter_second(
        term_ref, first, first_in, second_out, second_in, scatter_send, scatter_recv
    )
    for load in loads[4:8]:
        load.wait()
    slots = slot_ref[...].reshape(1, total)
    tile_gain = tile_gain_ref[...].reshape(1, tile_gain_ref.shape[0])
    slide_gain = slide_gain_ref[...].reshape(1, slide_gain_ref.shape[0])
    base = seq * rows
    bounds = []
    reached = 0
    for index in range(len_ref.shape[0]):
        reached = reached + len_ref[index]
        bounds.append(reached)
    slide_of = jnp.zeros_like(slots)
    for bound in bounds:
        slide_of = slide_of + (slots >= bound).astype(jnp.int32)
    window_of = jnp.zeros_like(slots)
    for index in range(1, GROUP_SEQ):
        window_of = window_of + (slots >= index * rows).astype(jnp.int32)
    lane_all = lax.broadcasted_iota(jnp.int32, (rows, total), 1)
    sub_all = lax.broadcasted_iota(jnp.int32, (rows, total), 0)
    pick_own = (lane_all == sub_all + base).astype(BF16)
    eye = (
        lax.broadcasted_iota(jnp.int32, (total, total), 0)
        == lax.broadcasted_iota(jnp.int32, (total, total), 1)
    ).astype(BF16)
    for head in range(local_heads):
        seg = seg_ref[mp * local_heads + head]
        rate = rate_ref[mp * local_heads + head]
        stride_mask = jnp.left_shift(jnp.int32(1), rate) - 1
        code = (
            slide_of * (GROUP_SEQ * GROUP_SEQ)
            + jnp.right_shift(window_of, jnp.full_like(window_of, seg)) * GROUP_SEQ
            + (slots & stride_mask)
        )
        code_rows = jnp.broadcast_to(code.astype(F32), (rows, total))
        code_bf = code_rows.astype(BF16)
        code_own_lane = rows_dot(code_bf, pick_own)
        code_all_sub = rows_dot(eye, code_bf)
        bias_row[head] = jnp.where(code_all_sub == code_own_lane[:1], 0.0, HIDDEN)
        code_own_sub = rows_dot(pick_own, code_bf)
        bias_col[head] = jnp.where(code_own_sub[:, :1] == code_rows, 0.0, HIDDEN)
    slot_rows = jnp.broadcast_to(slots, (rows, total))
    pick_heads = (slot_rows == sub_all + base).astype(BF16)
    arrange = (
        jnp.broadcast_to(slots, (total, total)) == lax.broadcasted_iota(jnp.int32, (total, total), 0)
    ).astype(BF16)

    summed = scatter_third(term_ref, second, first_in, second_in)
    tile_normed, tile_inverse = norm_parts(summed)
    lifted = (tile_normed * tile_gain).astype(BF16)
    loads[8].wait()
    embedded = plain_dot(lifted, slide_proj_ref[...])
    slide_normed, slide_inverse = norm_parts(embedded)
    entering_all[seq, mp] = (slide_normed * slide_gain).astype(BF16)

    pending = []

    def forward(source_seq, source_mp, send, recv, where):
        copy = remote(
            entering_all.at[source_seq, source_mp],
            entering_all.at[source_seq, source_mp],
            send,
            recv,
            where,
        )
        copy.start()
        pending.append(copy)
        return copy

    z_copies = []
    for offset in range(1, GROUP_SEQ):
        z_copies.append(
            forward(
                seq,
                mp,
                z_send.at[offset - 1],
                z_recv.at[offset - 1],
                {"seq": (seq + offset) % GROUP_SEQ},
            )
        )
    x_copies = [forward(seq, mp, x_send.at[0], x_recv.at[0], {"mp": across})]
    core_copies = [forward(seq, mp, core_send.at[0], core_recv.at[0], {"mp": sibling})]

    for copy in up_copies:
        copy.wait()
    upstream_ref[...] = cols_dot(arrange, upstream_all[...].reshape(total, head_cols)).astype(BF16)

    for offset in range(1, GROUP_SEQ):
        origin = (seq + GROUP_SEQ - offset) % GROUP_SEQ
        z_copies[offset - 1].wait_recv()
        x_copies.append(forward(origin, mp, x_send.at[offset], x_recv.at[offset], {"mp": across}))
        core_copies.append(
            forward(origin, mp, core_send.at[offset], core_recv.at[offset], {"mp": sibling})
        )
    for offset in range(GROUP_SEQ):
        origin = (seq + GROUP_SEQ - offset) % GROUP_SEQ
        x_copies[offset].wait_recv()
        core_copies.append(
            forward(
                origin,
                across,
                core_send.at[GROUP_SEQ + offset],
                core_recv.at[GROUP_SEQ + offset],
                {"mp": sibling},
            )
        )
    loads[9].wait()
    for copy in core_copies:
        copy.wait_recv()
    entering = entering_all[...].reshape(total, entering_all.shape[3])
    query_ref[...] = (rows_dot(entering, weight_ref[0]).astype(BF16).astype(F32) * SCALE).astype(
        BF16
    )
    key_ref[...] = rows_dot(entering, weight_ref[1]).astype(BF16)
    value_ref[...] = rows_dot(entering, weight_ref[2]).astype(BF16)
    for copy in pending:
        copy.wait_send()

    own_rows = pl.ds(pl.multiple_of(base, 64), rows)

    def head_only(values, head):
        lane_head = lax.broadcasted_iota(jnp.int32, values.shape, 1) // HEAD_DIM
        return jnp.where(lane_head == head, values, jnp.zeros_like(values))

    stats_pad[...] = jnp.zeros_like(stats_pad)
    heads_sum = jnp.zeros((rows, head_cols), F32)
    query_sum = jnp.zeros((rows, head_cols), F32)
    keys = key_ref[...]
    values = value_ref[...]
    for head in range(local_heads):
        scores = rows_dot(keys, head_only(query_ref[own_rows, :], head)) + bias_row[head]
        row_max = jnp.max(scores, axis=0, keepdims=True)
        raised = jnp.exp(scores - row_max)
        row_sum = jnp.sum(raised, axis=0, keepdims=True)
        probability = raised * (1.0 / row_sum)
        prob_grad = rows_dot(values, head_only(upstream_ref[own_rows, :], head))
        delta = jnp.sum(probability * prob_grad, axis=0, keepdims=True)
        stats_pad[2 * head : 2 * head + 1, :rows] = row_max + jnp.log(row_sum)
        stats_pad[2 * head + 1 : 2 * head + 2, :rows] = delta
        score_grad = (probability * (prob_grad - delta)).astype(BF16)
        heads_sum = heads_sum + cols_dot(probability.astype(BF16), head_only(values, head))
        query_sum = query_sum + cols_dot(score_grad, head_only(keys, head))
    stats_all[seq] = pltpu.roll(stats_pad[...], base, 1)
    heads_all[seq] = heads_sum.astype(BF16)
    stats_copies = []
    heads_copies = []
    for offset in range(1, GROUP_SEQ):
        copy = remote(
            stats_all.at[seq],
            stats_all.at[seq],
            stats_send.at[offset - 1],
            stats_recv.at[offset - 1],
            {"seq": (seq + offset) % GROUP_SEQ},
        )
        copy.start()
        stats_copies.append(copy)
    for offset in range(1, GROUP_SEQ):
        copy = remote(
            heads_all.at[seq],
            heads_all.at[seq],
            heads_send.at[offset - 1],
            heads_recv.at[offset - 1],
            {"seq": (seq + offset) % GROUP_SEQ},
        )
        copy.start()
        heads_copies.append(copy)
    own_keys = key_ref[own_rows, :]
    own_values = value_ref[own_rows, :]
    queries = query_ref[...]
    upstream = upstream_ref[...]
    for head in range(local_heads):
        score_buf[head] = rows_dot(own_keys, head_only(queries, head)) + bias_col[head]
        grad_buf[head] = rows_dot(own_values, head_only(upstream, head))
    for copy in stats_copies:
        copy.wait()
    stats = stats_all[0] + stats_all[1] + stats_all[2] + stats_all[3]
    key_sum = jnp.zeros((rows, head_cols), F32)
    value_sum = jnp.zeros((rows, head_cols), F32)
    for head in range(local_heads):
        probability = jnp.exp(score_buf[head] - stats[2 * head : 2 * head + 1])
        score_grad = probability * (grad_buf[head] - stats[2 * head + 1 : 2 * head + 2])
        value_sum = value_sum + plain_dot(probability.astype(BF16), head_only(upstream, head))
        key_sum = key_sum + plain_dot(score_grad.astype(BF16), head_only(queries, head))
    back_ref[...] = (
        plain_dot((query_sum * SCALE).astype(BF16), weight_ref[0])
        + plain_dot(key_sum.astype(BF16), weight_ref[1])
        + plain_dot(value_sum.astype(BF16), weight_ref[2])
    )
    back_first = scatter_first(back_ref, back_first_out, back_first_in, back_send, back_recv)
    back_second = scatter_second(
        back_ref, back_first, back_first_in, back_second_out, back_second_in, back_send, back_recv
    )
    entering_grad = scatter_third(back_ref, back_second, back_first_in, back_second_in)
    embedded_grad = norm_back(
        entering_grad * slide_gain, slide_normed, slide_inverse
    ).astype(BF16)
    lifted_grad = rows_dot(embedded_grad, slide_proj_ref[...])
    summed_grad = norm_back(lifted_grad * tile_gain, tile_normed, tile_inverse)
    mixed_all[mp] = (layer_scale * summed_grad).astype(BF16)

    def mixed_move(place, index, where):
        copy = remote(
            mixed_all.at[place],
            mixed_all.at[place],
            mixed_send.at[index],
            mixed_recv.at[index],
            {"mp": where},
        )
        copy.start()
        return copy

    mixed_x = mixed_move(mp, 0, across)
    mixed_core = mixed_move(mp, 1, sibling)
    tile_out[...] = summed_grad.astype(BF16)
    for copy in heads_copies:
        copy.wait()
    heads_out[...] = plain_dot(pick_heads, heads_all[...].reshape(total, head_cols)).astype(BF16)
    mixed_x.wait()
    mixed_corner = mixed_move(across, 2, sibling)
    mixed_core.wait()
    mixed_corner.wait()
    head_out[...] = rows_dot(
        mixed_all[...].reshape(rows, mixed_all.shape[2]), out_proj_ref[...]
    ).astype(BF16)


def fused_shards(
    tile_features,
    head_outputs,
    out_proj,
    layer_scale,
    tile_gain,
    slide_proj,
    slide_gain,
    qkv_weight,
    slide_slot,
    slide_len,
    seg_log,
    rate_log,
    out_grad,
):
    rows, width_part = tile_features.shape
    width = out_proj.shape[1]
    slide_width = slide_proj.shape[1]
    head_cols = qkv_weight.shape[2]
    local_heads = head_cols // HEAD_DIM
    share = rows // QUAD
    total = GROUP_SEQ * rows
    vmem = pl.BlockSpec(memory_space=pltpu.VMEM)
    smem = pl.BlockSpec(memory_space=pltpu.SMEM)
    hbm = pl.BlockSpec(memory_space=pltpu.HBM)
    dma = pltpu.SemaphoreType.DMA
    return pl.pallas_call(
        step_kernel,
        out_shape=(
            jax.ShapeDtypeStruct((rows, head_cols), BF16),
            jax.ShapeDtypeStruct((share, width), BF16),
            jax.ShapeDtypeStruct((rows, width_part), BF16),
        ),
        in_specs=[hbm] * 9 + [smem] * 3 + [hbm],
        out_specs=(vmem, vmem, vmem),
        scratch_shapes=[
            pltpu.VMEM((rows, width_part), BF16),
            pltpu.VMEM((rows, width_part), BF16),
            pltpu.VMEM((width_part, width), BF16),
            pltpu.VMEM((width,), F32),
            pltpu.VMEM((width,), F32),
            pltpu.VMEM((width, slide_width), BF16),
            pltpu.VMEM((slide_width,), F32),
            pltpu.VMEM((3, head_cols, slide_width), BF16),
            pltpu.VMEM((total,), jnp.int32),
            pltpu.VMEM((GROUP_SEQ, rows, head_cols), BF16),
            pltpu.VMEM((rows, width), F32),
            pltpu.VMEM((2, share, width), BF16),
            pltpu.VMEM((2, share, width), BF16),
            pltpu.VMEM((share, width), BF16),
            pltpu.VMEM((share, width), BF16),
            pltpu.VMEM((GROUP_SEQ, QUAD, share, slide_width), BF16),
            pltpu.VMEM((total, head_cols), BF16),
            pltpu.VMEM((total, head_cols), BF16),
            pltpu.VMEM((total, head_cols), BF16),
            pltpu.VMEM((total, head_cols), BF16),
            pltpu.VMEM((local_heads, total, rows), F32),
            pltpu.VMEM((local_heads, rows, total), F32),
            pltpu.VMEM((local_heads, rows, total), F32),
            pltpu.VMEM((local_heads, rows, total), F32),
            pltpu.VMEM((8, total), F32),
            pltpu.VMEM((GROUP_SEQ, 8, total), F32),
            pltpu.VMEM((GROUP_SEQ, rows, head_cols), BF16),
            pltpu.VMEM((rows, slide_width), F32),
            pltpu.VMEM((2, share, slide_width), BF16),
            pltpu.VMEM((2, share, slide_width), BF16),
            pltpu.VMEM((share, slide_width), BF16),
            pltpu.VMEM((share, slide_width), BF16),
            pltpu.VMEM((QUAD, share, width), BF16),
            dma((10,)),
            dma((3,)),
            dma((3,)),
            dma((3,)),
            dma((3,)),
            dma((3,)),
            dma((3,)),
            dma((4,)),
            dma((4,)),
            dma((8,)),
            dma((8,)),
            dma((3,)),
            dma((3,)),
            dma((3,)),
            dma((3,)),
            dma((3,)),
            dma((3,)),
            dma((3,)),
            dma((3,)),
        ],
        compiler_params=pltpu.CompilerParams(
            collective_id=0, has_side_effects=True, vmem_limit_bytes=VMEM_LIMIT
        ),
        name="slide_step",
    )(
        tile_features,
        head_outputs,
        out_proj,
        layer_scale,
        tile_gain,
        slide_proj,
        slide_gain,
        jnp.transpose(qkv_weight, (1, 2, 0)),
        slide_slot,
        slide_len,
        seg_log,
        rate_log,
        out_grad,
    )


def solution(mesh):
    fused = mesh.shape["seq"] == GROUP_SEQ and mesh.shape["mp"] == QUAD
    body = fused_shards if fused else shards
    in_specs = (
        P(("groups", "seq"), "mp"),
        P(("groups", "seq"), "mp"),
        P("mp", None),
        P(),
        P(),
        P(),
        P(),
        P(None, None, "mp"),
        P("groups"),
        P("groups"),
        P(),
        P(),
        P(("groups", "seq"), "mp"),
    )
    out_specs = (
        P(("groups", "seq"), "mp"),
        P(("groups", "seq", "mp"), None),
        P(("groups", "seq"), "mp"),
    )
    return jax.shard_map(body, mesh=mesh, in_specs=in_specs, out_specs=out_specs, check_vma=False)
```

```python
import jax
import jax.numpy as jnp
from jax import lax
from jax.experimental import pallas as pl
from jax.experimental.pallas import tpu as pltpu
from jax.sharding import PartitionSpec as P

HEAD_DIM = 64
SPAN_LOG = 2


EPSILON = 1e-06
SCALE = HEAD_DIM ** (-0.5)


def swapped(block, axis, distance):
    count = lax.axis_size(axis)
    route = []
    for low in range(count):
        high = low | 1 << distance
        if high != low and high < count:
            route += [(low, high), (high, low)]
    return lax.ppermute(block, axis, route)


def norm_parts(values):
    center = values - jnp.mean(values, axis=-1, keepdims=True)
    inverse = 1.0 / jnp.sqrt(jnp.mean(center * center, axis=-1, keepdims=True) + EPSILON)
    return (center * inverse, inverse)


def norm_back(upstream, normed, inverse):
    first_mean = jnp.mean(upstream, axis=-1, keepdims=True)
    second_mean = jnp.mean(upstream * normed, axis=-1, keepdims=True)
    return inverse * (upstream - first_mean - normed * second_mean)


def slide_ids(positions, slide_len):
    bounds = jnp.cumsum(slide_len)
    return jnp.sum((positions[:, None] >= bounds[None, :]).astype(jnp.int32), axis=1)


def visible(query_pos, key_pos, query_slide, key_slide, widths, strides):
    same_slide = (query_slide[:, None] == key_slide[None, :])[None, :, :]
    window = widths[:, None, None]
    same_window = query_pos[None, :, None] // window == key_pos[None, None, :] // window
    stride = strides[:, None, None]
    same_phase = query_pos[None, :, None] % stride == key_pos[None, None, :] % stride
    return same_slide & same_window & same_phase


def softmax_rows(scores, allowed):
    shifted = jnp.where(allowed, scores, -jnp.inf)
    row_max = jnp.max(shifted, axis=-1, keepdims=True)
    raised = jnp.exp(shifted - row_max)
    return raised / jnp.sum(raised, axis=-1, keepdims=True)


def share_sum(values):
    return lax.psum(values, "mp")


def reroute(buffer):
    return lax.all_to_all(buffer, "seq", split_axis=0, concat_axis=0, tiled=True)


def join_halves(own_part, partner_part, upper_half):
    return jnp.where(
        upper_half,
        jnp.concatenate([partner_part, own_part], axis=1),
        jnp.concatenate([own_part, partner_part], axis=1),
    )


def group_collect(stacked, seq_place):
    for bit_place in range(SPAN_LOG):
        partner_part = swapped(stacked, "seq", bit_place)
        stacked = join_halves(stacked, partner_part, seq_place >> bit_place & 1 == 1)
    return stacked


def group_reduce(stacked, seq_place):
    for bit_place in reversed(range(SPAN_LOG)):
        half_rows = stacked.shape[1] // 2
        upper_half = seq_place >> bit_place & 1 == 1
        lower_part = stacked[:, :half_rows]
        higher_part = stacked[:, half_rows:]
        kept_part = jnp.where(upper_half, higher_part, lower_part)
        given_part = jnp.where(upper_half, lower_part, higher_part)
        stacked = kept_part + swapped(given_part.astype(jnp.bfloat16), "seq", bit_place).astype(
            given_part.dtype
        )
    return stacked


def tile_forward(summed, tile_gain, slide_proj, slide_gain):
    tile_normed, tile_inverse = norm_parts(summed)
    lifted = (tile_normed * tile_gain).astype(jnp.bfloat16)
    embedded = jnp.dot(lifted, slide_proj, preferred_element_type=jnp.float32)
    slide_normed, slide_inverse = norm_parts(embedded)
    entering = (slide_normed * slide_gain).astype(jnp.bfloat16)
    return (entering, (tile_normed, tile_inverse, slide_normed, slide_inverse))


def tile_backward(entering_grad, saved_state, tile_gain, slide_proj, slide_gain, layer_scale):
    tile_normed, tile_inverse, slide_normed, slide_inverse = saved_state
    embedded_grad = norm_back(entering_grad * slide_gain, slide_normed, slide_inverse).astype(
        jnp.bfloat16
    )
    lifted_grad = lax.dot_general(
        embedded_grad, slide_proj, (((1,), (1,)), ((), ())), preferred_element_type=jnp.float32
    )
    summed_grad = norm_back(lifted_grad * tile_gain, tile_normed, tile_inverse)
    mixed_grad = (layer_scale * summed_grad).astype(jnp.bfloat16)
    return (summed_grad, mixed_grad)


def shards(
    tile_features,
    head_outputs,
    out_proj,
    layer_scale,
    tile_gain,
    slide_proj,
    slide_gain,
    qkv_weight,
    slide_slot,
    slide_len,
    seg_log,
    rate_log,
    out_grad,
):
    seq_count = lax.axis_size("seq")
    seq_place = lax.axis_index("seq")
    mp_count = lax.axis_size("mp")
    mp_place = lax.axis_index("mp")
    row_count, width_part = tile_features.shape
    share_rows = row_count // mp_count
    head_cols = qkv_weight.shape[2]
    local_heads = head_cols // HEAD_DIM
    group_size = 1 << SPAN_LOG
    group_count = group_size * row_count
    capacity = 2 * (row_count // seq_count)
    slot_total = seq_count * capacity
    column = mp_place * width_part
    weight_flat = qkv_weight.reshape(qkv_weight.shape[0], 3 * head_cols)
    scale = HEAD_DIM ** (-0.5)
    term = layer_scale * jnp.dot(head_outputs, out_proj, preferred_element_type=jnp.float32)
    own_block = lax.dynamic_slice_in_dim(term, column, width_part, 1) + tile_features.astype(
        jnp.float32
    )
    summed = share_sum(lax.dynamic_update_slice_in_dim(term, own_block, column, 1))
    entering, saved_state = tile_forward(summed, tile_gain, slide_proj, slide_gain)
    projected = jnp.dot(entering, weight_flat, preferred_element_type=jnp.float32).astype(
        jnp.bfloat16
    )
    tile_index = jnp.arange(row_count, dtype=jnp.int32)
    my_slots = lax.dynamic_slice_in_dim(slide_slot, seq_place * row_count, row_count, 0)
    target = my_slots // row_count
    send_rank = jnp.sum(
        ((target[:, None] == target[None, :]) & (tile_index[None, :] < tile_index[:, None])).astype(
            jnp.int32
        ),
        axis=1,
    )
    send_slot = target * capacity + send_rank
    every_tile = jnp.arange(slide_slot.shape[0], dtype=jnp.int32)
    anchor_all = jnp.zeros_like(slide_slot).at[slide_slot].set(every_tile)
    anchor = lax.dynamic_slice_in_dim(anchor_all, seq_place * row_count, row_count, 0)
    anchor_device = anchor // row_count
    anchor_row = anchor % row_count
    recv_rank = jnp.sum(
        (
            (anchor_device[:, None] == anchor_device[None, :])
            & (anchor_row[None, :] < anchor_row[:, None])
        ).astype(jnp.int32),
        axis=1,
    )
    recv_slot = anchor_device * capacity + recv_rank

    def pack(values, slot_list):
        slot_table = jnp.full((slot_total,), row_count, jnp.int32).at[slot_list].set(tile_index)
        padded = jnp.concatenate([values, jnp.zeros((1, values.shape[1]), values.dtype)], axis=0)
        return padded[slot_table].reshape(seq_count, capacity, values.shape[1])

    def unpack(buffer, slot_list):
        return buffer.reshape(slot_total, buffer.shape[2])[slot_list]

    arriving = unpack(reroute(pack(projected, send_slot)), recv_slot)
    queries = arriving[:, :head_cols]
    stacked = group_collect(
        jnp.stack([arriving[:, head_cols : 2 * head_cols], arriving[:, 2 * head_cols :]]), seq_place
    )
    keys_all = stacked[0].reshape(group_count, local_heads, HEAD_DIM)
    values_all = stacked[1].reshape(group_count, local_heads, HEAD_DIM)
    query_heads = queries.reshape(row_count, local_heads, HEAD_DIM)
    here_pos = seq_place * row_count + tile_index
    group_first = seq_place // group_size * group_count
    group_pos = group_first + jnp.arange(group_count, dtype=jnp.int32)
    here_slide = slide_ids(here_pos, slide_len)
    group_slide = slide_ids(group_pos, slide_len)
    head_start = mp_place * local_heads
    widths = row_count * jnp.left_shift(
        jnp.int32(1), lax.dynamic_slice_in_dim(seg_log, head_start, local_heads, 0)
    )
    strides = jnp.left_shift(
        jnp.int32(1), lax.dynamic_slice_in_dim(rate_log, head_start, local_heads, 0)
    )
    allowed = visible(here_pos, group_pos, here_slide, group_slide, widths, strides)
    scores = (
        jnp.einsum("ihd,jhd->hij", query_heads, keys_all, preferred_element_type=jnp.float32)
        * scale
    )
    probability = softmax_rows(scores, allowed)
    rounded = probability.astype(jnp.bfloat16)
    slide_heads = (
        jnp.einsum("hij,jhd->ihd", rounded, values_all, preferred_element_type=jnp.float32)
        .astype(jnp.bfloat16)
        .reshape(row_count, head_cols)
    )
    upstream = out_grad.reshape(row_count, local_heads, HEAD_DIM)
    prob_grad = jnp.einsum("ihd,jhd->hij", upstream, values_all, preferred_element_type=jnp.float32)
    delta = jnp.sum(probability * prob_grad, axis=-1, keepdims=True)
    score_grad = (probability * (prob_grad - delta)).astype(jnp.bfloat16)
    query_grad = (
        jnp.einsum("hij,jhd->ihd", score_grad, keys_all, preferred_element_type=jnp.float32) * scale
    ).astype(jnp.bfloat16)
    key_part = (
        jnp.einsum("hij,ihd->jhd", score_grad, query_heads, preferred_element_type=jnp.float32)
        * scale
    )
    value_part = jnp.einsum("hij,ihd->jhd", rounded, upstream, preferred_element_type=jnp.float32)
    reduced = group_reduce(
        jnp.stack(
            [key_part.reshape(group_count, head_cols), value_part.reshape(group_count, head_cols)]
        ),
        seq_place,
    )
    key_grad = reduced[0].astype(jnp.bfloat16)
    value_grad = reduced[1].astype(jnp.bfloat16)
    local_grad = jnp.concatenate(
        [query_grad.reshape(row_count, head_cols), key_grad, value_grad], axis=1
    )
    returning = unpack(reroute(pack(local_grad, recv_slot)), send_slot)
    entering_grad = share_sum(
        lax.dot_general(
            returning, weight_flat, (((1,), (1,)), ((), ())), preferred_element_type=jnp.float32
        )
    )
    summed_grad, mixed_grad = tile_backward(
        entering_grad, saved_state, tile_gain, slide_proj, slide_gain, layer_scale
    )
    tile_grad = lax.dynamic_slice_in_dim(summed_grad, mp_place * share_rows, share_rows, 0).astype(
        jnp.bfloat16
    )
    head_grad = lax.dot_general(
        mixed_grad, out_proj, (((1,), (1,)), ((), ())), preferred_element_type=jnp.float32
    ).astype(jnp.bfloat16)
    return (slide_heads, tile_grad, head_grad)


F32 = jnp.float32
BF16 = jnp.bfloat16
MESH = pl.DeviceIdType.MESH
HIDDEN = -1e30
GROUP_SEQ = 1 << SPAN_LOG
QUAD = 4
VMEM_LIMIT = 65472 * 1024


def rows_dot(left, right):
    return lax.dot_general(left, right, (((1,), (1,)), ((), ())), preferred_element_type=F32)


def cols_dot(left, right):
    return lax.dot_general(left, right, (((0,), (0,)), ((), ())), preferred_element_type=F32)


def plain_dot(left, right):
    return jnp.dot(left, right, preferred_element_type=F32)


def step_kernel(
    features_hbm,
    outputs_hbm,
    out_proj_hbm,
    layer_scale_hbm,
    tile_gain_hbm,
    slide_proj_hbm,
    slide_gain_hbm,
    weight_hbm,
    slot_hbm,
    len_ref,
    seg_ref,
    rate_ref,
    grad_hbm,
    heads_out,
    tile_out,
    head_out,
    features_ref,
    outputs_ref,
    out_proj_ref,
    layer_scale_ref,
    tile_gain_ref,
    slide_proj_ref,
    slide_gain_ref,
    weight_ref,
    slot_ref,
    upstream_all,
    term_ref,
    first_out,
    first_in,
    second_out,
    second_in,
    entering_all,
    query_ref,
    key_ref,
    value_ref,
    upstream_ref,
    bias_row,
    bias_col,
    score_buf,
    grad_buf,
    stats_pad,
    stats_line,
    stats_all,
    heads_all,
    back_ref,
    back_first_out,
    back_first_in,
    back_second_out,
    back_second_in,
    mixed_all,
    load_sem,
    up_send,
    up_recv,
    scatter_send,
    scatter_recv,
    z_send,
    z_recv,
    x_send,
    x_recv,
    core_send,
    core_recv,
    stats_send,
    stats_recv,
    heads_send,
    heads_recv,
    back_send,
    back_recv,
    mixed_send,
    mixed_recv,
):
    rows, width_part = features_ref.shape
    total = GROUP_SEQ * rows
    share = rows // QUAD
    head_cols = grad_hbm.shape[1]
    local_heads = head_cols // HEAD_DIM
    seq = lax.axis_index("seq")
    mp = lax.axis_index("mp")
    sibling = mp + 1 - 2 * (mp % 2)
    across = (mp + 2) % QUAD
    corner = (sibling + 2) % QUAD

    def remote(source, target, send, recv, where):
        return pltpu.make_async_remote_copy(
            src_ref=source,
            dst_ref=target,
            send_sem=send,
            recv_sem=recv,
            device_id=where,
            device_id_type=MESH,
        )

    barrier = pltpu.get_barrier_semaphore()
    for offset in range(1, GROUP_SEQ):
        pl.semaphore_signal(
            barrier, inc=1, device_id={"seq": (seq + offset) % GROUP_SEQ}, device_id_type=MESH
        )
    for offset in range(1, QUAD):
        pl.semaphore_signal(
            barrier, inc=1, device_id={"mp": (mp + offset) % QUAD}, device_id_type=MESH
        )

    loads = [
        pltpu.make_async_copy(source, target, load_sem.at[index])
        for index, (source, target) in enumerate(
            (
                (outputs_hbm, outputs_ref),
                (out_proj_hbm, out_proj_ref),
                (layer_scale_hbm, layer_scale_ref),
                (features_hbm, features_ref),
                (slot_hbm, slot_ref),
                (tile_gain_hbm, tile_gain_ref),
                (slide_gain_hbm, slide_gain_ref),
                (grad_hbm, upstream_all.at[seq]),
                (slide_proj_hbm, slide_proj_ref),
                (weight_hbm, weight_ref),
            )
        )
    ]
    for load in loads:
        load.start()
    for load in loads[:4]:
        load.wait()
    layer_scale = layer_scale_ref[...].reshape(1, layer_scale_ref.shape[0])
    term_ref[...] = layer_scale * plain_dot(outputs_ref[...], out_proj_ref[...])
    own_cols = pl.ds(pl.multiple_of(mp * width_part, 128), width_part)
    term_ref[:, own_cols] += features_ref[...].astype(F32)

    def share_of(place):
        return pl.ds(pl.multiple_of(place * share, 16), share)

    pl.semaphore_wait(barrier, GROUP_SEQ - 1 + QUAD - 1)

    def scatter_first(source, out_buf, in_buf, send, recv):
        copies = []
        for slot, place in ((1, corner), (0, sibling)):
            out_buf[slot] = source[share_of(place), :].astype(BF16)
            copy = remote(
                out_buf.at[slot], in_buf.at[slot], send.at[slot], recv.at[slot], {"mp": sibling}
            )
            copy.start()
            copies.append(copy)
        return copies

    def scatter_second(source, copies, in_buf, out_ref, in_ref, send, recv):
        copies[0].wait_recv()
        out_ref[...] = (source[share_of(across), :] + in_buf[1].astype(F32)).astype(BF16)
        copy = remote(out_ref, in_ref, send.at[2], recv.at[2], {"mp": across})
        copy.start()
        return copies + [copy]

    def scatter_third(source, copies, in_buf, in_ref):
        copies[1].wait_recv()
        partial = source[share_of(mp), :] + in_buf[0].astype(F32)
        copies[2].wait_recv()
        for each in copies:
            each.wait_send()
        return partial + in_ref[...].astype(F32)

    first = scatter_first(term_ref, first_out, first_in, scatter_send, scatter_recv)

    up_copies = []
    for offset in range(1, GROUP_SEQ):
        copy = remote(
            grad_hbm,
            upstream_all.at[seq],
            up_send.at[offset - 1],
            up_recv.at[offset - 1],
            {"seq": (seq + offset) % GROUP_SEQ},
        )
        copy.start()
        up_copies.append(copy)

    second = scatter_second(
        term_ref, first, first_in, second_out, second_in, scatter_send, scatter_recv
    )
    for load in loads[4:8]:
        load.wait()
    slots = slot_ref[...].reshape(1, total)
    tile_gain = tile_gain_ref[...].reshape(1, tile_gain_ref.shape[0])
    slide_gain = slide_gain_ref[...].reshape(1, slide_gain_ref.shape[0])
    base = seq * rows
    bounds = []
    reached = 0
    for index in range(len_ref.shape[0]):
        reached = reached + len_ref[index]
        bounds.append(reached)
    slide_of = jnp.zeros_like(slots)
    for bound in bounds:
        slide_of = slide_of + (slots >= bound).astype(jnp.int32)
    window_of = jnp.zeros_like(slots)
    for index in range(1, GROUP_SEQ):
        window_of = window_of + (slots >= index * rows).astype(jnp.int32)
    lane_all = lax.broadcasted_iota(jnp.int32, (rows, total), 1)
    sub_all = lax.broadcasted_iota(jnp.int32, (rows, total), 0)
    pick_own = (lane_all == sub_all + base).astype(BF16)
    eye = (
        lax.broadcasted_iota(jnp.int32, (total, total), 0)
        == lax.broadcasted_iota(jnp.int32, (total, total), 1)
    ).astype(BF16)
    for head in range(local_heads):
        seg = seg_ref[mp * local_heads + head]
        rate = rate_ref[mp * local_heads + head]
        stride_mask = jnp.left_shift(jnp.int32(1), rate) - 1
        code = (
            slide_of * (GROUP_SEQ * GROUP_SEQ)
            + jnp.right_shift(window_of, jnp.full_like(window_of, seg)) * GROUP_SEQ
            + (slots & stride_mask)
        )
        code_rows = jnp.broadcast_to(code.astype(F32), (rows, total))
        code_bf = code_rows.astype(BF16)
        code_own_lane = rows_dot(code_bf, pick_own)
        code_all_sub = rows_dot(eye, code_bf)
        bias_row[head] = jnp.where(code_all_sub == code_own_lane[:1], 0.0, HIDDEN)
        code_own_sub = rows_dot(pick_own, code_bf)
        bias_col[head] = jnp.where(code_own_sub[:, :1] == code_rows, 0.0, HIDDEN)
    slot_rows = jnp.broadcast_to(slots, (rows, total))
    pick_heads = (slot_rows == sub_all + base).astype(BF16)
    arrange = (
        jnp.broadcast_to(slots, (total, total)) == lax.broadcasted_iota(jnp.int32, (total, total), 0)
    ).astype(BF16)

    summed = scatter_third(term_ref, second, first_in, second_in)
    tile_normed, tile_inverse = norm_parts(summed)
    lifted = (tile_normed * tile_gain).astype(BF16)
    loads[8].wait()
    embedded = plain_dot(lifted, slide_proj_ref[...])
    slide_normed, slide_inverse = norm_parts(embedded)
    entering_all[seq, mp] = (slide_normed * slide_gain).astype(BF16)

    pending = []

    def forward(source_seq, source_mp, send, recv, where):
        copy = remote(
            entering_all.at[source_seq, source_mp],
            entering_all.at[source_seq, source_mp],
            send,
            recv,
            where,
        )
        copy.start()
        pending.append(copy)
        return copy

    z_copies = []
    for offset in range(1, GROUP_SEQ):
        z_copies.append(
            forward(
                seq,
                mp,
                z_send.at[offset - 1],
                z_recv.at[offset - 1],
                {"seq": (seq + offset) % GROUP_SEQ},
            )
        )
    x_copies = [forward(seq, mp, x_send.at[0], x_recv.at[0], {"mp": across})]
    core_copies = [forward(seq, mp, core_send.at[0], core_recv.at[0], {"mp": sibling})]

    def project(offset):
        core_copies[offset].wait_recv()
        core_copies[GROUP_SEQ + offset].wait_recv()
        origin = (seq + GROUP_SEQ - offset) % GROUP_SEQ
        entering = entering_all[origin].reshape(rows, entering_all.shape[3])
        block = pl.ds(pl.multiple_of(origin * rows, 64), rows)
        query = rows_dot(entering, weight_ref[0]).astype(BF16)
        query_ref[block, :] = (query.astype(F32) * SCALE).astype(BF16)
        key_ref[block, :] = rows_dot(entering, weight_ref[1]).astype(BF16)
        value_ref[block, :] = rows_dot(entering, weight_ref[2]).astype(BF16)

    for copy in up_copies:
        copy.wait()
    upstream_ref[...] = cols_dot(arrange, upstream_all[...].reshape(total, head_cols)).astype(BF16)

    for offset in range(1, GROUP_SEQ):
        origin = (seq + GROUP_SEQ - offset) % GROUP_SEQ
        z_copies[offset - 1].wait_recv()
        x_copies.append(forward(origin, mp, x_send.at[offset], x_recv.at[offset], {"mp": across}))
        core_copies.append(
            forward(origin, mp, core_send.at[offset], core_recv.at[offset], {"mp": sibling})
        )
    loads[9].wait()
    for offset in range(GROUP_SEQ):
        origin = (seq + GROUP_SEQ - offset) % GROUP_SEQ
        x_copies[offset].wait_recv()
        core_copies.append(
            forward(
                origin,
                across,
                core_send.at[GROUP_SEQ + offset],
                core_recv.at[GROUP_SEQ + offset],
                {"mp": sibling},
            )
        )
        if offset > 0:
            project(offset - 1)
    project(GROUP_SEQ - 1)
    for copy in pending:
        copy.wait_send()

    own_rows = pl.ds(pl.multiple_of(base, 64), rows)

    def head_only(values, head):
        lane_head = lax.broadcasted_iota(jnp.int32, values.shape, 1) // HEAD_DIM
        return jnp.where(lane_head == head, values, jnp.zeros_like(values))

    stats_pad[...] = jnp.zeros_like(stats_pad)
    heads_sum = jnp.zeros((rows, head_cols), F32)
    query_sum = jnp.zeros((rows, head_cols), F32)
    keys = key_ref[...]
    values = value_ref[...]
    for head in range(local_heads):
        scores = rows_dot(keys, head_only(query_ref[own_rows, :], head)) + bias_row[head]
        row_max = jnp.max(scores, axis=0, keepdims=True)
        raised = jnp.exp(scores - row_max)
        row_sum = jnp.sum(raised, axis=0, keepdims=True)
        probability = raised * (1.0 / row_sum)
        prob_grad = rows_dot(values, head_only(upstream_ref[own_rows, :], head))
        delta = jnp.sum(probability * prob_grad, axis=0, keepdims=True)
        stats_pad[2 * head : 2 * head + 1, :rows] = row_max + jnp.log(row_sum)
        stats_pad[2 * head + 1 : 2 * head + 2, :rows] = delta
        score_grad = (probability * (prob_grad - delta)).astype(BF16)
        heads_sum = heads_sum + cols_dot(probability.astype(BF16), head_only(values, head))
        query_sum = query_sum + cols_dot(score_grad, head_only(keys, head))
    stats_all[seq] = stats_pad[...]
    heads_all[seq] = heads_sum.astype(BF16)
    stats_copies = []
    heads_copies = []
    for offset in range(1, GROUP_SEQ):
        copy = remote(
            stats_all.at[seq],
            stats_all.at[seq],
            stats_send.at[offset - 1],
            stats_recv.at[offset - 1],
            {"seq": (seq + offset) % GROUP_SEQ},
        )
        copy.start()
        stats_copies.append(copy)
    for offset in range(1, GROUP_SEQ):
        copy = remote(
            heads_all.at[seq],
            heads_all.at[seq],
            heads_send.at[offset - 1],
            heads_recv.at[offset - 1],
            {"seq": (seq + offset) % GROUP_SEQ},
        )
        copy.start()
        heads_copies.append(copy)
    own_keys = key_ref[own_rows, :]
    own_values = value_ref[own_rows, :]
    queries = query_ref[...]
    upstream = upstream_ref[...]
    for head in range(local_heads):
        score_buf[head] = rows_dot(own_keys, head_only(queries, head)) + bias_col[head]
        grad_buf[head] = rows_dot(own_values, head_only(upstream, head))
    for copy in stats_copies:
        copy.wait()
    for origin in range(GROUP_SEQ):
        stats_line[:, origin * rows : (origin + 1) * rows] = stats_all[origin, :, :rows]
    stats = stats_line[...]
    key_sum = jnp.zeros((rows, head_cols), F32)
    value_sum = jnp.zeros((rows, head_cols), F32)
    for head in range(local_heads):
        probability = jnp.exp(score_buf[head] - stats[2 * head : 2 * head + 1])
        score_grad = probability * (grad_buf[head] - stats[2 * head + 1 : 2 * head + 2])
        value_sum = value_sum + plain_dot(probability.astype(BF16), head_only(upstream, head))
        key_sum = key_sum + plain_dot(score_grad.astype(BF16), head_only(queries, head))
    back_ref[...] = (
        plain_dot((query_sum * SCALE).astype(BF16), weight_ref[0])
        + plain_dot(key_sum.astype(BF16), weight_ref[1])
        + plain_dot(value_sum.astype(BF16), weight_ref[2])
    )
    back_first = scatter_first(back_ref, back_first_out, back_first_in, back_send, back_recv)
    back_second = scatter_second(
        back_ref, back_first, back_first_in, back_second_out, back_second_in, back_send, back_recv
    )
    entering_grad = scatter_third(back_ref, back_second, back_first_in, back_second_in)
    embedded_grad = norm_back(
        entering_grad * slide_gain, slide_normed, slide_inverse
    ).astype(BF16)
    lifted_grad = rows_dot(embedded_grad, slide_proj_ref[...])
    summed_grad = norm_back(lifted_grad * tile_gain, tile_normed, tile_inverse)
    mixed_all[mp] = (layer_scale * summed_grad).astype(BF16)

    def mixed_move(place, index, where):
        copy = remote(
            mixed_all.at[place],
            mixed_all.at[place],
            mixed_send.at[index],
            mixed_recv.at[index],
            {"mp": where},
        )
        copy.start()
        return copy

    mixed_x = mixed_move(mp, 0, across)
    mixed_core = mixed_move(mp, 1, sibling)
    tile_out[...] = summed_grad.astype(BF16)
    for copy in heads_copies:
        copy.wait()
    heads_out[...] = plain_dot(pick_heads, heads_all[...].reshape(total, head_cols)).astype(BF16)
    mixed_x.wait()
    mixed_corner = mixed_move(across, 2, sibling)
    mixed_core.wait()
    mixed_corner.wait()
    head_out[...] = rows_dot(
        mixed_all[...].reshape(rows, mixed_all.shape[2]), out_proj_ref[...]
    ).astype(BF16)


def finish_kernel(heads_in, tile_in, head_in, heads_out, tile_out, head_out, sems):
    pairs = ((heads_in, heads_out), (tile_in, tile_out), (head_in, head_out))
    copies = [
        pltpu.make_async_copy(source, target, sems.at[index])
        for index, (source, target) in enumerate(pairs)
    ]
    for copy in copies:
        copy.start()
    for copy in copies:
        copy.wait()


def fused_shards(
    tile_features,
    head_outputs,
    out_proj,
    layer_scale,
    tile_gain,
    slide_proj,
    slide_gain,
    qkv_weight,
    slide_slot,
    slide_len,
    seg_log,
    rate_log,
    out_grad,
):
    rows, width_part = tile_features.shape
    width = out_proj.shape[1]
    slide_width = slide_proj.shape[1]
    head_cols = qkv_weight.shape[2]
    local_heads = head_cols // HEAD_DIM
    share = rows // QUAD
    total = GROUP_SEQ * rows
    stats_lanes = -(-rows // 128) * 128
    vmem = pl.BlockSpec(memory_space=pltpu.VMEM)
    smem = pl.BlockSpec(memory_space=pltpu.SMEM)
    hbm = pl.BlockSpec(memory_space=pltpu.HBM)
    dma = pltpu.SemaphoreType.DMA
    results = (
        jax.ShapeDtypeStruct((rows, head_cols), BF16),
        jax.ShapeDtypeStruct((share, width), BF16),
        jax.ShapeDtypeStruct((rows, width_part), BF16),
    )
    computed = pl.pallas_call(
        step_kernel,
        out_shape=results,
        in_specs=[hbm] * 9 + [smem] * 3 + [hbm],
        out_specs=(vmem, vmem, vmem),
        scratch_shapes=[
            pltpu.VMEM((rows, width_part), BF16),
            pltpu.VMEM((rows, width_part), BF16),
            pltpu.VMEM((width_part, width), BF16),
            pltpu.VMEM((width,), F32),
            pltpu.VMEM((width,), F32),
            pltpu.VMEM((width, slide_width), BF16),
            pltpu.VMEM((slide_width,), F32),
            pltpu.VMEM((3, head_cols, slide_width), BF16),
            pltpu.VMEM((total,), jnp.int32),
            pltpu.VMEM((GROUP_SEQ, rows, head_cols), BF16),
            pltpu.VMEM((rows, width), F32),
            pltpu.VMEM((2, share, width), BF16),
            pltpu.VMEM((2, share, width), BF16),
            pltpu.VMEM((share, width), BF16),
            pltpu.VMEM((share, width), BF16),
            pltpu.VMEM((GROUP_SEQ, QUAD, share, slide_width), BF16),
            pltpu.VMEM((total, head_cols), BF16),
            pltpu.VMEM((total, head_cols), BF16),
            pltpu.VMEM((total, head_cols), BF16),
            pltpu.VMEM((total, head_cols), BF16),
            pltpu.VMEM((local_heads, total, rows), F32),
            pltpu.VMEM((local_heads, rows, total), F32),
            pltpu.VMEM((local_heads, rows, total), F32),
            pltpu.VMEM((local_heads, rows, total), F32),
            pltpu.VMEM((8, stats_lanes), F32),
            pltpu.VMEM((8, total), F32),
            pltpu.VMEM((GROUP_SEQ, 8, stats_lanes), F32),
            pltpu.VMEM((GROUP_SEQ, rows, head_cols), BF16),
            pltpu.VMEM((rows, slide_width), F32),
            pltpu.VMEM((2, share, slide_width), BF16),
            pltpu.VMEM((2, share, slide_width), BF16),
            pltpu.VMEM((share, slide_width), BF16),
            pltpu.VMEM((share, slide_width), BF16),
            pltpu.VMEM((QUAD, share, width), BF16),
            dma((10,)),
            dma((3,)),
            dma((3,)),
            dma((3,)),
            dma((3,)),
            dma((3,)),
            dma((3,)),
            dma((4,)),
            dma((4,)),
            dma((8,)),
            dma((8,)),
            dma((3,)),
            dma((3,)),
            dma((3,)),
            dma((3,)),
            dma((3,)),
            dma((3,)),
            dma((3,)),
            dma((3,)),
        ],
        compiler_params=pltpu.CompilerParams(
            collective_id=0, has_side_effects=True, vmem_limit_bytes=VMEM_LIMIT
        ),
        name="slide_step",
    )(
        tile_features,
        head_outputs,
        out_proj,
        layer_scale,
        tile_gain,
        slide_proj,
        slide_gain,
        jnp.transpose(qkv_weight, (1, 2, 0)),
        slide_slot,
        slide_len,
        seg_log,
        rate_log,
        out_grad,
    )
    return pl.pallas_call(
        finish_kernel,
        out_shape=results,
        in_specs=[hbm] * 3,
        out_specs=(hbm,) * 3,
        scratch_shapes=[dma((3,))],
        compiler_params=pltpu.CompilerParams(vmem_limit_bytes=VMEM_LIMIT),
        name="finish",
    )(*computed)


def solution(mesh):
    fused = mesh.shape["seq"] == GROUP_SEQ and mesh.shape["mp"] == QUAD
    body = fused_shards if fused else shards
    in_specs = (
        P(("groups", "seq"), "mp"),
        P(("groups", "seq"), "mp"),
        P("mp", None),
        P(),
        P(),
        P(),
        P(),
        P(None, None, "mp"),
        P("groups"),
        P("groups"),
        P(),
        P(),
        P(("groups", "seq"), "mp"),
    )
    out_specs = (
        P(("groups", "seq"), "mp"),
        P(("groups", "seq", "mp"), None),
        P(("groups", "seq"), "mp"),
    )
    return jax.shard_map(body, mesh=mesh, in_specs=in_specs, out_specs=out_specs, check_vma=False)
```

```python
import jax
import jax.numpy as jnp
from jax import lax
from jax.experimental import pallas as pl
from jax.experimental.pallas import tpu as pltpu
from jax.sharding import PartitionSpec as P

HEAD_DIM = 64
SPAN_LOG = 2


EPSILON = 1e-06
SCALE = HEAD_DIM ** (-0.5)


def swapped(block, axis, distance):
    count = lax.axis_size(axis)
    route = []
    for low in range(count):
        high = low | 1 << distance
        if high != low and high < count:
            route += [(low, high), (high, low)]
    return lax.ppermute(block, axis, route)


def norm_parts(values):
    center = values - jnp.mean(values, axis=-1, keepdims=True)
    inverse = 1.0 / jnp.sqrt(jnp.mean(center * center, axis=-1, keepdims=True) + EPSILON)
    return (center * inverse, inverse)


def norm_back(upstream, normed, inverse):
    first_mean = jnp.mean(upstream, axis=-1, keepdims=True)
    second_mean = jnp.mean(upstream * normed, axis=-1, keepdims=True)
    return inverse * (upstream - first_mean - normed * second_mean)


def slide_ids(positions, slide_len):
    bounds = jnp.cumsum(slide_len)
    return jnp.sum((positions[:, None] >= bounds[None, :]).astype(jnp.int32), axis=1)


def visible(query_pos, key_pos, query_slide, key_slide, widths, strides):
    same_slide = (query_slide[:, None] == key_slide[None, :])[None, :, :]
    window = widths[:, None, None]
    same_window = query_pos[None, :, None] // window == key_pos[None, None, :] // window
    stride = strides[:, None, None]
    same_phase = query_pos[None, :, None] % stride == key_pos[None, None, :] % stride
    return same_slide & same_window & same_phase


def softmax_rows(scores, allowed):
    shifted = jnp.where(allowed, scores, -jnp.inf)
    row_max = jnp.max(shifted, axis=-1, keepdims=True)
    raised = jnp.exp(shifted - row_max)
    return raised / jnp.sum(raised, axis=-1, keepdims=True)


def share_sum(values):
    return lax.psum(values, "mp")


def reroute(buffer):
    return lax.all_to_all(buffer, "seq", split_axis=0, concat_axis=0, tiled=True)


def join_halves(own_part, partner_part, upper_half):
    return jnp.where(
        upper_half,
        jnp.concatenate([partner_part, own_part], axis=1),
        jnp.concatenate([own_part, partner_part], axis=1),
    )


def group_collect(stacked, seq_place):
    for bit_place in range(SPAN_LOG):
        partner_part = swapped(stacked, "seq", bit_place)
        stacked = join_halves(stacked, partner_part, seq_place >> bit_place & 1 == 1)
    return stacked


def group_reduce(stacked, seq_place):
    for bit_place in reversed(range(SPAN_LOG)):
        half_rows = stacked.shape[1] // 2
        upper_half = seq_place >> bit_place & 1 == 1
        lower_part = stacked[:, :half_rows]
        higher_part = stacked[:, half_rows:]
        kept_part = jnp.where(upper_half, higher_part, lower_part)
        given_part = jnp.where(upper_half, lower_part, higher_part)
        stacked = kept_part + swapped(given_part.astype(jnp.bfloat16), "seq", bit_place).astype(
            given_part.dtype
        )
    return stacked


def tile_forward(summed, tile_gain, slide_proj, slide_gain):
    tile_normed, tile_inverse = norm_parts(summed)
    lifted = (tile_normed * tile_gain).astype(jnp.bfloat16)
    embedded = jnp.dot(lifted, slide_proj, preferred_element_type=jnp.float32)
    slide_normed, slide_inverse = norm_parts(embedded)
    entering = (slide_normed * slide_gain).astype(jnp.bfloat16)
    return (entering, (tile_normed, tile_inverse, slide_normed, slide_inverse))


def tile_backward(entering_grad, saved_state, tile_gain, slide_proj, slide_gain, layer_scale):
    tile_normed, tile_inverse, slide_normed, slide_inverse = saved_state
    embedded_grad = norm_back(entering_grad * slide_gain, slide_normed, slide_inverse).astype(
        jnp.bfloat16
    )
    lifted_grad = lax.dot_general(
        embedded_grad, slide_proj, (((1,), (1,)), ((), ())), preferred_element_type=jnp.float32
    )
    summed_grad = norm_back(lifted_grad * tile_gain, tile_normed, tile_inverse)
    mixed_grad = (layer_scale * summed_grad).astype(jnp.bfloat16)
    return (summed_grad, mixed_grad)


def shards(
    tile_features,
    head_outputs,
    out_proj,
    layer_scale,
    tile_gain,
    slide_proj,
    slide_gain,
    qkv_weight,
    slide_slot,
    slide_len,
    seg_log,
    rate_log,
    out_grad,
):
    seq_count = lax.axis_size("seq")
    seq_place = lax.axis_index("seq")
    mp_count = lax.axis_size("mp")
    mp_place = lax.axis_index("mp")
    row_count, width_part = tile_features.shape
    share_rows = row_count // mp_count
    head_cols = qkv_weight.shape[2]
    local_heads = head_cols // HEAD_DIM
    group_size = 1 << SPAN_LOG
    group_count = group_size * row_count
    capacity = 2 * (row_count // seq_count)
    slot_total = seq_count * capacity
    column = mp_place * width_part
    weight_flat = qkv_weight.reshape(qkv_weight.shape[0], 3 * head_cols)
    scale = HEAD_DIM ** (-0.5)
    term = layer_scale * jnp.dot(head_outputs, out_proj, preferred_element_type=jnp.float32)
    own_block = lax.dynamic_slice_in_dim(term, column, width_part, 1) + tile_features.astype(
        jnp.float32
    )
    summed = share_sum(lax.dynamic_update_slice_in_dim(term, own_block, column, 1))
    entering, saved_state = tile_forward(summed, tile_gain, slide_proj, slide_gain)
    projected = jnp.dot(entering, weight_flat, preferred_element_type=jnp.float32).astype(
        jnp.bfloat16
    )
    tile_index = jnp.arange(row_count, dtype=jnp.int32)
    my_slots = lax.dynamic_slice_in_dim(slide_slot, seq_place * row_count, row_count, 0)
    target = my_slots // row_count
    send_rank = jnp.sum(
        ((target[:, None] == target[None, :]) & (tile_index[None, :] < tile_index[:, None])).astype(
            jnp.int32
        ),
        axis=1,
    )
    send_slot = target * capacity + send_rank
    every_tile = jnp.arange(slide_slot.shape[0], dtype=jnp.int32)
    anchor_all = jnp.zeros_like(slide_slot).at[slide_slot].set(every_tile)
    anchor = lax.dynamic_slice_in_dim(anchor_all, seq_place * row_count, row_count, 0)
    anchor_device = anchor // row_count
    anchor_row = anchor % row_count
    recv_rank = jnp.sum(
        (
            (anchor_device[:, None] == anchor_device[None, :])
            & (anchor_row[None, :] < anchor_row[:, None])
        ).astype(jnp.int32),
        axis=1,
    )
    recv_slot = anchor_device * capacity + recv_rank

    def pack(values, slot_list):
        slot_table = jnp.full((slot_total,), row_count, jnp.int32).at[slot_list].set(tile_index)
        padded = jnp.concatenate([values, jnp.zeros((1, values.shape[1]), values.dtype)], axis=0)
        return padded[slot_table].reshape(seq_count, capacity, values.shape[1])

    def unpack(buffer, slot_list):
        return buffer.reshape(slot_total, buffer.shape[2])[slot_list]

    arriving = unpack(reroute(pack(projected, send_slot)), recv_slot)
    queries = arriving[:, :head_cols]
    stacked = group_collect(
        jnp.stack([arriving[:, head_cols : 2 * head_cols], arriving[:, 2 * head_cols :]]), seq_place
    )
    keys_all = stacked[0].reshape(group_count, local_heads, HEAD_DIM)
    values_all = stacked[1].reshape(group_count, local_heads, HEAD_DIM)
    query_heads = queries.reshape(row_count, local_heads, HEAD_DIM)
    here_pos = seq_place * row_count + tile_index
    group_first = seq_place // group_size * group_count
    group_pos = group_first + jnp.arange(group_count, dtype=jnp.int32)
    here_slide = slide_ids(here_pos, slide_len)
    group_slide = slide_ids(group_pos, slide_len)
    head_start = mp_place * local_heads
    widths = row_count * jnp.left_shift(
        jnp.int32(1), lax.dynamic_slice_in_dim(seg_log, head_start, local_heads, 0)
    )
    strides = jnp.left_shift(
        jnp.int32(1), lax.dynamic_slice_in_dim(rate_log, head_start, local_heads, 0)
    )
    allowed = visible(here_pos, group_pos, here_slide, group_slide, widths, strides)
    scores = (
        jnp.einsum("ihd,jhd->hij", query_heads, keys_all, preferred_element_type=jnp.float32)
        * scale
    )
    probability = softmax_rows(scores, allowed)
    rounded = probability.astype(jnp.bfloat16)
    slide_heads = (
        jnp.einsum("hij,jhd->ihd", rounded, values_all, preferred_element_type=jnp.float32)
        .astype(jnp.bfloat16)
        .reshape(row_count, head_cols)
    )
    upstream = out_grad.reshape(row_count, local_heads, HEAD_DIM)
    prob_grad = jnp.einsum("ihd,jhd->hij", upstream, values_all, preferred_element_type=jnp.float32)
    delta = jnp.sum(probability * prob_grad, axis=-1, keepdims=True)
    score_grad = (probability * (prob_grad - delta)).astype(jnp.bfloat16)
    query_grad = (
        jnp.einsum("hij,jhd->ihd", score_grad, keys_all, preferred_element_type=jnp.float32) * scale
    ).astype(jnp.bfloat16)
    key_part = (
        jnp.einsum("hij,ihd->jhd", score_grad, query_heads, preferred_element_type=jnp.float32)
        * scale
    )
    value_part = jnp.einsum("hij,ihd->jhd", rounded, upstream, preferred_element_type=jnp.float32)
    reduced = group_reduce(
        jnp.stack(
            [key_part.reshape(group_count, head_cols), value_part.reshape(group_count, head_cols)]
        ),
        seq_place,
    )
    key_grad = reduced[0].astype(jnp.bfloat16)
    value_grad = reduced[1].astype(jnp.bfloat16)
    local_grad = jnp.concatenate(
        [query_grad.reshape(row_count, head_cols), key_grad, value_grad], axis=1
    )
    returning = unpack(reroute(pack(local_grad, recv_slot)), send_slot)
    entering_grad = share_sum(
        lax.dot_general(
            returning, weight_flat, (((1,), (1,)), ((), ())), preferred_element_type=jnp.float32
        )
    )
    summed_grad, mixed_grad = tile_backward(
        entering_grad, saved_state, tile_gain, slide_proj, slide_gain, layer_scale
    )
    tile_grad = lax.dynamic_slice_in_dim(summed_grad, mp_place * share_rows, share_rows, 0).astype(
        jnp.bfloat16
    )
    head_grad = lax.dot_general(
        mixed_grad, out_proj, (((1,), (1,)), ((), ())), preferred_element_type=jnp.float32
    ).astype(jnp.bfloat16)
    return (slide_heads, tile_grad, head_grad)


F32 = jnp.float32
BF16 = jnp.bfloat16
MESH = pl.DeviceIdType.MESH
HIDDEN = -1e30
GROUP_SEQ = 1 << SPAN_LOG
QUAD = 4
VMEM_LIMIT = 65472 * 1024


def rows_dot(left, right):
    return lax.dot_general(left, right, (((1,), (1,)), ((), ())), preferred_element_type=F32)


def cols_dot(left, right):
    return lax.dot_general(left, right, (((0,), (0,)), ((), ())), preferred_element_type=F32)


def plain_dot(left, right):
    return jnp.dot(left, right, preferred_element_type=F32)


def step_kernel(
    features_hbm,
    outputs_hbm,
    out_proj_hbm,
    layer_scale_hbm,
    tile_gain_hbm,
    slide_proj_hbm,
    slide_gain_hbm,
    weight_hbm,
    slot_hbm,
    len_ref,
    seg_ref,
    rate_ref,
    grad_hbm,
    heads_out,
    tile_out,
    head_out,
    features_ref,
    outputs_ref,
    out_proj_ref,
    layer_scale_ref,
    tile_gain_ref,
    slide_proj_ref,
    slide_gain_ref,
    weight_ref,
    slot_ref,
    upstream_all,
    term_ref,
    first_out,
    first_in,
    second_out,
    second_in,
    entering_all,
    query_ref,
    key_ref,
    value_ref,
    upstream_ref,
    bias_row,
    bias_col,
    score_buf,
    grad_buf,
    stats_pad,
    stats_line,
    stats_all,
    heads_all,
    back_ref,
    back_first_out,
    back_first_in,
    back_second_out,
    back_second_in,
    mixed_all,
    summed_out,
    summed_in,
    load_sem,
    up_send,
    up_recv,
    scatter_send,
    scatter_recv,
    z_send,
    z_recv,
    x_send,
    x_recv,
    core_send,
    core_recv,
    stats_send,
    stats_recv,
    heads_send,
    heads_recv,
    back_send,
    back_recv,
    mixed_send,
    mixed_recv,
):
    rows, width_part = features_ref.shape
    total = GROUP_SEQ * rows
    share = rows // QUAD
    head_cols = grad_hbm.shape[1]
    local_heads = head_cols // HEAD_DIM
    seq = lax.axis_index("seq")
    mp = lax.axis_index("mp")
    sibling = mp + 1 - 2 * (mp % 2)
    across = (mp + 2) % QUAD
    corner = (sibling + 2) % QUAD

    def remote(source, target, send, recv, where):
        return pltpu.make_async_remote_copy(
            src_ref=source,
            dst_ref=target,
            send_sem=send,
            recv_sem=recv,
            device_id=where,
            device_id_type=MESH,
        )

    barrier = pltpu.get_barrier_semaphore()
    for offset in range(1, GROUP_SEQ):
        pl.semaphore_signal(
            barrier, inc=1, device_id={"seq": (seq + offset) % GROUP_SEQ}, device_id_type=MESH
        )
    for offset in range(1, QUAD):
        pl.semaphore_signal(
            barrier, inc=1, device_id={"mp": (mp + offset) % QUAD}, device_id_type=MESH
        )

    loads = [
        pltpu.make_async_copy(source, target, load_sem.at[index])
        for index, (source, target) in enumerate(
            (
                (outputs_hbm, outputs_ref),
                (out_proj_hbm, out_proj_ref),
                (layer_scale_hbm, layer_scale_ref),
                (features_hbm, features_ref),
                (slot_hbm, slot_ref),
                (tile_gain_hbm, tile_gain_ref),
                (slide_gain_hbm, slide_gain_ref),
                (grad_hbm, upstream_all.at[seq]),
                (slide_proj_hbm, slide_proj_ref),
                (weight_hbm, weight_ref),
            )
        )
    ]
    for load in loads:
        load.start()
    for load in loads[:4]:
        load.wait()
    layer_scale = layer_scale_ref[...].reshape(1, layer_scale_ref.shape[0])
    term_ref[...] = layer_scale * plain_dot(outputs_ref[...], out_proj_ref[...])
    own_cols = pl.ds(pl.multiple_of(mp * width_part, 128), width_part)
    term_ref[:, own_cols] += features_ref[...].astype(F32)

    def share_of(place):
        return pl.ds(pl.multiple_of(place * share, 16), share)

    pl.semaphore_wait(barrier, GROUP_SEQ - 1 + QUAD - 1)

    def scatter_first(source, out_buf, in_buf, send, recv):
        copies = []
        for slot, place in ((1, corner), (0, sibling)):
            out_buf[slot] = source[share_of(place), :].astype(BF16)
            copy = remote(
                out_buf.at[slot], in_buf.at[slot], send.at[slot], recv.at[slot], {"mp": sibling}
            )
            copy.start()
            copies.append(copy)
        return copies

    def scatter_second(source, copies, in_buf, out_ref, in_ref, send, recv):
        copies[0].wait_recv()
        out_ref[...] = (source[share_of(across), :] + in_buf[1].astype(F32)).astype(BF16)
        copy = remote(out_ref, in_ref, send.at[2], recv.at[2], {"mp": across})
        copy.start()
        return copies + [copy]

    def scatter_third(source, copies, in_buf, in_ref):
        copies[1].wait_recv()
        partial = source[share_of(mp), :] + in_buf[0].astype(F32)
        copies[2].wait_recv()
        for each in copies:
            each.wait_send()
        return partial + in_ref[...].astype(F32)

    first = scatter_first(term_ref, first_out, first_in, scatter_send, scatter_recv)

    up_copies = []
    for offset in range(1, GROUP_SEQ):
        copy = remote(
            grad_hbm,
            upstream_all.at[seq],
            up_send.at[offset - 1],
            up_recv.at[offset - 1],
            {"seq": (seq + offset) % GROUP_SEQ},
        )
        copy.start()
        up_copies.append(copy)

    second = scatter_second(
        term_ref, first, first_in, second_out, second_in, scatter_send, scatter_recv
    )
    for load in loads[4:8]:
        load.wait()
    slots = slot_ref[...].reshape(1, total)
    tile_gain = tile_gain_ref[...].reshape(1, tile_gain_ref.shape[0])
    slide_gain = slide_gain_ref[...].reshape(1, slide_gain_ref.shape[0])
    base = seq * rows
    bounds = []
    reached = 0
    for index in range(len_ref.shape[0]):
        reached = reached + len_ref[index]
        bounds.append(reached)
    slide_of = jnp.zeros_like(slots)
    for bound in bounds:
        slide_of = slide_of + (slots >= bound).astype(jnp.int32)
    window_of = jnp.zeros_like(slots)
    for index in range(1, GROUP_SEQ):
        window_of = window_of + (slots >= index * rows).astype(jnp.int32)
    lane_all = lax.broadcasted_iota(jnp.int32, (rows, total), 1)
    sub_all = lax.broadcasted_iota(jnp.int32, (rows, total), 0)
    pick_own = (lane_all == sub_all + base).astype(BF16)
    eye = (
        lax.broadcasted_iota(jnp.int32, (total, total), 0)
        == lax.broadcasted_iota(jnp.int32, (total, total), 1)
    ).astype(BF16)
    for head in range(local_heads):
        seg = seg_ref[mp * local_heads + head]
        rate = rate_ref[mp * local_heads + head]
        stride_mask = jnp.left_shift(jnp.int32(1), rate) - 1
        code = (
            slide_of * (GROUP_SEQ * GROUP_SEQ)
            + jnp.right_shift(window_of, jnp.full_like(window_of, seg)) * GROUP_SEQ
            + (slots & stride_mask)
        )
        code_rows = jnp.broadcast_to(code.astype(F32), (rows, total))
        code_bf = code_rows.astype(BF16)
        code_own_lane = rows_dot(code_bf, pick_own)
        code_all_sub = rows_dot(eye, code_bf)
        bias_row[head] = jnp.where(code_all_sub == code_own_lane[:1], 0.0, HIDDEN)
        code_own_sub = rows_dot(pick_own, code_bf)
        bias_col[head] = jnp.where(code_own_sub[:, :1] == code_rows, 0.0, HIDDEN)
    slot_rows = jnp.broadcast_to(slots, (rows, total))
    pick_heads = (slot_rows == sub_all + base).astype(BF16)
    arrange = (
        jnp.broadcast_to(slots, (total, total)) == lax.broadcasted_iota(jnp.int32, (total, total), 0)
    ).astype(BF16)

    summed = scatter_third(term_ref, second, first_in, second_in)
    loads[8].wait()

    def norms_of(block):
        tile_normed, tile_inverse = norm_parts(block)
        lifted = (tile_normed * tile_gain).astype(BF16)
        slide_normed, slide_inverse = norm_parts(plain_dot(lifted, slide_proj_ref[...]))
        return tile_normed, tile_inverse, slide_normed, slide_inverse

    own_norms = norms_of(summed)
    entering_all[seq, mp] = (own_norms[2] * slide_gain).astype(BF16)

    pending = []

    def forward(source_seq, source_mp, send, recv, where):
        copy = remote(
            entering_all.at[source_seq, source_mp],
            entering_all.at[source_seq, source_mp],
            send,
            recv,
            where,
        )
        copy.start()
        pending.append(copy)
        return copy

    z_copies = []
    for offset in range(1, GROUP_SEQ):
        z_copies.append(
            forward(
                seq,
                mp,
                z_send.at[offset - 1],
                z_recv.at[offset - 1],
                {"seq": (seq + offset) % GROUP_SEQ},
            )
        )
    x_copies = [forward(seq, mp, x_send.at[0], x_recv.at[0], {"mp": across})]
    core_copies = [forward(seq, mp, core_send.at[0], core_recv.at[0], {"mp": sibling})]

    def project(offset):
        core_copies[offset].wait_recv()
        core_copies[GROUP_SEQ + offset].wait_recv()
        origin = (seq + GROUP_SEQ - offset) % GROUP_SEQ
        entering = entering_all[origin].reshape(rows, entering_all.shape[3])
        block = pl.ds(pl.multiple_of(origin * rows, 64), rows)
        query = rows_dot(entering, weight_ref[0]).astype(BF16)
        query_ref[block, :] = (query.astype(F32) * SCALE).astype(BF16)
        key_ref[block, :] = rows_dot(entering, weight_ref[1]).astype(BF16)
        value_ref[block, :] = rows_dot(entering, weight_ref[2]).astype(BF16)

    for copy in up_copies:
        copy.wait()
    upstream_ref[...] = cols_dot(arrange, upstream_all[...].reshape(total, head_cols)).astype(BF16)

    for offset in range(1, GROUP_SEQ):
        origin = (seq + GROUP_SEQ - offset) % GROUP_SEQ
        z_copies[offset - 1].wait_recv()
        x_copies.append(forward(origin, mp, x_send.at[offset], x_recv.at[offset], {"mp": across}))
        core_copies.append(
            forward(origin, mp, core_send.at[offset], core_recv.at[offset], {"mp": sibling})
        )
    summed_out[...] = summed
    summed_copy = remote(
        summed_out, summed_in, mixed_send.at[0], mixed_recv.at[0], {"mp": across}
    )
    summed_copy.start()
    loads[9].wait()
    for offset in range(GROUP_SEQ):
        origin = (seq + GROUP_SEQ - offset) % GROUP_SEQ
        x_copies[offset].wait_recv()
        core_copies.append(
            forward(
                origin,
                across,
                core_send.at[GROUP_SEQ + offset],
                core_recv.at[GROUP_SEQ + offset],
                {"mp": sibling},
            )
        )
        if offset > 0:
            project(offset - 1)
    project(GROUP_SEQ - 1)
    for copy in pending:
        copy.wait_send()

    own_rows = pl.ds(pl.multiple_of(base, 64), rows)

    def head_only(values, head):
        lane_head = lax.broadcasted_iota(jnp.int32, values.shape, 1) // HEAD_DIM
        return jnp.where(lane_head == head, values, jnp.zeros_like(values))

    stats_pad[...] = jnp.zeros_like(stats_pad)
    heads_sum = jnp.zeros((rows, head_cols), F32)
    query_sum = jnp.zeros((rows, head_cols), F32)
    keys = key_ref[...]
    values = value_ref[...]
    for head in range(local_heads):
        scores = rows_dot(keys, head_only(query_ref[own_rows, :], head)) + bias_row[head]
        row_max = jnp.max(scores, axis=0, keepdims=True)
        raised = jnp.exp(scores - row_max)
        row_sum = jnp.sum(raised, axis=0, keepdims=True)
        probability = raised * (1.0 / row_sum)
        prob_grad = rows_dot(values, head_only(upstream_ref[own_rows, :], head))
        delta = jnp.sum(probability * prob_grad, axis=0, keepdims=True)
        stats_pad[2 * head : 2 * head + 1, :rows] = row_max + jnp.log(row_sum)
        stats_pad[2 * head + 1 : 2 * head + 2, :rows] = delta
        score_grad = (probability * (prob_grad - delta)).astype(BF16)
        heads_sum = heads_sum + cols_dot(probability.astype(BF16), head_only(values, head))
        query_sum = query_sum + cols_dot(score_grad, head_only(keys, head))
    stats_all[seq] = stats_pad[...]
    heads_all[seq] = heads_sum.astype(BF16)
    stats_copies = []
    heads_copies = []
    for offset in range(1, GROUP_SEQ):
        copy = remote(
            stats_all.at[seq],
            stats_all.at[seq],
            stats_send.at[offset - 1],
            stats_recv.at[offset - 1],
            {"seq": (seq + offset) % GROUP_SEQ},
        )
        copy.start()
        stats_copies.append(copy)
    for offset in range(1, GROUP_SEQ):
        copy = remote(
            heads_all.at[seq],
            heads_all.at[seq],
            heads_send.at[offset - 1],
            heads_recv.at[offset - 1],
            {"seq": (seq + offset) % GROUP_SEQ},
        )
        copy.start()
        heads_copies.append(copy)
    own_keys = key_ref[own_rows, :]
    own_values = value_ref[own_rows, :]
    queries = query_ref[...]
    upstream = upstream_ref[...]
    for head in range(local_heads):
        score_buf[head] = rows_dot(own_keys, head_only(queries, head)) + bias_col[head]
        grad_buf[head] = rows_dot(own_values, head_only(upstream, head))
    summed_copy.wait()
    tile_normed, tile_inverse, slide_normed, slide_inverse = (
        jnp.concatenate(pair, axis=0) for pair in zip(own_norms, norms_of(summed_in[...]))
    )
    for copy in stats_copies:
        copy.wait()
    for origin in range(GROUP_SEQ):
        stats_line[:, origin * rows : (origin + 1) * rows] = stats_all[origin, :, :rows]
    stats = stats_line[...]
    key_sum = jnp.zeros((rows, head_cols), F32)
    value_sum = jnp.zeros((rows, head_cols), F32)
    for head in range(local_heads):
        probability = jnp.exp(score_buf[head] - stats[2 * head : 2 * head + 1])
        score_grad = probability * (grad_buf[head] - stats[2 * head + 1 : 2 * head + 2])
        value_sum = value_sum + plain_dot(probability.astype(BF16), head_only(upstream, head))
        key_sum = key_sum + plain_dot(score_grad.astype(BF16), head_only(queries, head))
    back_ref[...] = (
        plain_dot((query_sum * SCALE).astype(BF16), weight_ref[0])
        + plain_dot(key_sum.astype(BF16), weight_ref[1])
        + plain_dot(value_sum.astype(BF16), weight_ref[2])
    )
    back_first = scatter_first(back_ref, back_first_out, back_first_in, back_send, back_recv)
    back_first[0].wait_recv()
    partial_across = back_ref[share_of(across), :] + back_first_in[1].astype(F32)
    back_first[1].wait_recv()
    partial_own = back_ref[share_of(mp), :] + back_first_in[0].astype(F32)
    back_second_out[0] = partial_own.astype(BF16)
    back_second_out[1] = partial_across.astype(BF16)
    back_copy = remote(
        back_second_out, back_second_in, back_send.at[2], back_recv.at[2], {"mp": across}
    )
    back_copy.start()
    for copy in back_first:
        copy.wait_send()
    back_copy.wait()
    entering_grad = jnp.concatenate(
        [
            partial_own + back_second_in[1].astype(F32),
            partial_across + back_second_in[0].astype(F32),
        ],
        axis=0,
    )
    embedded_grad = norm_back(
        entering_grad * slide_gain, slide_normed, slide_inverse
    ).astype(BF16)
    lifted_grad = rows_dot(embedded_grad, slide_proj_ref[...])
    summed_grad = norm_back(lifted_grad * tile_gain, tile_normed, tile_inverse)
    mixed = (layer_scale * summed_grad).astype(BF16)
    mixed_all[mp] = mixed[:share]
    mixed_all[across] = mixed[share:]

    def mixed_move(place, index, where):
        copy = remote(
            mixed_all.at[place],
            mixed_all.at[place],
            mixed_send.at[index],
            mixed_recv.at[index],
            {"mp": where},
        )
        copy.start()
        return copy

    mixed_core = mixed_move(mp, 1, sibling)
    mixed_corner = mixed_move(across, 2, sibling)
    tile_out[...] = summed_grad[:share].astype(BF16)
    for copy in heads_copies:
        copy.wait()
    heads_out[...] = plain_dot(pick_heads, heads_all[...].reshape(total, head_cols)).astype(BF16)
    mixed_core.wait()
    mixed_corner.wait()
    head_out[...] = rows_dot(
        mixed_all[...].reshape(rows, mixed_all.shape[2]), out_proj_ref[...]
    ).astype(BF16)


def finish_kernel(
    heads_in, tile_in, head_in, heads_out, tile_out, head_out, heads_mid, tile_mid, head_mid, sems
):
    triples = (
        (heads_in, heads_mid, heads_out),
        (tile_in, tile_mid, tile_out),
        (head_in, head_mid, head_out),
    )
    loads = []
    stores = []
    for index, (source, middle, target) in enumerate(triples):
        loads.append(pltpu.make_async_copy(source, middle, sems.at[0, index]))
        stores.append(pltpu.make_async_copy(middle, target, sems.at[1, index]))
    for load in loads:
        load.start()
    for load, store in zip(loads, stores):
        load.wait()
        store.start()
    for store in stores:
        store.wait()


def fused_shards(
    tile_features,
    head_outputs,
    out_proj,
    layer_scale,
    tile_gain,
    slide_proj,
    slide_gain,
    qkv_weight,
    slide_slot,
    slide_len,
    seg_log,
    rate_log,
    out_grad,
):
    rows, width_part = tile_features.shape
    width = out_proj.shape[1]
    slide_width = slide_proj.shape[1]
    head_cols = qkv_weight.shape[2]
    local_heads = head_cols // HEAD_DIM
    share = rows // QUAD
    total = GROUP_SEQ * rows
    stats_lanes = -(-rows // 128) * 128
    vmem = pl.BlockSpec(memory_space=pltpu.VMEM)
    smem = pl.BlockSpec(memory_space=pltpu.SMEM)
    hbm = pl.BlockSpec(memory_space=pltpu.HBM)
    dma = pltpu.SemaphoreType.DMA
    results = (
        jax.ShapeDtypeStruct((rows, head_cols), BF16),
        jax.ShapeDtypeStruct((share, width), BF16),
        jax.ShapeDtypeStruct((rows, width_part), BF16),
    )
    computed = pl.pallas_call(
        step_kernel,
        out_shape=results,
        in_specs=[hbm] * 9 + [smem] * 3 + [hbm],
        out_specs=(vmem, vmem, vmem),
        scratch_shapes=[
            pltpu.VMEM((rows, width_part), BF16),
            pltpu.VMEM((rows, width_part), BF16),
            pltpu.VMEM((width_part, width), BF16),
            pltpu.VMEM((width,), F32),
            pltpu.VMEM((width,), F32),
            pltpu.VMEM((width, slide_width), BF16),
            pltpu.VMEM((slide_width,), F32),
            pltpu.VMEM((3, head_cols, slide_width), BF16),
            pltpu.VMEM((total,), jnp.int32),
            pltpu.VMEM((GROUP_SEQ, rows, head_cols), BF16),
            pltpu.VMEM((rows, width), F32),
            pltpu.VMEM((2, share, width), BF16),
            pltpu.VMEM((2, share, width), BF16),
            pltpu.VMEM((share, width), BF16),
            pltpu.VMEM((share, width), BF16),
            pltpu.VMEM((GROUP_SEQ, QUAD, share, slide_width), BF16),
            pltpu.VMEM((total, head_cols), BF16),
            pltpu.VMEM((total, head_cols), BF16),
            pltpu.VMEM((total, head_cols), BF16),
            pltpu.VMEM((total, head_cols), BF16),
            pltpu.VMEM((local_heads, total, rows), F32),
            pltpu.VMEM((local_heads, rows, total), F32),
            pltpu.VMEM((local_heads, rows, total), F32),
            pltpu.VMEM((local_heads, rows, total), F32),
            pltpu.VMEM((8, stats_lanes), F32),
            pltpu.VMEM((8, total), F32),
            pltpu.VMEM((GROUP_SEQ, 8, stats_lanes), F32),
            pltpu.VMEM((GROUP_SEQ, rows, head_cols), BF16),
            pltpu.VMEM((rows, slide_width), F32),
            pltpu.VMEM((2, share, slide_width), BF16),
            pltpu.VMEM((2, share, slide_width), BF16),
            pltpu.VMEM((2, share, slide_width), BF16),
            pltpu.VMEM((2, share, slide_width), BF16),
            pltpu.VMEM((QUAD, share, width), BF16),
            pltpu.VMEM((share, width), F32),
            pltpu.VMEM((share, width), F32),
            dma((10,)),
            dma((3,)),
            dma((3,)),
            dma((3,)),
            dma((3,)),
            dma((3,)),
            dma((3,)),
            dma((4,)),
            dma((4,)),
            dma((8,)),
            dma((8,)),
            dma((3,)),
            dma((3,)),
            dma((3,)),
            dma((3,)),
            dma((3,)),
            dma((3,)),
            dma((3,)),
            dma((3,)),
        ],
        compiler_params=pltpu.CompilerParams(
            collective_id=0, has_side_effects=True, vmem_limit_bytes=VMEM_LIMIT
        ),
        name="slide_step",
    )(
        tile_features,
        head_outputs,
        out_proj,
        layer_scale,
        tile_gain,
        slide_proj,
        slide_gain,
        jnp.transpose(qkv_weight, (1, 2, 0)),
        slide_slot,
        slide_len,
        seg_log,
        rate_log,
        out_grad,
    )
    return pl.pallas_call(
        finish_kernel,
        out_shape=results,
        in_specs=[hbm] * 3,
        out_specs=(hbm,) * 3,
        scratch_shapes=[pltpu.VMEM(each.shape, each.dtype) for each in results] + [dma((2, 3))],
        compiler_params=pltpu.CompilerParams(vmem_limit_bytes=VMEM_LIMIT),
        name="finish",
    )(*computed)


def solution(mesh):
    fused = mesh.shape["seq"] == GROUP_SEQ and mesh.shape["mp"] == QUAD
    body = fused_shards if fused else shards
    in_specs = (
        P(("groups", "seq"), "mp"),
        P(("groups", "seq"), "mp"),
        P("mp", None),
        P(),
        P(),
        P(),
        P(),
        P(None, None, "mp"),
        P("groups"),
        P("groups"),
        P(),
        P(),
        P(("groups", "seq"), "mp"),
    )
    out_specs = (
        P(("groups", "seq"), "mp"),
        P(("groups", "seq", "mp"), None),
        P(("groups", "seq"), "mp"),
    )
    return jax.shard_map(body, mesh=mesh, in_specs=in_specs, out_specs=out_specs, check_vma=False)
```

```python
import jax
import jax.numpy as jnp
from jax import lax
from jax.experimental import pallas as pl
from jax.experimental.pallas import tpu as pltpu
from jax.sharding import PartitionSpec as P

HEAD_DIM = 64
SPAN_LOG = 2


EPSILON = 1e-06
SCALE = HEAD_DIM ** (-0.5)


def swapped(block, axis, distance):
    count = lax.axis_size(axis)
    route = []
    for low in range(count):
        high = low | 1 << distance
        if high != low and high < count:
            route += [(low, high), (high, low)]
    return lax.ppermute(block, axis, route)


def norm_parts(values):
    center = values - jnp.mean(values, axis=-1, keepdims=True)
    inverse = 1.0 / jnp.sqrt(jnp.mean(center * center, axis=-1, keepdims=True) + EPSILON)
    return (center * inverse, inverse)


def norm_back(upstream, normed, inverse):
    first_mean = jnp.mean(upstream, axis=-1, keepdims=True)
    second_mean = jnp.mean(upstream * normed, axis=-1, keepdims=True)
    return inverse * (upstream - first_mean - normed * second_mean)


def slide_ids(positions, slide_len):
    bounds = jnp.cumsum(slide_len)
    return jnp.sum((positions[:, None] >= bounds[None, :]).astype(jnp.int32), axis=1)


def visible(query_pos, key_pos, query_slide, key_slide, widths, strides):
    same_slide = (query_slide[:, None] == key_slide[None, :])[None, :, :]
    window = widths[:, None, None]
    same_window = query_pos[None, :, None] // window == key_pos[None, None, :] // window
    stride = strides[:, None, None]
    same_phase = query_pos[None, :, None] % stride == key_pos[None, None, :] % stride
    return same_slide & same_window & same_phase


def softmax_rows(scores, allowed):
    shifted = jnp.where(allowed, scores, -jnp.inf)
    row_max = jnp.max(shifted, axis=-1, keepdims=True)
    raised = jnp.exp(shifted - row_max)
    return raised / jnp.sum(raised, axis=-1, keepdims=True)


def share_sum(values):
    return lax.psum(values, "mp")


def reroute(buffer):
    return lax.all_to_all(buffer, "seq", split_axis=0, concat_axis=0, tiled=True)


def join_halves(own_part, partner_part, upper_half):
    return jnp.where(
        upper_half,
        jnp.concatenate([partner_part, own_part], axis=1),
        jnp.concatenate([own_part, partner_part], axis=1),
    )


def group_collect(stacked, seq_place):
    for bit_place in range(SPAN_LOG):
        partner_part = swapped(stacked, "seq", bit_place)
        stacked = join_halves(stacked, partner_part, seq_place >> bit_place & 1 == 1)
    return stacked


def group_reduce(stacked, seq_place):
    for bit_place in reversed(range(SPAN_LOG)):
        half_rows = stacked.shape[1] // 2
        upper_half = seq_place >> bit_place & 1 == 1
        lower_part = stacked[:, :half_rows]
        higher_part = stacked[:, half_rows:]
        kept_part = jnp.where(upper_half, higher_part, lower_part)
        given_part = jnp.where(upper_half, lower_part, higher_part)
        stacked = kept_part + swapped(given_part.astype(jnp.bfloat16), "seq", bit_place).astype(
            given_part.dtype
        )
    return stacked


def tile_forward(summed, tile_gain, slide_proj, slide_gain):
    tile_normed, tile_inverse = norm_parts(summed)
    lifted = (tile_normed * tile_gain).astype(jnp.bfloat16)
    embedded = jnp.dot(lifted, slide_proj, preferred_element_type=jnp.float32)
    slide_normed, slide_inverse = norm_parts(embedded)
    entering = (slide_normed * slide_gain).astype(jnp.bfloat16)
    return (entering, (tile_normed, tile_inverse, slide_normed, slide_inverse))


def tile_backward(entering_grad, saved_state, tile_gain, slide_proj, slide_gain, layer_scale):
    tile_normed, tile_inverse, slide_normed, slide_inverse = saved_state
    embedded_grad = norm_back(entering_grad * slide_gain, slide_normed, slide_inverse).astype(
        jnp.bfloat16
    )
    lifted_grad = lax.dot_general(
        embedded_grad, slide_proj, (((1,), (1,)), ((), ())), preferred_element_type=jnp.float32
    )
    summed_grad = norm_back(lifted_grad * tile_gain, tile_normed, tile_inverse)
    mixed_grad = (layer_scale * summed_grad).astype(jnp.bfloat16)
    return (summed_grad, mixed_grad)


def shards(
    tile_features,
    head_outputs,
    out_proj,
    layer_scale,
    tile_gain,
    slide_proj,
    slide_gain,
    qkv_weight,
    slide_slot,
    slide_len,
    seg_log,
    rate_log,
    out_grad,
):
    seq_count = lax.axis_size("seq")
    seq_place = lax.axis_index("seq")
    mp_count = lax.axis_size("mp")
    mp_place = lax.axis_index("mp")
    row_count, width_part = tile_features.shape
    share_rows = row_count // mp_count
    head_cols = qkv_weight.shape[2]
    local_heads = head_cols // HEAD_DIM
    group_size = 1 << SPAN_LOG
    group_count = group_size * row_count
    capacity = 2 * (row_count // seq_count)
    slot_total = seq_count * capacity
    column = mp_place * width_part
    weight_flat = qkv_weight.reshape(qkv_weight.shape[0], 3 * head_cols)
    scale = HEAD_DIM ** (-0.5)
    term = layer_scale * jnp.dot(head_outputs, out_proj, preferred_element_type=jnp.float32)
    own_block = lax.dynamic_slice_in_dim(term, column, width_part, 1) + tile_features.astype(
        jnp.float32
    )
    summed = share_sum(lax.dynamic_update_slice_in_dim(term, own_block, column, 1))
    entering, saved_state = tile_forward(summed, tile_gain, slide_proj, slide_gain)
    projected = jnp.dot(entering, weight_flat, preferred_element_type=jnp.float32).astype(
        jnp.bfloat16
    )
    tile_index = jnp.arange(row_count, dtype=jnp.int32)
    my_slots = lax.dynamic_slice_in_dim(slide_slot, seq_place * row_count, row_count, 0)
    target = my_slots // row_count
    send_rank = jnp.sum(
        ((target[:, None] == target[None, :]) & (tile_index[None, :] < tile_index[:, None])).astype(
            jnp.int32
        ),
        axis=1,
    )
    send_slot = target * capacity + send_rank
    every_tile = jnp.arange(slide_slot.shape[0], dtype=jnp.int32)
    anchor_all = jnp.zeros_like(slide_slot).at[slide_slot].set(every_tile)
    anchor = lax.dynamic_slice_in_dim(anchor_all, seq_place * row_count, row_count, 0)
    anchor_device = anchor // row_count
    anchor_row = anchor % row_count
    recv_rank = jnp.sum(
        (
            (anchor_device[:, None] == anchor_device[None, :])
            & (anchor_row[None, :] < anchor_row[:, None])
        ).astype(jnp.int32),
        axis=1,
    )
    recv_slot = anchor_device * capacity + recv_rank

    def pack(values, slot_list):
        slot_table = jnp.full((slot_total,), row_count, jnp.int32).at[slot_list].set(tile_index)
        padded = jnp.concatenate([values, jnp.zeros((1, values.shape[1]), values.dtype)], axis=0)
        return padded[slot_table].reshape(seq_count, capacity, values.shape[1])

    def unpack(buffer, slot_list):
        return buffer.reshape(slot_total, buffer.shape[2])[slot_list]

    arriving = unpack(reroute(pack(projected, send_slot)), recv_slot)
    queries = arriving[:, :head_cols]
    stacked = group_collect(
        jnp.stack([arriving[:, head_cols : 2 * head_cols], arriving[:, 2 * head_cols :]]), seq_place
    )
    keys_all = stacked[0].reshape(group_count, local_heads, HEAD_DIM)
    values_all = stacked[1].reshape(group_count, local_heads, HEAD_DIM)
    query_heads = queries.reshape(row_count, local_heads, HEAD_DIM)
    here_pos = seq_place * row_count + tile_index
    group_first = seq_place // group_size * group_count
    group_pos = group_first + jnp.arange(group_count, dtype=jnp.int32)
    here_slide = slide_ids(here_pos, slide_len)
    group_slide = slide_ids(group_pos, slide_len)
    head_start = mp_place * local_heads
    widths = row_count * jnp.left_shift(
        jnp.int32(1), lax.dynamic_slice_in_dim(seg_log, head_start, local_heads, 0)
    )
    strides = jnp.left_shift(
        jnp.int32(1), lax.dynamic_slice_in_dim(rate_log, head_start, local_heads, 0)
    )
    allowed = visible(here_pos, group_pos, here_slide, group_slide, widths, strides)
    scores = (
        jnp.einsum("ihd,jhd->hij", query_heads, keys_all, preferred_element_type=jnp.float32)
        * scale
    )
    probability = softmax_rows(scores, allowed)
    rounded = probability.astype(jnp.bfloat16)
    slide_heads = (
        jnp.einsum("hij,jhd->ihd", rounded, values_all, preferred_element_type=jnp.float32)
        .astype(jnp.bfloat16)
        .reshape(row_count, head_cols)
    )
    upstream = out_grad.reshape(row_count, local_heads, HEAD_DIM)
    prob_grad = jnp.einsum("ihd,jhd->hij", upstream, values_all, preferred_element_type=jnp.float32)
    delta = jnp.sum(probability * prob_grad, axis=-1, keepdims=True)
    score_grad = (probability * (prob_grad - delta)).astype(jnp.bfloat16)
    query_grad = (
        jnp.einsum("hij,jhd->ihd", score_grad, keys_all, preferred_element_type=jnp.float32) * scale
    ).astype(jnp.bfloat16)
    key_part = (
        jnp.einsum("hij,ihd->jhd", score_grad, query_heads, preferred_element_type=jnp.float32)
        * scale
    )
    value_part = jnp.einsum("hij,ihd->jhd", rounded, upstream, preferred_element_type=jnp.float32)
    reduced = group_reduce(
        jnp.stack(
            [key_part.reshape(group_count, head_cols), value_part.reshape(group_count, head_cols)]
        ),
        seq_place,
    )
    key_grad = reduced[0].astype(jnp.bfloat16)
    value_grad = reduced[1].astype(jnp.bfloat16)
    local_grad = jnp.concatenate(
        [query_grad.reshape(row_count, head_cols), key_grad, value_grad], axis=1
    )
    returning = unpack(reroute(pack(local_grad, recv_slot)), send_slot)
    entering_grad = share_sum(
        lax.dot_general(
            returning, weight_flat, (((1,), (1,)), ((), ())), preferred_element_type=jnp.float32
        )
    )
    summed_grad, mixed_grad = tile_backward(
        entering_grad, saved_state, tile_gain, slide_proj, slide_gain, layer_scale
    )
    tile_grad = lax.dynamic_slice_in_dim(summed_grad, mp_place * share_rows, share_rows, 0).astype(
        jnp.bfloat16
    )
    head_grad = lax.dot_general(
        mixed_grad, out_proj, (((1,), (1,)), ((), ())), preferred_element_type=jnp.float32
    ).astype(jnp.bfloat16)
    return (slide_heads, tile_grad, head_grad)


F32 = jnp.float32
BF16 = jnp.bfloat16
MESH = pl.DeviceIdType.MESH
HIDDEN = -1e30
GROUP_SEQ = 1 << SPAN_LOG
QUAD = 4
VMEM_LIMIT = 65472 * 1024


def rows_dot(left, right):
    return lax.dot_general(left, right, (((1,), (1,)), ((), ())), preferred_element_type=F32)


def cols_dot(left, right):
    return lax.dot_general(left, right, (((0,), (0,)), ((), ())), preferred_element_type=F32)


def plain_dot(left, right):
    return jnp.dot(left, right, preferred_element_type=F32)


def step_kernel(
    features_hbm,
    outputs_hbm,
    out_proj_hbm,
    layer_scale_hbm,
    tile_gain_hbm,
    slide_proj_hbm,
    slide_gain_hbm,
    weight_hbm,
    slot_hbm,
    len_ref,
    seg_ref,
    rate_ref,
    grad_hbm,
    heads_out,
    tile_out,
    head_out,
    features_ref,
    outputs_ref,
    out_proj_ref,
    layer_scale_ref,
    tile_gain_ref,
    slide_proj_ref,
    slide_gain_ref,
    weight_ref,
    slot_ref,
    upstream_all,
    term_ref,
    first_out,
    first_in,
    second_out,
    second_in,
    entering_all,
    query_ref,
    key_ref,
    value_ref,
    upstream_ref,
    bias_row,
    bias_col,
    rounded_buf,
    score_grad_buf,
    score_buf,
    grad_buf,
    stats_pad,
    stats_line,
    stats_all,
    heads_all,
    back_ref,
    back_first_out,
    back_first_in,
    back_second_out,
    back_second_in,
    mixed_all,
    summed_out,
    summed_in,
    load_sem,
    up_send,
    up_recv,
    scatter_send,
    scatter_recv,
    z_send,
    z_recv,
    x_send,
    x_recv,
    core_send,
    core_recv,
    stats_send,
    stats_recv,
    heads_send,
    heads_recv,
    back_send,
    back_recv,
    mixed_send,
    mixed_recv,
):
    rows, width_part = features_ref.shape
    total = GROUP_SEQ * rows
    share = rows // QUAD
    head_cols = grad_hbm.shape[1]
    local_heads = head_cols // HEAD_DIM
    seq = lax.axis_index("seq")
    mp = lax.axis_index("mp")
    sibling = mp + 1 - 2 * (mp % 2)
    across = (mp + 2) % QUAD
    corner = (sibling + 2) % QUAD

    def remote(source, target, send, recv, where):
        return pltpu.make_async_remote_copy(
            src_ref=source,
            dst_ref=target,
            send_sem=send,
            recv_sem=recv,
            device_id=where,
            device_id_type=MESH,
        )

    barrier = pltpu.get_barrier_semaphore()
    for offset in range(1, GROUP_SEQ):
        pl.semaphore_signal(
            barrier, inc=1, device_id={"seq": (seq + offset) % GROUP_SEQ}, device_id_type=MESH
        )
    for offset in range(1, QUAD):
        pl.semaphore_signal(
            barrier, inc=1, device_id={"mp": (mp + offset) % QUAD}, device_id_type=MESH
        )

    loads = [
        pltpu.make_async_copy(source, target, load_sem.at[index])
        for index, (source, target) in enumerate(
            (
                (outputs_hbm, outputs_ref),
                (out_proj_hbm, out_proj_ref),
                (layer_scale_hbm, layer_scale_ref),
                (features_hbm, features_ref),
                (slot_hbm, slot_ref),
                (tile_gain_hbm, tile_gain_ref),
                (slide_gain_hbm, slide_gain_ref),
                (grad_hbm, upstream_all.at[seq]),
                (slide_proj_hbm, slide_proj_ref),
                (weight_hbm, weight_ref),
            )
        )
    ]
    for load in loads:
        load.start()
    for load in loads[:4]:
        load.wait()
    layer_scale = layer_scale_ref[...].reshape(1, layer_scale_ref.shape[0])
    term_ref[...] = layer_scale * plain_dot(outputs_ref[...], out_proj_ref[...])
    own_cols = pl.ds(pl.multiple_of(mp * width_part, 128), width_part)
    term_ref[:, own_cols] += features_ref[...].astype(F32)

    def share_of(place):
        return pl.ds(pl.multiple_of(place * share, 16), share)

    pl.semaphore_wait(barrier, GROUP_SEQ - 1 + QUAD - 1)

    def scatter_first(source, out_buf, in_buf, send, recv):
        copies = []
        for slot, place in ((1, corner), (0, sibling)):
            out_buf[slot] = source[share_of(place), :].astype(BF16)
            copy = remote(
                out_buf.at[slot], in_buf.at[slot], send.at[slot], recv.at[slot], {"mp": sibling}
            )
            copy.start()
            copies.append(copy)
        return copies

    def scatter_second(source, copies, in_buf, out_ref, in_ref, send, recv):
        copies[0].wait_recv()
        out_ref[...] = (source[share_of(across), :] + in_buf[1].astype(F32)).astype(BF16)
        copy = remote(out_ref, in_ref, send.at[2], recv.at[2], {"mp": across})
        copy.start()
        return copies + [copy]

    def scatter_third(source, copies, in_buf, in_ref):
        copies[1].wait_recv()
        partial = source[share_of(mp), :] + in_buf[0].astype(F32)
        copies[2].wait_recv()
        for each in copies:
            each.wait_send()
        return partial + in_ref[...].astype(F32)

    first = scatter_first(term_ref, first_out, first_in, scatter_send, scatter_recv)

    up_copies = []
    for offset in range(1, GROUP_SEQ):
        copy = remote(
            grad_hbm,
            upstream_all.at[seq],
            up_send.at[offset - 1],
            up_recv.at[offset - 1],
            {"seq": (seq + offset) % GROUP_SEQ},
        )
        copy.start()
        up_copies.append(copy)

    second = scatter_second(
        term_ref, first, first_in, second_out, second_in, scatter_send, scatter_recv
    )
    for load in loads[4:8]:
        load.wait()
    slots = slot_ref[...].reshape(1, total)
    tile_gain = tile_gain_ref[...].reshape(1, tile_gain_ref.shape[0])
    slide_gain = slide_gain_ref[...].reshape(1, slide_gain_ref.shape[0])
    base = seq * rows
    bounds = []
    reached = 0
    for index in range(len_ref.shape[0]):
        reached = reached + len_ref[index]
        bounds.append(reached)
    slide_of = jnp.zeros_like(slots)
    for bound in bounds:
        slide_of = slide_of + (slots >= bound).astype(jnp.int32)
    window_of = jnp.zeros_like(slots)
    for index in range(1, GROUP_SEQ):
        window_of = window_of + (slots >= index * rows).astype(jnp.int32)
    lane_all = lax.broadcasted_iota(jnp.int32, (rows, total), 1)
    sub_all = lax.broadcasted_iota(jnp.int32, (rows, total), 0)
    pick_own = (lane_all == sub_all + base).astype(BF16)
    eye = (
        lax.broadcasted_iota(jnp.int32, (total, total), 0)
        == lax.broadcasted_iota(jnp.int32, (total, total), 1)
    ).astype(BF16)
    for head in range(local_heads):
        seg = seg_ref[mp * local_heads + head]
        rate = rate_ref[mp * local_heads + head]
        stride_mask = jnp.left_shift(jnp.int32(1), rate) - 1
        code = (
            slide_of * (GROUP_SEQ * GROUP_SEQ)
            + jnp.right_shift(window_of, jnp.full_like(window_of, seg)) * GROUP_SEQ
            + (slots & stride_mask)
        )
        code_rows = jnp.broadcast_to(code.astype(F32), (rows, total))
        code_bf = code_rows.astype(BF16)
        code_own_lane = rows_dot(code_bf, pick_own)
        code_all_sub = rows_dot(eye, code_bf)
        bias_row[head] = jnp.where(code_all_sub == code_own_lane[:1], 0.0, HIDDEN)
        code_own_sub = rows_dot(pick_own, code_bf)
        bias_col[head] = jnp.where(code_own_sub[:, :1] == code_rows, 0.0, HIDDEN)
    slot_rows = jnp.broadcast_to(slots, (rows, total))
    pick_heads = (slot_rows == sub_all + base).astype(BF16)
    arrange = (
        jnp.broadcast_to(slots, (total, total)) == lax.broadcasted_iota(jnp.int32, (total, total), 0)
    ).astype(BF16)

    summed = scatter_third(term_ref, second, first_in, second_in)
    loads[8].wait()

    def norms_of(block):
        tile_normed, tile_inverse = norm_parts(block)
        lifted = (tile_normed * tile_gain).astype(BF16)
        slide_normed, slide_inverse = norm_parts(plain_dot(lifted, slide_proj_ref[...]))
        return tile_normed, tile_inverse, slide_normed, slide_inverse

    own_norms = norms_of(summed)
    entering_all[seq, mp] = (own_norms[2] * slide_gain).astype(BF16)

    pending = []

    def forward(source_seq, source_mp, send, recv, where):
        copy = remote(
            entering_all.at[source_seq, source_mp],
            entering_all.at[source_seq, source_mp],
            send,
            recv,
            where,
        )
        copy.start()
        pending.append(copy)
        return copy

    z_copies = []
    for offset in range(1, GROUP_SEQ):
        z_copies.append(
            forward(
                seq,
                mp,
                z_send.at[offset - 1],
                z_recv.at[offset - 1],
                {"seq": (seq + offset) % GROUP_SEQ},
            )
        )
    x_copies = [forward(seq, mp, x_send.at[0], x_recv.at[0], {"mp": across})]
    core_copies = [forward(seq, mp, core_send.at[0], core_recv.at[0], {"mp": sibling})]

    def project(offset):
        core_copies[offset].wait_recv()
        core_copies[GROUP_SEQ + offset].wait_recv()
        origin = (seq + GROUP_SEQ - offset) % GROUP_SEQ
        entering = entering_all[origin].reshape(rows, entering_all.shape[3])
        block = pl.ds(pl.multiple_of(origin * rows, 64), rows)
        query = rows_dot(entering, weight_ref[0]).astype(BF16)
        query_ref[block, :] = (query.astype(F32) * SCALE).astype(BF16)
        key_ref[block, :] = rows_dot(entering, weight_ref[1]).astype(BF16)
        value_ref[block, :] = rows_dot(entering, weight_ref[2]).astype(BF16)

    for copy in up_copies:
        copy.wait()
    upstream_ref[...] = cols_dot(arrange, upstream_all[...].reshape(total, head_cols)).astype(BF16)

    for offset in range(1, GROUP_SEQ):
        origin = (seq + GROUP_SEQ - offset) % GROUP_SEQ
        z_copies[offset - 1].wait_recv()
        x_copies.append(forward(origin, mp, x_send.at[offset], x_recv.at[offset], {"mp": across}))
        core_copies.append(
            forward(origin, mp, core_send.at[offset], core_recv.at[offset], {"mp": sibling})
        )
    summed_out[...] = summed
    summed_copy = remote(
        summed_out, summed_in, mixed_send.at[0], mixed_recv.at[0], {"mp": across}
    )
    summed_copy.start()
    loads[9].wait()
    for offset in range(GROUP_SEQ):
        origin = (seq + GROUP_SEQ - offset) % GROUP_SEQ
        x_copies[offset].wait_recv()
        core_copies.append(
            forward(
                origin,
                across,
                core_send.at[GROUP_SEQ + offset],
                core_recv.at[GROUP_SEQ + offset],
                {"mp": sibling},
            )
        )
        if offset > 0:
            project(offset - 1)
    project(GROUP_SEQ - 1)
    for copy in pending:
        copy.wait_send()

    own_rows = pl.ds(pl.multiple_of(base, 64), rows)

    def head_only(values, head):
        lane_head = lax.broadcasted_iota(jnp.int32, values.shape, 1) // HEAD_DIM
        return jnp.where(lane_head == head, values, jnp.zeros_like(values))

    stats_pad[...] = jnp.zeros_like(stats_pad)
    heads_sum = jnp.zeros((rows, head_cols), F32)
    query_sum = jnp.zeros((rows, head_cols), F32)
    keys = key_ref[...]
    values = value_ref[...]
    for head in range(local_heads):
        scores = rows_dot(keys, head_only(query_ref[own_rows, :], head)) + bias_row[head]
        row_max = jnp.max(scores, axis=0, keepdims=True)
        raised = jnp.exp(scores - row_max)
        row_sum = jnp.sum(raised, axis=0, keepdims=True)
        probability = raised * (1.0 / row_sum)
        prob_grad = rows_dot(values, head_only(upstream_ref[own_rows, :], head))
        delta = jnp.sum(probability * prob_grad, axis=0, keepdims=True)
        stats_pad[2 * head : 2 * head + 1, :rows] = row_max + jnp.log(row_sum)
        stats_pad[2 * head + 1 : 2 * head + 2, :rows] = delta
        rounded_buf[head] = probability.astype(BF16)
        score_grad_buf[head] = (probability * (prob_grad - delta)).astype(BF16)
    stats_all[seq] = stats_pad[...]
    stats_copies = []
    heads_copies = []
    for offset in range(1, GROUP_SEQ):
        copy = remote(
            stats_all.at[seq],
            stats_all.at[seq],
            stats_send.at[offset - 1],
            stats_recv.at[offset - 1],
            {"seq": (seq + offset) % GROUP_SEQ},
        )
        copy.start()
        stats_copies.append(copy)
    for head in range(local_heads):
        heads_sum = heads_sum + cols_dot(rounded_buf[head], head_only(values, head))
        query_sum = query_sum + cols_dot(score_grad_buf[head], head_only(keys, head))
    heads_all[seq] = heads_sum.astype(BF16)
    for offset in range(1, GROUP_SEQ):
        copy = remote(
            heads_all.at[seq],
            heads_all.at[seq],
            heads_send.at[offset - 1],
            heads_recv.at[offset - 1],
            {"seq": (seq + offset) % GROUP_SEQ},
        )
        copy.start()
        heads_copies.append(copy)
    own_keys = key_ref[own_rows, :]
    own_values = value_ref[own_rows, :]
    queries = query_ref[...]
    upstream = upstream_ref[...]
    for head in range(local_heads):
        score_buf[head] = rows_dot(own_keys, head_only(queries, head)) + bias_col[head]
        grad_buf[head] = rows_dot(own_values, head_only(upstream, head))
    summed_copy.wait()
    tile_normed, tile_inverse, slide_normed, slide_inverse = (
        jnp.concatenate(pair, axis=0) for pair in zip(own_norms, norms_of(summed_in[...]))
    )
    back_ref[...] = plain_dot((query_sum * SCALE).astype(BF16), weight_ref[0])
    for copy in stats_copies:
        copy.wait()
    for origin in range(GROUP_SEQ):
        stats_line[:, origin * rows : (origin + 1) * rows] = stats_all[origin, :, :rows]
    stats = stats_line[...]
    key_sum = jnp.zeros((rows, head_cols), F32)
    value_sum = jnp.zeros((rows, head_cols), F32)
    for head in range(local_heads):
        probability = jnp.exp(score_buf[head] - stats[2 * head : 2 * head + 1])
        score_grad = probability * (grad_buf[head] - stats[2 * head + 1 : 2 * head + 2])
        value_sum = value_sum + plain_dot(probability.astype(BF16), head_only(upstream, head))
        key_sum = key_sum + plain_dot(score_grad.astype(BF16), head_only(queries, head))
    back_ref[...] += (
        plain_dot(key_sum.astype(BF16), weight_ref[1])
        + plain_dot(value_sum.astype(BF16), weight_ref[2])
    )
    back_first = scatter_first(back_ref, back_first_out, back_first_in, back_send, back_recv)
    back_first[0].wait_recv()
    partial_across = back_ref[share_of(across), :] + back_first_in[1].astype(F32)
    back_first[1].wait_recv()
    partial_own = back_ref[share_of(mp), :] + back_first_in[0].astype(F32)
    back_second_out[0] = partial_own.astype(BF16)
    back_second_out[1] = partial_across.astype(BF16)
    back_copy = remote(
        back_second_out, back_second_in, back_send.at[2], back_recv.at[2], {"mp": across}
    )
    back_copy.start()
    for copy in back_first:
        copy.wait_send()
    back_copy.wait()
    entering_grad = jnp.concatenate(
        [
            partial_own + back_second_in[1].astype(F32),
            partial_across + back_second_in[0].astype(F32),
        ],
        axis=0,
    )
    embedded_grad = norm_back(
        entering_grad * slide_gain, slide_normed, slide_inverse
    ).astype(BF16)
    lifted_grad = rows_dot(embedded_grad, slide_proj_ref[...])
    summed_grad = norm_back(lifted_grad * tile_gain, tile_normed, tile_inverse)
    mixed = (layer_scale * summed_grad).astype(BF16)
    mixed_all[mp] = mixed[:share]
    mixed_all[across] = mixed[share:]

    def mixed_move(place, index, where):
        copy = remote(
            mixed_all.at[place],
            mixed_all.at[place],
            mixed_send.at[index],
            mixed_recv.at[index],
            {"mp": where},
        )
        copy.start()
        return copy

    mixed_core = mixed_move(mp, 1, sibling)
    mixed_corner = mixed_move(across, 2, sibling)
    tile_out[...] = summed_grad[:share].astype(BF16)
    for copy in heads_copies:
        copy.wait()
    heads_out[...] = plain_dot(pick_heads, heads_all[...].reshape(total, head_cols)).astype(BF16)
    mixed_core.wait()
    mixed_corner.wait()
    head_out[...] = rows_dot(
        mixed_all[...].reshape(rows, mixed_all.shape[2]), out_proj_ref[...]
    ).astype(BF16)


def finish_kernel(
    heads_in, tile_in, head_in, heads_out, tile_out, head_out, heads_mid, tile_mid, head_mid, sems
):
    triples = (
        (heads_in, heads_mid, heads_out),
        (tile_in, tile_mid, tile_out),
        (head_in, head_mid, head_out),
    )
    loads = []
    stores = []
    for index, (source, middle, target) in enumerate(triples):
        loads.append(pltpu.make_async_copy(source, middle, sems.at[0, index]))
        stores.append(pltpu.make_async_copy(middle, target, sems.at[1, index]))
    for load in loads:
        load.start()
    for load, store in zip(loads, stores):
        load.wait()
        store.start()
    for store in stores:
        store.wait()


def fused_shards(
    tile_features,
    head_outputs,
    out_proj,
    layer_scale,
    tile_gain,
    slide_proj,
    slide_gain,
    qkv_weight,
    slide_slot,
    slide_len,
    seg_log,
    rate_log,
    out_grad,
):
    rows, width_part = tile_features.shape
    width = out_proj.shape[1]
    slide_width = slide_proj.shape[1]
    head_cols = qkv_weight.shape[2]
    local_heads = head_cols // HEAD_DIM
    share = rows // QUAD
    total = GROUP_SEQ * rows
    stats_lanes = -(-rows // 128) * 128
    vmem = pl.BlockSpec(memory_space=pltpu.VMEM)
    smem = pl.BlockSpec(memory_space=pltpu.SMEM)
    hbm = pl.BlockSpec(memory_space=pltpu.HBM)
    dma = pltpu.SemaphoreType.DMA
    results = (
        jax.ShapeDtypeStruct((rows, head_cols), BF16),
        jax.ShapeDtypeStruct((share, width), BF16),
        jax.ShapeDtypeStruct((rows, width_part), BF16),
    )
    computed = pl.pallas_call(
        step_kernel,
        out_shape=results,
        in_specs=[hbm] * 9 + [smem] * 3 + [hbm],
        out_specs=(vmem, vmem, vmem),
        scratch_shapes=[
            pltpu.VMEM((rows, width_part), BF16),
            pltpu.VMEM((rows, width_part), BF16),
            pltpu.VMEM((width_part, width), BF16),
            pltpu.VMEM((width,), F32),
            pltpu.VMEM((width,), F32),
            pltpu.VMEM((width, slide_width), BF16),
            pltpu.VMEM((slide_width,), F32),
            pltpu.VMEM((3, head_cols, slide_width), BF16),
            pltpu.VMEM((total,), jnp.int32),
            pltpu.VMEM((GROUP_SEQ, rows, head_cols), BF16),
            pltpu.VMEM((rows, width), F32),
            pltpu.VMEM((2, share, width), BF16),
            pltpu.VMEM((2, share, width), BF16),
            pltpu.VMEM((share, width), BF16),
            pltpu.VMEM((share, width), BF16),
            pltpu.VMEM((GROUP_SEQ, QUAD, share, slide_width), BF16),
            pltpu.VMEM((total, head_cols), BF16),
            pltpu.VMEM((total, head_cols), BF16),
            pltpu.VMEM((total, head_cols), BF16),
            pltpu.VMEM((total, head_cols), BF16),
            pltpu.VMEM((local_heads, total, rows), F32),
            pltpu.VMEM((local_heads, rows, total), F32),
            pltpu.VMEM((local_heads, total, rows), BF16),
            pltpu.VMEM((local_heads, total, rows), BF16),
            pltpu.VMEM((local_heads, rows, total), F32),
            pltpu.VMEM((local_heads, rows, total), F32),
            pltpu.VMEM((8, stats_lanes), F32),
            pltpu.VMEM((8, total), F32),
            pltpu.VMEM((GROUP_SEQ, 8, stats_lanes), F32),
            pltpu.VMEM((GROUP_SEQ, rows, head_cols), BF16),
            pltpu.VMEM((rows, slide_width), F32),
            pltpu.VMEM((2, share, slide_width), BF16),
            pltpu.VMEM((2, share, slide_width), BF16),
            pltpu.VMEM((2, share, slide_width), BF16),
            pltpu.VMEM((2, share, slide_width), BF16),
            pltpu.VMEM((QUAD, share, width), BF16),
            pltpu.VMEM((share, width), F32),
            pltpu.VMEM((share, width), F32),
            dma((10,)),
            dma((3,)),
            dma((3,)),
            dma((3,)),
            dma((3,)),
            dma((3,)),
            dma((3,)),
            dma((4,)),
            dma((4,)),
            dma((8,)),
            dma((8,)),
            dma((3,)),
            dma((3,)),
            dma((3,)),
            dma((3,)),
            dma((3,)),
            dma((3,)),
            dma((3,)),
            dma((3,)),
        ],
        compiler_params=pltpu.CompilerParams(
            collective_id=0, has_side_effects=True, vmem_limit_bytes=VMEM_LIMIT
        ),
        name="slide_step",
    )(
        tile_features,
        head_outputs,
        out_proj,
        layer_scale,
        tile_gain,
        slide_proj,
        slide_gain,
        jnp.transpose(qkv_weight, (1, 2, 0)),
        slide_slot,
        slide_len,
        seg_log,
        rate_log,
        out_grad,
    )
    return pl.pallas_call(
        finish_kernel,
        out_shape=results,
        in_specs=[hbm] * 3,
        out_specs=(hbm,) * 3,
        scratch_shapes=[pltpu.VMEM(each.shape, each.dtype) for each in results] + [dma((2, 3))],
        compiler_params=pltpu.CompilerParams(vmem_limit_bytes=VMEM_LIMIT),
        name="finish",
    )(*computed)


def solution(mesh):
    fused = mesh.shape["seq"] == GROUP_SEQ and mesh.shape["mp"] == QUAD
    body = fused_shards if fused else shards
    in_specs = (
        P(("groups", "seq"), "mp"),
        P(("groups", "seq"), "mp"),
        P("mp", None),
        P(),
        P(),
        P(),
        P(),
        P(None, None, "mp"),
        P("groups"),
        P("groups"),
        P(),
        P(),
        P(("groups", "seq"), "mp"),
    )
    out_specs = (
        P(("groups", "seq"), "mp"),
        P(("groups", "seq", "mp"), None),
        P(("groups", "seq"), "mp"),
    )
    return jax.shard_map(body, mesh=mesh, in_specs=in_specs, out_specs=out_specs, check_vma=False)
```

```python
import jax
import jax.numpy as jnp
from jax import lax
from jax.experimental import pallas as pl
from jax.experimental.pallas import tpu as pltpu
from jax.sharding import PartitionSpec as P

HEAD_DIM = 64
SPAN_LOG = 2


EPSILON = 1e-06
SCALE = HEAD_DIM ** (-0.5)


def swapped(block, axis, distance):
    count = lax.axis_size(axis)
    route = []
    for low in range(count):
        high = low | 1 << distance
        if high != low and high < count:
            route += [(low, high), (high, low)]
    return lax.ppermute(block, axis, route)


def norm_parts(values):
    center = values - jnp.mean(values, axis=-1, keepdims=True)
    inverse = 1.0 / jnp.sqrt(jnp.mean(center * center, axis=-1, keepdims=True) + EPSILON)
    return (center * inverse, inverse)


def norm_back(upstream, normed, inverse):
    first_mean = jnp.mean(upstream, axis=-1, keepdims=True)
    second_mean = jnp.mean(upstream * normed, axis=-1, keepdims=True)
    return inverse * (upstream - first_mean - normed * second_mean)


def slide_ids(positions, slide_len):
    bounds = jnp.cumsum(slide_len)
    return jnp.sum((positions[:, None] >= bounds[None, :]).astype(jnp.int32), axis=1)


def visible(query_pos, key_pos, query_slide, key_slide, widths, strides):
    same_slide = (query_slide[:, None] == key_slide[None, :])[None, :, :]
    window = widths[:, None, None]
    same_window = query_pos[None, :, None] // window == key_pos[None, None, :] // window
    stride = strides[:, None, None]
    same_phase = query_pos[None, :, None] % stride == key_pos[None, None, :] % stride
    return same_slide & same_window & same_phase


def softmax_rows(scores, allowed):
    shifted = jnp.where(allowed, scores, -jnp.inf)
    row_max = jnp.max(shifted, axis=-1, keepdims=True)
    raised = jnp.exp(shifted - row_max)
    return raised / jnp.sum(raised, axis=-1, keepdims=True)


def share_sum(values):
    return lax.psum(values, "mp")


def reroute(buffer):
    return lax.all_to_all(buffer, "seq", split_axis=0, concat_axis=0, tiled=True)


def join_halves(own_part, partner_part, upper_half):
    return jnp.where(
        upper_half,
        jnp.concatenate([partner_part, own_part], axis=1),
        jnp.concatenate([own_part, partner_part], axis=1),
    )


def group_collect(stacked, seq_place):
    for bit_place in range(SPAN_LOG):
        partner_part = swapped(stacked, "seq", bit_place)
        stacked = join_halves(stacked, partner_part, seq_place >> bit_place & 1 == 1)
    return stacked


def group_reduce(stacked, seq_place):
    for bit_place in reversed(range(SPAN_LOG)):
        half_rows = stacked.shape[1] // 2
        upper_half = seq_place >> bit_place & 1 == 1
        lower_part = stacked[:, :half_rows]
        higher_part = stacked[:, half_rows:]
        kept_part = jnp.where(upper_half, higher_part, lower_part)
        given_part = jnp.where(upper_half, lower_part, higher_part)
        stacked = kept_part + swapped(given_part.astype(jnp.bfloat16), "seq", bit_place).astype(
            given_part.dtype
        )
    return stacked


def tile_forward(summed, tile_gain, slide_proj, slide_gain):
    tile_normed, tile_inverse = norm_parts(summed)
    lifted = (tile_normed * tile_gain).astype(jnp.bfloat16)
    embedded = jnp.dot(lifted, slide_proj, preferred_element_type=jnp.float32)
    slide_normed, slide_inverse = norm_parts(embedded)
    entering = (slide_normed * slide_gain).astype(jnp.bfloat16)
    return (entering, (tile_normed, tile_inverse, slide_normed, slide_inverse))


def tile_backward(entering_grad, saved_state, tile_gain, slide_proj, slide_gain, layer_scale):
    tile_normed, tile_inverse, slide_normed, slide_inverse = saved_state
    embedded_grad = norm_back(entering_grad * slide_gain, slide_normed, slide_inverse).astype(
        jnp.bfloat16
    )
    lifted_grad = lax.dot_general(
        embedded_grad, slide_proj, (((1,), (1,)), ((), ())), preferred_element_type=jnp.float32
    )
    summed_grad = norm_back(lifted_grad * tile_gain, tile_normed, tile_inverse)
    mixed_grad = (layer_scale * summed_grad).astype(jnp.bfloat16)
    return (summed_grad, mixed_grad)


def shards(
    tile_features,
    head_outputs,
    out_proj,
    layer_scale,
    tile_gain,
    slide_proj,
    slide_gain,
    qkv_weight,
    slide_slot,
    slide_len,
    seg_log,
    rate_log,
    out_grad,
):
    seq_count = lax.axis_size("seq")
    seq_place = lax.axis_index("seq")
    mp_count = lax.axis_size("mp")
    mp_place = lax.axis_index("mp")
    row_count, width_part = tile_features.shape
    share_rows = row_count // mp_count
    head_cols = qkv_weight.shape[2]
    local_heads = head_cols // HEAD_DIM
    group_size = 1 << SPAN_LOG
    group_count = group_size * row_count
    capacity = 2 * (row_count // seq_count)
    slot_total = seq_count * capacity
    column = mp_place * width_part
    weight_flat = qkv_weight.reshape(qkv_weight.shape[0], 3 * head_cols)
    scale = HEAD_DIM ** (-0.5)
    term = layer_scale * jnp.dot(head_outputs, out_proj, preferred_element_type=jnp.float32)
    own_block = lax.dynamic_slice_in_dim(term, column, width_part, 1) + tile_features.astype(
        jnp.float32
    )
    summed = share_sum(lax.dynamic_update_slice_in_dim(term, own_block, column, 1))
    entering, saved_state = tile_forward(summed, tile_gain, slide_proj, slide_gain)
    projected = jnp.dot(entering, weight_flat, preferred_element_type=jnp.float32).astype(
        jnp.bfloat16
    )
    tile_index = jnp.arange(row_count, dtype=jnp.int32)
    my_slots = lax.dynamic_slice_in_dim(slide_slot, seq_place * row_count, row_count, 0)
    target = my_slots // row_count
    send_rank = jnp.sum(
        ((target[:, None] == target[None, :]) & (tile_index[None, :] < tile_index[:, None])).astype(
            jnp.int32
        ),
        axis=1,
    )
    send_slot = target * capacity + send_rank
    every_tile = jnp.arange(slide_slot.shape[0], dtype=jnp.int32)
    anchor_all = jnp.zeros_like(slide_slot).at[slide_slot].set(every_tile)
    anchor = lax.dynamic_slice_in_dim(anchor_all, seq_place * row_count, row_count, 0)
    anchor_device = anchor // row_count
    anchor_row = anchor % row_count
    recv_rank = jnp.sum(
        (
            (anchor_device[:, None] == anchor_device[None, :])
            & (anchor_row[None, :] < anchor_row[:, None])
        ).astype(jnp.int32),
        axis=1,
    )
    recv_slot = anchor_device * capacity + recv_rank

    def pack(values, slot_list):
        slot_table = jnp.full((slot_total,), row_count, jnp.int32).at[slot_list].set(tile_index)
        padded = jnp.concatenate([values, jnp.zeros((1, values.shape[1]), values.dtype)], axis=0)
        return padded[slot_table].reshape(seq_count, capacity, values.shape[1])

    def unpack(buffer, slot_list):
        return buffer.reshape(slot_total, buffer.shape[2])[slot_list]

    arriving = unpack(reroute(pack(projected, send_slot)), recv_slot)
    queries = arriving[:, :head_cols]
    stacked = group_collect(
        jnp.stack([arriving[:, head_cols : 2 * head_cols], arriving[:, 2 * head_cols :]]), seq_place
    )
    keys_all = stacked[0].reshape(group_count, local_heads, HEAD_DIM)
    values_all = stacked[1].reshape(group_count, local_heads, HEAD_DIM)
    query_heads = queries.reshape(row_count, local_heads, HEAD_DIM)
    here_pos = seq_place * row_count + tile_index
    group_first = seq_place // group_size * group_count
    group_pos = group_first + jnp.arange(group_count, dtype=jnp.int32)
    here_slide = slide_ids(here_pos, slide_len)
    group_slide = slide_ids(group_pos, slide_len)
    head_start = mp_place * local_heads
    widths = row_count * jnp.left_shift(
        jnp.int32(1), lax.dynamic_slice_in_dim(seg_log, head_start, local_heads, 0)
    )
    strides = jnp.left_shift(
        jnp.int32(1), lax.dynamic_slice_in_dim(rate_log, head_start, local_heads, 0)
    )
    allowed = visible(here_pos, group_pos, here_slide, group_slide, widths, strides)
    scores = (
        jnp.einsum("ihd,jhd->hij", query_heads, keys_all, preferred_element_type=jnp.float32)
        * scale
    )
    probability = softmax_rows(scores, allowed)
    rounded = probability.astype(jnp.bfloat16)
    slide_heads = (
        jnp.einsum("hij,jhd->ihd", rounded, values_all, preferred_element_type=jnp.float32)
        .astype(jnp.bfloat16)
        .reshape(row_count, head_cols)
    )
    upstream = out_grad.reshape(row_count, local_heads, HEAD_DIM)
    prob_grad = jnp.einsum("ihd,jhd->hij", upstream, values_all, preferred_element_type=jnp.float32)
    delta = jnp.sum(probability * prob_grad, axis=-1, keepdims=True)
    score_grad = (probability * (prob_grad - delta)).astype(jnp.bfloat16)
    query_grad = (
        jnp.einsum("hij,jhd->ihd", score_grad, keys_all, preferred_element_type=jnp.float32) * scale
    ).astype(jnp.bfloat16)
    key_part = (
        jnp.einsum("hij,ihd->jhd", score_grad, query_heads, preferred_element_type=jnp.float32)
        * scale
    )
    value_part = jnp.einsum("hij,ihd->jhd", rounded, upstream, preferred_element_type=jnp.float32)
    reduced = group_reduce(
        jnp.stack(
            [key_part.reshape(group_count, head_cols), value_part.reshape(group_count, head_cols)]
        ),
        seq_place,
    )
    key_grad = reduced[0].astype(jnp.bfloat16)
    value_grad = reduced[1].astype(jnp.bfloat16)
    local_grad = jnp.concatenate(
        [query_grad.reshape(row_count, head_cols), key_grad, value_grad], axis=1
    )
    returning = unpack(reroute(pack(local_grad, recv_slot)), send_slot)
    entering_grad = share_sum(
        lax.dot_general(
            returning, weight_flat, (((1,), (1,)), ((), ())), preferred_element_type=jnp.float32
        )
    )
    summed_grad, mixed_grad = tile_backward(
        entering_grad, saved_state, tile_gain, slide_proj, slide_gain, layer_scale
    )
    tile_grad = lax.dynamic_slice_in_dim(summed_grad, mp_place * share_rows, share_rows, 0).astype(
        jnp.bfloat16
    )
    head_grad = lax.dot_general(
        mixed_grad, out_proj, (((1,), (1,)), ((), ())), preferred_element_type=jnp.float32
    ).astype(jnp.bfloat16)
    return (slide_heads, tile_grad, head_grad)


F32 = jnp.float32
BF16 = jnp.bfloat16
MESH = pl.DeviceIdType.MESH
HIDDEN = -1e30
GROUP_SEQ = 1 << SPAN_LOG
QUAD = 4
VMEM_LIMIT = 65472 * 1024


def rows_dot(left, right):
    return lax.dot_general(left, right, (((1,), (1,)), ((), ())), preferred_element_type=F32)


def cols_dot(left, right):
    return lax.dot_general(left, right, (((0,), (0,)), ((), ())), preferred_element_type=F32)


def plain_dot(left, right):
    return jnp.dot(left, right, preferred_element_type=F32)


def step_kernel(
    features_hbm,
    outputs_hbm,
    out_proj_hbm,
    layer_scale_hbm,
    tile_gain_hbm,
    slide_proj_hbm,
    slide_gain_hbm,
    weight_hbm,
    slot_hbm,
    len_ref,
    seg_ref,
    rate_ref,
    grad_hbm,
    heads_out,
    tile_out,
    head_out,
    features_ref,
    outputs_ref,
    out_proj_ref,
    layer_scale_ref,
    tile_gain_ref,
    slide_proj_ref,
    slide_gain_ref,
    weight_ref,
    slot_ref,
    upstream_all,
    term_ref,
    first_out,
    first_in,
    second_out,
    second_in,
    entering_all,
    query_ref,
    key_ref,
    value_ref,
    upstream_ref,
    bias_row,
    bias_col,
    rounded_buf,
    score_grad_buf,
    score_buf,
    grad_buf,
    stats_pad,
    stats_line,
    stats_all,
    heads_all,
    back_ref,
    back_first_out,
    back_first_in,
    back_second_out,
    back_second_in,
    mixed_all,
    summed_out,
    summed_in,
    load_sem,
    up_send,
    up_recv,
    scatter_send,
    scatter_recv,
    z_send,
    z_recv,
    x_send,
    x_recv,
    core_send,
    core_recv,
    stats_send,
    stats_recv,
    heads_send,
    heads_recv,
    back_send,
    back_recv,
    mixed_send,
    mixed_recv,
):
    rows, width_part = features_ref.shape
    total = GROUP_SEQ * rows
    share = rows // QUAD
    head_cols = grad_hbm.shape[1]
    local_heads = head_cols // HEAD_DIM
    seq = lax.axis_index("seq")
    mp = lax.axis_index("mp")
    sibling = mp + 1 - 2 * (mp % 2)
    across = (mp + 2) % QUAD
    corner = (sibling + 2) % QUAD

    def remote(source, target, send, recv, where):
        return pltpu.make_async_remote_copy(
            src_ref=source,
            dst_ref=target,
            send_sem=send,
            recv_sem=recv,
            device_id=where,
            device_id_type=MESH,
        )

    barrier = pltpu.get_barrier_semaphore()
    for offset in range(1, GROUP_SEQ):
        pl.semaphore_signal(
            barrier, inc=1, device_id={"seq": (seq + offset) % GROUP_SEQ}, device_id_type=MESH
        )
    for offset in range(1, QUAD):
        pl.semaphore_signal(
            barrier, inc=1, device_id={"mp": (mp + offset) % QUAD}, device_id_type=MESH
        )

    loads = [
        pltpu.make_async_copy(source, target, load_sem.at[index])
        for index, (source, target) in enumerate(
            (
                (outputs_hbm, outputs_ref),
                (out_proj_hbm, out_proj_ref),
                (layer_scale_hbm, layer_scale_ref),
                (features_hbm, features_ref),
                (slot_hbm, slot_ref),
                (tile_gain_hbm, tile_gain_ref),
                (slide_gain_hbm, slide_gain_ref),
                (grad_hbm, upstream_all.at[seq]),
                (slide_proj_hbm, slide_proj_ref),
                (weight_hbm, weight_ref),
            )
        )
    ]
    for load in loads:
        load.start()
    for load in loads[:4]:
        load.wait()
    layer_scale = layer_scale_ref[...].reshape(1, layer_scale_ref.shape[0])
    term_ref[...] = layer_scale * plain_dot(outputs_ref[...], out_proj_ref[...])
    own_cols = pl.ds(pl.multiple_of(mp * width_part, 128), width_part)
    term_ref[:, own_cols] += features_ref[...].astype(F32)

    def share_of(place):
        return pl.ds(pl.multiple_of(place * share, 16), share)

    pl.semaphore_wait(barrier, GROUP_SEQ - 1 + QUAD - 1)

    def scatter_first(source, out_buf, in_buf, send, recv):
        copies = []
        for slot, place in ((1, corner), (0, sibling)):
            out_buf[slot] = source[share_of(place), :].astype(BF16)
            copy = remote(
                out_buf.at[slot], in_buf.at[slot], send.at[slot], recv.at[slot], {"mp": sibling}
            )
            copy.start()
            copies.append(copy)
        return copies

    def scatter_second(source, copies, in_buf, out_ref, in_ref, send, recv):
        copies[0].wait_recv()
        out_ref[...] = (source[share_of(across), :] + in_buf[1].astype(F32)).astype(BF16)
        copy = remote(out_ref, in_ref, send.at[2], recv.at[2], {"mp": across})
        copy.start()
        return copies + [copy]

    def scatter_third(source, copies, in_buf, in_ref):
        copies[1].wait_recv()
        partial = source[share_of(mp), :] + in_buf[0].astype(F32)
        copies[2].wait_recv()
        for each in copies:
            each.wait_send()
        return partial + in_ref[...].astype(F32)

    first = scatter_first(term_ref, first_out, first_in, scatter_send, scatter_recv)

    up_copies = []
    for offset in range(1, GROUP_SEQ):
        copy = remote(
            grad_hbm,
            upstream_all.at[seq],
            up_send.at[offset - 1],
            up_recv.at[offset - 1],
            {"seq": (seq + offset) % GROUP_SEQ},
        )
        copy.start()
        up_copies.append(copy)

    second = scatter_second(
        term_ref, first, first_in, second_out, second_in, scatter_send, scatter_recv
    )
    for load in loads[4:8]:
        load.wait()
    slots = slot_ref[...].reshape(1, total)
    tile_gain = tile_gain_ref[...].reshape(1, tile_gain_ref.shape[0])
    slide_gain = slide_gain_ref[...].reshape(1, slide_gain_ref.shape[0])
    base = seq * rows
    bounds = []
    reached = 0
    for index in range(len_ref.shape[0]):
        reached = reached + len_ref[index]
        bounds.append(reached)
    slide_of = jnp.zeros_like(slots)
    for bound in bounds:
        slide_of = slide_of + (slots >= bound).astype(jnp.int32)
    window_of = jnp.zeros_like(slots)
    for index in range(1, GROUP_SEQ):
        window_of = window_of + (slots >= index * rows).astype(jnp.int32)
    lane_all = lax.broadcasted_iota(jnp.int32, (rows, total), 1)
    sub_all = lax.broadcasted_iota(jnp.int32, (rows, total), 0)
    pick_own = (lane_all == sub_all + base).astype(BF16)
    eye = (
        lax.broadcasted_iota(jnp.int32, (total, total), 0)
        == lax.broadcasted_iota(jnp.int32, (total, total), 1)
    ).astype(BF16)
    for head in range(local_heads):
        seg = seg_ref[mp * local_heads + head]
        rate = rate_ref[mp * local_heads + head]
        stride_mask = jnp.left_shift(jnp.int32(1), rate) - 1
        code = (
            slide_of * (GROUP_SEQ * GROUP_SEQ)
            + jnp.right_shift(window_of, jnp.full_like(window_of, seg)) * GROUP_SEQ
            + (slots & stride_mask)
        )
        code_rows = jnp.broadcast_to(code.astype(F32), (rows, total))
        code_bf = code_rows.astype(BF16)
        code_own_lane = rows_dot(code_bf, pick_own)
        code_all_sub = rows_dot(eye, code_bf)
        bias_row[head] = jnp.where(code_all_sub == code_own_lane[:1], 0.0, HIDDEN)
        code_own_sub = rows_dot(pick_own, code_bf)
        bias_col[head] = jnp.where(code_own_sub[:, :1] == code_rows, 0.0, HIDDEN)
    slot_rows = jnp.broadcast_to(slots, (rows, total))
    pick_heads = (slot_rows == sub_all + base).astype(BF16)
    arrange = (
        jnp.broadcast_to(slots, (total, total)) == lax.broadcasted_iota(jnp.int32, (total, total), 0)
    ).astype(BF16)

    summed = scatter_third(term_ref, second, first_in, second_in)
    loads[8].wait()

    def norms_of(block):
        tile_normed, tile_inverse = norm_parts(block)
        lifted = (tile_normed * tile_gain).astype(BF16)
        slide_normed, slide_inverse = norm_parts(plain_dot(lifted, slide_proj_ref[...]))
        return tile_normed, tile_inverse, slide_normed, slide_inverse

    own_norms = norms_of(summed)
    entering_all[seq, mp] = (own_norms[2] * slide_gain).astype(BF16)

    pending = []

    def forward(source_seq, source_mp, send, recv, where):
        copy = remote(
            entering_all.at[source_seq, source_mp],
            entering_all.at[source_seq, source_mp],
            send,
            recv,
            where,
        )
        copy.start()
        pending.append(copy)
        return copy

    z_copies = []
    for offset in range(1, GROUP_SEQ):
        z_copies.append(
            forward(
                seq,
                mp,
                z_send.at[offset - 1],
                z_recv.at[offset - 1],
                {"seq": (seq + offset) % GROUP_SEQ},
            )
        )
    x_copies = [forward(seq, mp, x_send.at[0], x_recv.at[0], {"mp": across})]
    core_copies = [forward(seq, mp, core_send.at[0], core_recv.at[0], {"mp": sibling})]

    def project(offset):
        core_copies[offset].wait_recv()
        core_copies[GROUP_SEQ + offset].wait_recv()
        origin = (seq + GROUP_SEQ - offset) % GROUP_SEQ
        entering = entering_all[origin].reshape(rows, entering_all.shape[3])
        block = pl.ds(pl.multiple_of(origin * rows, 64), rows)
        query = rows_dot(entering, weight_ref[0]).astype(BF16)
        query_ref[block, :] = (query.astype(F32) * SCALE).astype(BF16)
        key_ref[block, :] = rows_dot(entering, weight_ref[1]).astype(BF16)
        value_ref[block, :] = rows_dot(entering, weight_ref[2]).astype(BF16)

    for copy in up_copies:
        copy.wait()
    upstream_ref[...] = cols_dot(arrange, upstream_all[...].reshape(total, head_cols)).astype(BF16)

    for offset in range(1, GROUP_SEQ):
        origin = (seq + GROUP_SEQ - offset) % GROUP_SEQ
        z_copies[offset - 1].wait_recv()
        x_copies.append(forward(origin, mp, x_send.at[offset], x_recv.at[offset], {"mp": across}))
        core_copies.append(
            forward(origin, mp, core_send.at[offset], core_recv.at[offset], {"mp": sibling})
        )
    summed_out[...] = summed
    summed_copy = remote(
        summed_out, summed_in, mixed_send.at[0], mixed_recv.at[0], {"mp": across}
    )
    summed_copy.start()
    loads[9].wait()
    for offset in range(GROUP_SEQ):
        origin = (seq + GROUP_SEQ - offset) % GROUP_SEQ
        x_copies[offset].wait_recv()
        core_copies.append(
            forward(
                origin,
                across,
                core_send.at[GROUP_SEQ + offset],
                core_recv.at[GROUP_SEQ + offset],
                {"mp": sibling},
            )
        )
        if offset > 0:
            project(offset - 1)
    project(GROUP_SEQ - 1)
    for copy in pending:
        copy.wait_send()

    own_rows = pl.ds(pl.multiple_of(base, 64), rows)

    def head_only(values, head):
        lane_head = lax.broadcasted_iota(jnp.int32, values.shape, 1) // HEAD_DIM
        return jnp.where(lane_head == head, values, jnp.zeros_like(values))

    stats_pad[...] = jnp.zeros_like(stats_pad)
    heads_sum = jnp.zeros((rows, head_cols), F32)
    query_sum = jnp.zeros((rows, head_cols), F32)
    keys = key_ref[...]
    values = value_ref[...]
    for head in range(local_heads):
        scores = rows_dot(keys, head_only(query_ref[own_rows, :], head)) + bias_row[head]
        row_max = jnp.max(scores, axis=0, keepdims=True)
        raised = jnp.exp(scores - row_max)
        row_sum = jnp.sum(raised, axis=0, keepdims=True)
        probability = raised * (1.0 / row_sum)
        prob_grad = rows_dot(values, head_only(upstream_ref[own_rows, :], head))
        delta = jnp.sum(probability * prob_grad, axis=0, keepdims=True)
        stats_pad[2 * head : 2 * head + 1, :rows] = row_max + jnp.log(row_sum)
        stats_pad[2 * head + 1 : 2 * head + 2, :rows] = delta
        rounded_buf[head] = probability.astype(BF16)
        score_grad_buf[head] = (probability * (prob_grad - delta)).astype(BF16)
    stats_all[seq] = stats_pad[...]
    stats_copies = []
    heads_copies = []
    for offset in range(1, GROUP_SEQ):
        copy = remote(
            stats_all.at[seq],
            stats_all.at[seq],
            stats_send.at[offset - 1],
            stats_recv.at[offset - 1],
            {"seq": (seq + offset) % GROUP_SEQ},
        )
        copy.start()
        stats_copies.append(copy)
    for head in range(local_heads):
        heads_sum = heads_sum + cols_dot(rounded_buf[head], head_only(values, head))
        query_sum = query_sum + cols_dot(score_grad_buf[head], head_only(keys, head))
    heads_all[seq] = heads_sum.astype(BF16)
    for offset in range(1, GROUP_SEQ):
        copy = remote(
            heads_all.at[seq],
            heads_all.at[seq],
            heads_send.at[offset - 1],
            heads_recv.at[offset - 1],
            {"seq": (seq + offset) % GROUP_SEQ},
        )
        copy.start()
        heads_copies.append(copy)
    own_keys = key_ref[own_rows, :]
    own_values = value_ref[own_rows, :]
    queries = query_ref[...]
    upstream = upstream_ref[...]
    for head in range(local_heads):
        score_buf[head] = rows_dot(own_keys, head_only(queries, head)) + bias_col[head]
        grad_buf[head] = rows_dot(own_values, head_only(upstream, head))
    summed_copy.wait()
    tile_normed, tile_inverse, slide_normed, slide_inverse = (
        jnp.concatenate(pair, axis=0) for pair in zip(own_norms, norms_of(summed_in[...]))
    )
    back_ref[...] = plain_dot((query_sum * SCALE).astype(BF16), weight_ref[0])
    for copy in stats_copies:
        copy.wait()
    for origin in range(GROUP_SEQ):
        stats_line[:, origin * rows : (origin + 1) * rows] = stats_all[origin, :, :rows]
    stats = stats_line[...]
    key_sum = jnp.zeros((rows, head_cols), F32)
    value_sum = jnp.zeros((rows, head_cols), F32)
    for head in range(local_heads):
        probability = jnp.exp(score_buf[head] - stats[2 * head : 2 * head + 1])
        score_grad = probability * (grad_buf[head] - stats[2 * head + 1 : 2 * head + 2])
        value_sum = value_sum + plain_dot(probability.astype(BF16), head_only(upstream, head))
        key_sum = key_sum + plain_dot(score_grad.astype(BF16), head_only(queries, head))
    back_ref[...] += (
        plain_dot(key_sum.astype(BF16), weight_ref[1])
        + plain_dot(value_sum.astype(BF16), weight_ref[2])
    )
    back_first = scatter_first(back_ref, back_first_out, back_first_in, back_send, back_recv)
    back_first[0].wait_recv()
    partial_across = back_ref[share_of(across), :] + back_first_in[1].astype(F32)
    back_first[1].wait_recv()
    partial_own = back_ref[share_of(mp), :] + back_first_in[0].astype(F32)
    back_second_out[0] = partial_own.astype(BF16)
    back_second_out[1] = partial_across.astype(BF16)
    back_copy = remote(
        back_second_out, back_second_in, back_send.at[2], back_recv.at[2], {"mp": across}
    )
    back_copy.start()
    for copy in back_first:
        copy.wait_send()
    back_copy.wait()
    entering_grad = jnp.concatenate(
        [
            partial_own + back_second_in[1].astype(F32),
            partial_across + back_second_in[0].astype(F32),
        ],
        axis=0,
    )
    embedded_grad = norm_back(
        entering_grad * slide_gain, slide_normed, slide_inverse
    ).astype(BF16)
    lifted_grad = rows_dot(embedded_grad, slide_proj_ref[...])
    summed_grad = norm_back(lifted_grad * tile_gain, tile_normed, tile_inverse)
    mixed = (layer_scale * summed_grad).astype(BF16)
    mixed_all[mp] = mixed[:share]
    mixed_all[across] = mixed[share:]

    def mixed_move(place, index, where):
        copy = remote(
            mixed_all.at[place],
            mixed_all.at[place],
            mixed_send.at[index],
            mixed_recv.at[index],
            {"mp": where},
        )
        copy.start()
        return copy

    mixed_core = mixed_move(mp, 1, sibling)
    mixed_corner = mixed_move(across, 2, sibling)
    tile_out[...] = summed_grad[:share].astype(BF16)
    for copy in heads_copies:
        copy.wait()
    heads_out[...] = plain_dot(pick_heads, heads_all[...].reshape(total, head_cols)).astype(BF16)

    def head_rows(first_place, second_place):
        block = jnp.concatenate([mixed_all[first_place], mixed_all[second_place]], axis=0)
        product = rows_dot(block, out_proj_ref[...]).astype(BF16)
        head_out[share_of(first_place), :] = product[:share]
        head_out[share_of(second_place), :] = product[share:]

    head_rows(mp, across)
    mixed_core.wait()
    mixed_corner.wait()
    head_rows(sibling, corner)


def finish_kernel(
    heads_in, tile_in, head_in, heads_out, tile_out, head_out, heads_mid, tile_mid, head_mid, sems
):
    triples = (
        (heads_in, heads_mid, heads_out),
        (tile_in, tile_mid, tile_out),
        (head_in, head_mid, head_out),
    )
    loads = []
    stores = []
    for index, (source, middle, target) in enumerate(triples):
        loads.append(pltpu.make_async_copy(source, middle, sems.at[0, index]))
        stores.append(pltpu.make_async_copy(middle, target, sems.at[1, index]))
    for load in loads:
        load.start()
    for load, store in zip(loads, stores):
        load.wait()
        store.start()
    for store in stores:
        store.wait()


def fused_shards(
    tile_features,
    head_outputs,
    out_proj,
    layer_scale,
    tile_gain,
    slide_proj,
    slide_gain,
    qkv_weight,
    slide_slot,
    slide_len,
    seg_log,
    rate_log,
    out_grad,
):
    rows, width_part = tile_features.shape
    width = out_proj.shape[1]
    slide_width = slide_proj.shape[1]
    head_cols = qkv_weight.shape[2]
    local_heads = head_cols // HEAD_DIM
    share = rows // QUAD
    total = GROUP_SEQ * rows
    stats_lanes = -(-rows // 128) * 128
    vmem = pl.BlockSpec(memory_space=pltpu.VMEM)
    smem = pl.BlockSpec(memory_space=pltpu.SMEM)
    hbm = pl.BlockSpec(memory_space=pltpu.HBM)
    dma = pltpu.SemaphoreType.DMA
    results = (
        jax.ShapeDtypeStruct((rows, head_cols), BF16),
        jax.ShapeDtypeStruct((share, width), BF16),
        jax.ShapeDtypeStruct((rows, width_part), BF16),
    )
    computed = pl.pallas_call(
        step_kernel,
        out_shape=results,
        in_specs=[hbm] * 9 + [smem] * 3 + [hbm],
        out_specs=(vmem, vmem, vmem),
        scratch_shapes=[
            pltpu.VMEM((rows, width_part), BF16),
            pltpu.VMEM((rows, width_part), BF16),
            pltpu.VMEM((width_part, width), BF16),
            pltpu.VMEM((width,), F32),
            pltpu.VMEM((width,), F32),
            pltpu.VMEM((width, slide_width), BF16),
            pltpu.VMEM((slide_width,), F32),
            pltpu.VMEM((3, head_cols, slide_width), BF16),
            pltpu.VMEM((total,), jnp.int32),
            pltpu.VMEM((GROUP_SEQ, rows, head_cols), BF16),
            pltpu.VMEM((rows, width), F32),
            pltpu.VMEM((2, share, width), BF16),
            pltpu.VMEM((2, share, width), BF16),
            pltpu.VMEM((share, width), BF16),
            pltpu.VMEM((share, width), BF16),
            pltpu.VMEM((GROUP_SEQ, QUAD, share, slide_width), BF16),
            pltpu.VMEM((total, head_cols), BF16),
            pltpu.VMEM((total, head_cols), BF16),
            pltpu.VMEM((total, head_cols), BF16),
            pltpu.VMEM((total, head_cols), BF16),
            pltpu.VMEM((local_heads, total, rows), F32),
            pltpu.VMEM((local_heads, rows, total), F32),
            pltpu.VMEM((local_heads, total, rows), BF16),
            pltpu.VMEM((local_heads, total, rows), BF16),
            pltpu.VMEM((local_heads, rows, total), F32),
            pltpu.VMEM((local_heads, rows, total), F32),
            pltpu.VMEM((8, stats_lanes), F32),
            pltpu.VMEM((8, total), F32),
            pltpu.VMEM((GROUP_SEQ, 8, stats_lanes), F32),
            pltpu.VMEM((GROUP_SEQ, rows, head_cols), BF16),
            pltpu.VMEM((rows, slide_width), F32),
            pltpu.VMEM((2, share, slide_width), BF16),
            pltpu.VMEM((2, share, slide_width), BF16),
            pltpu.VMEM((2, share, slide_width), BF16),
            pltpu.VMEM((2, share, slide_width), BF16),
            pltpu.VMEM((QUAD, share, width), BF16),
            pltpu.VMEM((share, width), F32),
            pltpu.VMEM((share, width), F32),
            dma((10,)),
            dma((3,)),
            dma((3,)),
            dma((3,)),
            dma((3,)),
            dma((3,)),
            dma((3,)),
            dma((4,)),
            dma((4,)),
            dma((8,)),
            dma((8,)),
            dma((3,)),
            dma((3,)),
            dma((3,)),
            dma((3,)),
            dma((3,)),
            dma((3,)),
            dma((3,)),
            dma((3,)),
        ],
        compiler_params=pltpu.CompilerParams(
            collective_id=0, has_side_effects=True, vmem_limit_bytes=VMEM_LIMIT
        ),
        name="slide_step",
    )(
        tile_features,
        head_outputs,
        out_proj,
        layer_scale,
        tile_gain,
        slide_proj,
        slide_gain,
        jnp.transpose(qkv_weight, (1, 2, 0)),
        slide_slot,
        slide_len,
        seg_log,
        rate_log,
        out_grad,
    )
    return pl.pallas_call(
        finish_kernel,
        out_shape=results,
        in_specs=[hbm] * 3,
        out_specs=(hbm,) * 3,
        scratch_shapes=[pltpu.VMEM(each.shape, each.dtype) for each in results] + [dma((2, 3))],
        compiler_params=pltpu.CompilerParams(vmem_limit_bytes=VMEM_LIMIT),
        name="finish",
    )(*computed)


def solution(mesh):
    fused = mesh.shape["seq"] == GROUP_SEQ and mesh.shape["mp"] == QUAD
    body = fused_shards if fused else shards
    in_specs = (
        P(("groups", "seq"), "mp"),
        P(("groups", "seq"), "mp"),
        P("mp", None),
        P(),
        P(),
        P(),
        P(),
        P(None, None, "mp"),
        P("groups"),
        P("groups"),
        P(),
        P(),
        P(("groups", "seq"), "mp"),
    )
    out_specs = (
        P(("groups", "seq"), "mp"),
        P(("groups", "seq", "mp"), None),
        P(("groups", "seq"), "mp"),
    )
    return jax.shard_map(body, mesh=mesh, in_specs=in_specs, out_specs=out_specs, check_vma=False)
```
